256 devices in a mesh: row: 16 (over z, x_lo), col: 16 (over y, x_hi, core).
Axes of the slice: x: 4 (x_hi: 2, x_lo: 2; x = x_hi * 2 + x_lo), y: 4, z: 8, core: 2. Of those that a mesh axis runs over, the one named last changes fastest.
Arguments:
- right_side: float32 [9, 49152], P(None, 'row'), may hold values from -12 to 12
- noise_level: float32 [49152], P('row'), may hold values from 0.5 to 2
- run_index: int32 [49152], P('row'), may hold values from 0 to 24575
- step_index: int32 [49152], P('row'), may hold values from 0 to 127
- run_features: float32 [16, 24576], replicated, may hold values from -5 to 5
Outputs:
- solution_field: float32 [9, 49152], P(None, 'row')
- residual: float32 [9, 49152], P(None, 'row')
The draws below stay inside these ranges and needn't reach their ends.
All inputs are finite; a program needn't handle non-finite values.
Results may differ from the reference program's by a relative error of at most 0.0003.
Values sent between devices are 32-bit elements; how exact they have to be, the bound alone decides.
No kernel may reach another device: no remote copies, remote signals or barrier semaphores. Data moves between devices by JAX's collectives and lax.ppermute only.
A program may use at most 64 MiB of HBM per device.

```python
import math
import jax
import jax.numpy as jnp
from jax import lax

FEAT = 16
PROBES = 9
STEPS = 128
ITERS = 2
N = 49152
RUNS = 24576


def draw_right_side(key, part):
    key = jax.random.fold_in(key, 11)
    first = jax.random.fold_in(key, 0)
    position = jnp.arange(N, dtype=jnp.float32) / N
    scale = 1.0 + 2.0 * position
    values = jax.random.truncated_normal(first, -3.5, 3.5, (PROBES, N), jnp.float32)
    return (values * scale[None, :]).astype(jnp.float32)


def place_ends(values, own_key, least, top_value):
    dims = values.shape
    place = [jax.random.randint(jax.random.fold_in(own_key, axis), (), 0, dims[axis]) for axis in range(len(dims))]
    values = values.at[tuple(place)].set(least)
    longest = dims.index(max(dims))
    place[longest] = (place[longest] + 1) % dims[longest]
    return values.at[tuple(place)].set(top_value)


def block_levels(stream_key, shape, cuts, least, largest):
    def one(dim, shards_of):
        heights = jax.random.uniform(jax.random.fold_in(jax.random.fold_in(stream_key, 6), dim), (shards_of,), jnp.float32, least / len(cuts), largest / len(cuts))
        return jnp.repeat(jnp.exp(heights), shape[dim] // shards_of).reshape((-1,) + (1,) * (len(shape) - dim - 1))

    factor_of = one(*cuts[0])
    for cut in cuts[1:]:
        factor_of = factor_of * one(*cut)
    return factor_of


def centred(own_key, dims, deviation, most, held_as=jnp.bfloat16):
    return jnp.clip(deviation * jax.random.normal(own_key, dims, jnp.float32), -most, most).astype(held_as)


def setup_inputs(seed: int = 0) -> dict:
    key_list = jax.random.split(jax.random.key(seed), 6)
    return {
        "right_side": draw_right_side(jax.random.fold_in(key_list[5], 71), 0),
        "noise_level": jnp.clip(jnp.exp(math.log(2.0) - 1.3862944 * jax.random.uniform(key_list[1], (N,), jnp.float32) ** block_levels(key_list[1], (N,), ((0, 16),), -0.2, 0.2)), 0.5, 2.0),
        "run_index": place_ends(jax.random.randint(key_list[2], (N,), 0, RUNS), jax.random.fold_in(key_list[2], 1), 0, RUNS - 1).astype(jnp.int32),
        "step_index": place_ends(jax.random.randint(key_list[3], (N,), 0, STEPS), jax.random.fold_in(key_list[3], 1), 0, STEPS - 1).astype(jnp.int32),
        "run_features": centred(key_list[4], (FEAT, RUNS), 0.35, 5.0, jnp.float32),
    }


decay_power = 1.5
decay_offset = 8.0


def point_features(run_index, step_index, run_features):
    runs = jnp.take(run_features, run_index, axis=1)
    steps_float = step_index.astype(runs.dtype)[None, :]
    return jnp.concatenate([runs, steps_float], axis=0)


def kernel_rows(row_feat, col_feat):
    left = row_feat[:-1]
    right = col_feat[:-1]
    cross = jnp.dot(left.T, right, precision=lax.Precision.HIGHEST)
    dist = jnp.sum(left * left, axis=0)[:, None] + jnp.sum(right * right, axis=0)[None, :] - 2.0 * cross
    spread = row_feat[-1][:, None] + col_feat[-1][None, :] + decay_offset
    return jnp.exp(-0.5 * dist - decay_power * jnp.log(spread / decay_offset))


def apply_rows(vector, row_feat, col_feat):
    width = row_feat.shape[1]
    block = 512 if width % 512 == 0 else width
    blocks = row_feat.reshape(row_feat.shape[0], width // block, block).transpose(1, 0, 2)

    def single(features):
        kernel_block = kernel_rows(features, col_feat)
        return jnp.einsum("cw,bw->cb", vector, kernel_block, precision=lax.Precision.HIGHEST)

    result = lax.map(single, blocks)
    return result.transpose(1, 0, 2).reshape(vector.shape[0], width)


def reference(right_side, noise_level, run_index, step_index, run_features):
    features = point_features(run_index, step_index, run_features)

    def operate(vector):
        return apply_rows(vector, features, features) + noise_level[None, :] * vector

    solution_field = jnp.zeros_like(right_side)
    residual = right_side
    direction = right_side
    norm_now = jnp.sum(residual * residual, axis=1)
    for count in range(ITERS):
        image = operate(direction)
        step_size = norm_now / jnp.sum(direction * image, axis=1)
        solution_field = solution_field + step_size[:, None] * direction
        residual = residual - step_size[:, None] * image
        norm_next = jnp.sum(residual * residual, axis=1)
        direction = residual + (norm_next / norm_now)[:, None] * direction
        norm_now = norm_next
    return solution_field, residual
```

```python
import functools
import math

import jax
import jax.numpy as jnp
from jax import lax
from jax.experimental import pallas as pl
from jax.experimental.pallas import tpu as pltpu
from jax.sharding import PartitionSpec as P

LANES = 128
SIDE = 16
FEAT = 16
PROBES = 9
ROWS = 16
MORE = 24
DEPTH = 128
LOG2E = 1.4426950408889634
F32 = jnp.float32
BF16 = jnp.bfloat16
VMEM = pltpu.VMEM
MIB = 1024 * 1024


def vspec():
    return pl.BlockSpec(memory_space=VMEM)


def sspec():
    return pl.BlockSpec(memory_space=pltpu.SMEM)


def params(mib=14):
    return pltpu.CompilerParams(vmem_limit_bytes=mib * MIB)


def gather_body(idx_ref, tab_ref, out_ref):
    lane = lax.broadcasted_iota(jnp.int32, (FEAT, LANES), 1)

    def group(g, _):
        base = pl.multiple_of(g * LANES, LANES)
        acc = jnp.zeros((FEAT, LANES), F32)
        for p in range(LANES):
            run = idx_ref[base + p]
            start = pl.multiple_of((run >> 7) * LANES, LANES)
            tile = tab_ref[:, pl.ds(start, LANES)]
            tile = pltpu.roll(tile, (p + LANES) - (run & (LANES - 1)), 1)
            acc = jnp.where(lane == p, tile, acc)
        out_ref[:, pl.ds(base, LANES)] = acc
        return 0

    lax.fori_loop(0, out_ref.shape[1] // LANES, group, 0)


def gather(idx, table):
    n = idx.shape[0]
    return pl.pallas_call(
        gather_body,
        out_shape=jax.ShapeDtypeStruct((FEAT, n), F32),
        in_specs=[sspec(), vspec()],
        out_specs=vspec(),
        compiler_params=params(),
        cost_estimate=pl.CostEstimate(flops=n * 4000, bytes_accessed=4 * table.size, transcendentals=0),
        name="gather",
    )(idx, table)


def thirds(x):
    a = x.astype(BF16).astype(F32)
    b = (x - a).astype(BF16).astype(F32)
    return a, b, x - a - b


def to_lanes(column, first):
    lane = lax.broadcasted_iota(jnp.int32, (PROBES, LANES), 1)
    sub = lax.broadcasted_iota(jnp.int32, (PROBES, LANES), 0)
    return jnp.sum(jnp.where(lane == sub + first, column, 0.0), axis=0, keepdims=True)


def to_column(row, first):
    lane = lax.broadcasted_iota(jnp.int32, (PROBES, LANES), 1)
    sub = lax.broadcasted_iota(jnp.int32, (PROBES, LANES), 0)
    return jnp.sum(jnp.where(lane == sub + first, row, 0.0), axis=1, keepdims=True)


def unpack(v_ref, nat, tiles):
    for t in range(tiles):
        lanes = slice(t * LANES, (t + 1) * LANES)
        nat[0:8, lanes] = v_ref[t // 2, 8 * (t % 2) : 8 * (t % 2) + 8, :]
        m = 8 * tiles + t
        nat[8:9, lanes] = v_ref[m // ROWS, m % ROWS : m % ROWS + 1, :]


def pack_tile(out_ref, res, tile, tiles):
    out_ref[tile // 2, pl.ds(pl.multiple_of(8 * (tile % 2), 8), 8), :] = res[0:8]
    m = 8 * tiles + tile
    out_ref[m // ROWS, pl.ds(m % ROWS, 1), :] = res[8:9]


def clear_rest(out_ref, tiles):
    m = 9 * tiles
    out_ref[m // ROWS, m % ROWS : ROWS, :] = jnp.zeros((ROWS - m % ROWS, LANES), F32)
    for s in range(m // ROWS + 1, SIDE):
        out_ref[s, 0:ROWS, :] = jnp.zeros((ROWS, LANES), F32)


def build_body(lf_ref, ls_ref, rf_ref, rs_ref, b_ref, bj_ref, noise_ref, flag_ref, khi_ref, klo_ref, out_ref,
               left, right, vec, acc, steps, scal, *, pt, qt):
    n = lf_ref.shape[1]
    m = rf_ref.shape[1]
    tiles = m // LANES
    ch = 512

    def operand(features, is_left):
        f = features * math.sqrt(LOG2E)
        a, b, c = thirds(f)
        norm = -0.5 * jnp.sum(f * f, axis=0, keepdims=True)
        if is_left:
            norm = norm + 1.5 * math.log2(8.0)
        na, nb, nc = thirds(norm)
        one = jnp.ones_like(norm)
        if is_left:
            parts = [a, a, b, b, a, c, na, nb, nc, one, one, one]
        else:
            parts = [a, b, a, b, c, a, one, one, one, na, nb, nc]
        pad = jnp.zeros((DEPTH - 6 * FEAT - 6, f.shape[1]), F32)
        return jnp.concatenate(parts + [pad], axis=0)

    def prepare(t, _):
        o = pl.ds(pl.multiple_of(t * ch, ch), ch)
        left[o, :] = jnp.transpose(operand(lf_ref[:, o], True)).astype(BF16)
        step = ls_ref[:, o].astype(F32) + 8.0
        steps[o, :] = jnp.transpose(jnp.broadcast_to(step, (LANES, ch)))
        right[:, o] = operand(rf_ref[:, o], False).astype(BF16)
        v = b_ref[:, o]
        high = v.astype(BF16).astype(F32)
        zero = jnp.zeros((ROWS - PROBES, ch), F32)
        vec[:, o] = jnp.concatenate([high, zero, v - high, zero], axis=0).astype(BF16)
        return 0

    lax.fori_loop(0, n // ch, prepare, 0)
    scal[...] = jnp.zeros_like(scal)

    def column(jq, _):
        oq = pl.ds(pl.multiple_of(jq * qt, qt), qt)
        right_tile = right[:, oq]
        right_step = rs_ref[:, oq].astype(F32)
        acc[...] = jnp.zeros_like(acc)

        def row(ip, _):
            op = pl.ds(pl.multiple_of(ip * pt, pt), pt)
            power = jnp.dot(left[op, :], right_tile, preferred_element_type=F32)
            spread = jnp.concatenate([steps[op, :]] * (qt // LANES), axis=1) + right_step
            root = lax.rsqrt(spread)
            k = jnp.exp2(power) * (root * (root * root))
            high = k.astype(BF16)
            low = (k - high.astype(F32)).astype(BF16)
            khi_ref[op, oq] = high
            klo_ref[op, oq] = low
            v = vec[:, op]
            y = jnp.dot(v, high, preferred_element_type=F32)
            z = jnp.dot(v[0:ROWS], low, preferred_element_type=F32)
            acc[...] += y[0:ROWS] + y[ROWS:] + z
            return 0

        lax.fori_loop(0, n // pt, row, 0, unroll=n // pt)
        res = acc[0:PROBES, :] + flag_ref[0] * (noise_ref[:, oq] * b_ref[:, oq])
        bj = bj_ref[:, oq]
        scal[0:PROBES, 0:1] += jnp.sum(res * bj, axis=1, keepdims=True)
        scal[0:PROBES, 1:2] += jnp.sum(bj * bj, axis=1, keepdims=True)
        for t in range(qt // LANES):
            pack_tile(out_ref, res[:, t * LANES : (t + 1) * LANES], jq * (qt // LANES) + t, tiles)
        return 0

    clear_rest(out_ref, tiles)
    lax.fori_loop(0, m // qt, column, 0)
    line = to_lanes(scal[0:PROBES, 0:1], 0) + to_lanes(scal[0:PROBES, 1:2] * (1.0 / SIDE), 16)
    for s in range(SIDE):
        out_ref[s, ROWS:MORE, :] = jnp.broadcast_to(line, (MORE - ROWS, LANES))


def build(lf, ls, rf, rs, b, bj, noise, flag, pt=512, qt=1024):
    n, m = lf.shape[1], rf.shape[1]
    half = VMEM((n, m), BF16)
    return pl.pallas_call(
        functools.partial(build_body, pt=pt, qt=qt),
        out_shape=(half, half, jax.ShapeDtypeStruct((SIDE, MORE, LANES), F32)),
        in_specs=[vspec()] * 7 + [sspec()],
        out_specs=(vspec(), vspec(), vspec()),
        scratch_shapes=[
            VMEM((n, DEPTH), BF16),
            VMEM((DEPTH, m), BF16),
            VMEM((2 * ROWS, n), BF16),
            VMEM((ROWS, qt), F32),
            VMEM((n, LANES), F32),
            VMEM((ROWS, LANES), F32),
        ],
        compiler_params=params(),
        cost_estimate=pl.CostEstimate(flops=n * m * 1000, bytes_accessed=n * m * 4, transcendentals=2 * n * m),
        name="build",
    )(lf, ls.reshape(1, n), rf, rs.reshape(1, m), b, bj, noise.reshape(1, n), flag)


def apply_body(khi_ref, klo_ref, w_ref, noise_ref, flag_ref, out_ref, nat, vec, *, pt):
    n, m = khi_ref.shape
    tiles = m // LANES
    unpack(w_ref, nat, tiles)
    w = nat[0:PROBES, :]
    high = w.astype(BF16).astype(F32)
    zero = jnp.zeros((ROWS - PROBES, m), F32)
    vec[...] = jnp.concatenate([high, zero, w - high, zero], axis=0).astype(BF16)
    clear_rest(out_ref, n // LANES)
    dims = (((1,), (1,)), ((), ()))

    def row(ip, _):
        op = pl.ds(pl.multiple_of(ip * pt, pt), pt)
        y = lax.dot_general(vec[...], khi_ref[op, :], dims, preferred_element_type=F32)
        z = lax.dot_general(vec[0:ROWS, :], klo_ref[op, :], dims, preferred_element_type=F32)
        res = (y[0:ROWS] + y[ROWS:] + z)[0:PROBES]
        res = res + flag_ref[0] * (noise_ref[:, op] * nat[0:PROBES, op])
        for t in range(pt // LANES):
            pack_tile(out_ref, res[:, t * LANES : (t + 1) * LANES], ip * (pt // LANES) + t, n // LANES)
        return 0

    lax.fori_loop(0, n // pt, row, 0)


def apply(khi, klo, w, noise, flag, pt=512):
    n, m = khi.shape
    khi = pltpu.with_memory_space_constraint(khi, VMEM)
    klo = pltpu.with_memory_space_constraint(klo, VMEM)
    return pl.pallas_call(
        functools.partial(apply_body, pt=pt),
        out_shape=jax.ShapeDtypeStruct((SIDE, ROWS, LANES), F32),
        in_specs=[vspec()] * 4 + [sspec()],
        out_specs=vspec(),
        scratch_shapes=[VMEM((ROWS, m), F32), VMEM((2 * ROWS, m), BF16)],
        compiler_params=params(),
        cost_estimate=pl.CostEstimate(flops=n * m * 600, bytes_accessed=n * m * 4, transcendentals=0),
        name="apply",
    )(khi, klo, w, noise.reshape(1, n), flag)


def first_sum_body(in_ref, chunk_ref, line_ref):
    total = jnp.sum(in_ref[...], axis=0)
    for s in range(SIDE):
        chunk_ref[s] = total[0:ROWS]
        line_ref[s] = total[ROWS:MORE]


def first_sum(got):
    return pl.pallas_call(
        first_sum_body,
        out_shape=(
            jax.ShapeDtypeStruct((SIDE, ROWS, LANES), F32),
            jax.ShapeDtypeStruct((SIDE, MORE - ROWS, LANES), F32),
        ),
        in_specs=[vspec()],
        out_specs=(vspec(), vspec()),
        compiler_params=params(),
        name="first_sum",
    )(got)


def second_sum_body(in_ref, line_ref, out_ref):
    total = jnp.sum(in_ref[...], axis=0)
    line = jnp.sum(line_ref[...], axis=0)
    for s in range(SIDE):
        out_ref[s, 0:ROWS, :] = total
        out_ref[s, ROWS:MORE, :] = line


def second_sum(got, line):
    return pl.pallas_call(
        second_sum_body,
        out_shape=jax.ShapeDtypeStruct((SIDE, MORE, LANES), F32),
        in_specs=[vspec(), vspec()],
        out_specs=vspec(),
        compiler_params=params(),
        name="second_sum",
    )(got, line)


def scalar_body(b_ref, w_ref, z_ref, line_ref, out_ref, nw, nz):
    tiles = b_ref.shape[1] // LANES
    unpack(w_ref, nw, tiles)
    unpack(z_ref, nz, tiles)
    line = jnp.sum(line_ref[...], axis=0)[0:1]
    bw, bb = to_column(line, 0), to_column(line, 16)
    w = nw[0:PROBES, :]
    r = b_ref[...] - (bb / bw) * w
    rr = jnp.sum(r * r, axis=1, keepdims=True)
    rw = jnp.sum(r * w, axis=1, keepdims=True)
    rz = jnp.sum(r * nz[0:PROBES, :], axis=1, keepdims=True)
    out = to_lanes(rr * (1.0 / SIDE), 0) + to_lanes(rw * (1.0 / SIDE), 16) + to_lanes(rz, 32)
    for s in range(SIDE):
        out_ref[s] = jnp.broadcast_to(out, (MORE - ROWS, LANES))


def scalars(b, w, z, line):
    n = b.shape[1]
    return pl.pallas_call(
        scalar_body,
        out_shape=jax.ShapeDtypeStruct((SIDE, MORE - ROWS, LANES), F32),
        in_specs=[vspec()] * 4,
        out_specs=vspec(),
        scratch_shapes=[VMEM((ROWS, n), F32), VMEM((ROWS, n), F32)],
        compiler_params=params(),
        name="scalars",
    )(b, w, z, line)


def finish_body(b_ref, w_ref, a_ref, line_ref, x_ref, r_ref, nw, na):
    tiles = b_ref.shape[1] // LANES
    unpack(w_ref, nw, tiles)
    unpack(a_ref, na, tiles)
    line = jnp.sum(line_ref[...], axis=0)[0:1]
    bw, bb = to_column(line, 0), to_column(line, 16)
    more = jnp.sum(a_ref[:, ROWS:MORE, :], axis=0)[0:1]
    rr, rw, ra = to_column(more, 0), to_column(more, 16), to_column(more, 32)
    first = bb / bw
    beta = rr / bb
    second = rr / ((rw - first * ra) + 2.0 * beta * rw + beta * beta * bw)
    b = b_ref[...]
    w = nw[0:PROBES, :]
    r = b - first * w
    x_ref[...] = first * b + second * (r + beta * b)
    r_ref[...] = r - second * ((w - first * na[0:PROBES, :]) + beta * w)


def finish(b, w, a, line):
    n = b.shape[1]
    out = jax.ShapeDtypeStruct((PROBES, n), F32)
    return pl.pallas_call(
        finish_body,
        out_shape=(out, out),
        in_specs=[vspec()] * 4,
        out_specs=(vspec(), vspec()),
        scratch_shapes=[VMEM((ROWS, n), F32), VMEM((ROWS, n), F32)],
        compiler_params=params(),
        name="finish",
    )(b, w, a, line)


def on_device(right_side, noise_level, run_index, step_index, run_features):
    swap = [(i * SIDE + j, j * SIDE + i) for i in range(SIDE) for j in range(SIDE)]

    def swapped(x):
        return lax.ppermute(x, ("row", "col"), swap)

    def exchange(x, axis):
        return lax.all_to_all(x, axis, 0, 0)

    flag = (lax.axis_index("row") == lax.axis_index("col")).astype(F32).reshape(1)
    other = swapped(jnp.stack([run_index, step_index]))
    other_side = swapped(right_side)
    own_feat = gather(run_index, run_features)
    col_feat = gather(other[0], run_features)
    khi, klo, part = build(own_feat, step_index, col_feat, other[1], right_side, other_side, noise_level, flag)
    chunk, line = first_sum(exchange(part, "row"))
    product = exchange(chunk, "row")
    line = exchange(line, "col")
    own_product = swapped(product)
    part = apply(khi, klo, product, noise_level, flag)
    more = exchange(scalars(right_side, own_product, part, line), "row")
    again = exchange(second_sum(exchange(part, "col"), more), "col")
    return finish(right_side, own_product, again, line)


def solution(mesh):
    return jax.shard_map(
        on_device,
        mesh=mesh,
        in_specs=(P(None, "row"), P("row"), P("row"), P("row"), P()),
        out_specs=(P(None, "row"), P(None, "row")),
        check_vma=False,
    )
```

```python
import functools
import math

import jax
import jax.numpy as jnp
from jax import lax
from jax.experimental import pallas as pl
from jax.experimental.pallas import tpu as pltpu
from jax.sharding import PartitionSpec as P

LANES = 128
SIDE = 16
FEAT = 16
PROBES = 9
ROWS = 16
BUILD = 10
MORE = 24
PACK = 8
DEPTH = 128
LOG2E = 1.4426950408889634
F32 = jnp.float32
BF16 = jnp.bfloat16
F8 = jnp.float8_e4m3fn
TOP = 240.0
LIFT = 65536.0
VMEM = pltpu.VMEM
MIB = 1024 * 1024


def vspec():
    return pl.BlockSpec(memory_space=VMEM)


def sspec():
    return pl.BlockSpec(memory_space=pltpu.SMEM)


def params(mib=2):
    return pltpu.CompilerParams(vmem_limit_bytes=mib * MIB)


def thirds(x):
    a = x.astype(BF16).astype(F32)
    b = (x - a).astype(BF16).astype(F32)
    return a, b, x - a - b


def to_lanes(column, first):
    lane = lax.broadcasted_iota(jnp.int32, (PROBES, LANES), 1)
    sub = lax.broadcasted_iota(jnp.int32, (PROBES, LANES), 0)
    return jnp.sum(jnp.where(lane == sub + first, column, 0.0), axis=0, keepdims=True)


def to_column(row, first):
    lane = lax.broadcasted_iota(jnp.int32, (PROBES, LANES), 1)
    sub = lax.broadcasted_iota(jnp.int32, (PROBES, LANES), 0)
    return jnp.sum(jnp.where(lane == sub + first, row, 0.0), axis=1, keepdims=True)


def unpack(v_ref, nat, tiles):
    for t in range(tiles):
        lanes = slice(t * LANES, (t + 1) * LANES)
        nat[0:8, lanes] = v_ref[t // 2, 8 * (t % 2) : 8 * (t % 2) + 8, :]
        m = 8 * tiles + t
        nat[8:9, lanes] = v_ref[m // ROWS, m % ROWS : m % ROWS + 1, :]


def pack_tile(out_ref, res, tile, tiles):
    out_ref[tile // 2, pl.ds(pl.multiple_of(8 * (tile % 2), 8), 8), :] = res[0:8]
    m = 8 * tiles + tile
    out_ref[m // ROWS, pl.ds(m % ROWS, 1), :] = res[8:9]


def clear_rest(out_ref, tiles):
    m = 9 * tiles
    out_ref[m // ROWS, m % ROWS : ROWS, :] = jnp.zeros((ROWS - m % ROWS, LANES), F32)
    for s in range(m // ROWS + 1, SIDE):
        out_ref[s, 0:ROWS, :] = jnp.zeros((ROWS, LANES), F32)


def codes(run_index):
    row = ((run_index >> 10) << 7) + (run_index & 127)
    return (((run_index >> 7) & 7) << 12) + row


def by_groups(read, table, rows_a, rows_b, make, groups):
    def fetch(g, rows):
        for p in range(LANES):
            rows[p : p + 1, :] = table[pl.ds(read(g, p) & 4095, 1), :]

    def pair(h, _):
        fetch(2 * h + 1, rows_b)
        make(2 * h, rows_a)
        fetch(jnp.minimum(2 * h + 2, groups - 1), rows_a)
        make(2 * h + 1, rows_b)
        return 0

    fetch(0, rows_a)
    lax.fori_loop(0, groups // 2, pair, 0)


def factors(v):
    zero = jnp.zeros((ROWS - PROBES, v.shape[1]), F32)
    high = v.astype(BF16).astype(F32)
    halves = jnp.concatenate([high, zero, v - high, zero], axis=0).astype(BF16)
    top = jnp.max(jnp.abs(v), axis=1, keepdims=True)
    top = jnp.where(top > 0.0, top, 1.0)
    u = v * (TOP / top)
    coarse = u.astype(F8).astype(F32)
    small = jnp.concatenate([coarse, zero, (u - coarse), zero], axis=0).astype(F8)
    return halves, small, top * (1.0 / (TOP * LIFT))


def selector(blocks):
    src = lax.broadcasted_iota(jnp.int32, (LANES, LANES), 0)
    dst = lax.broadcasted_iota(jnp.int32, (LANES, LANES), 1)
    hit = dst // FEAT == blocks[0]
    for block in blocks[1:]:
        hit = hit | (dst // FEAT == block)
    return jnp.where(hit & (src % FEAT == dst % FEAT), 1.0, 0.0).astype(BF16)


LEFT = ((0, 1, 4), (2, 3), (5,))
RIGHT = ((0, 2, 5), (1, 3), (4,))


def operand(rows, code, picks, is_left):
    lane = lax.broadcasted_iota(jnp.int32, (LANES, LANES), 1)
    group = jnp.transpose(jnp.broadcast_to((code >> 12).astype(F32), (LANES, LANES)))
    f = jnp.where((lane >> 4).astype(F32) == group, rows * math.sqrt(LOG2E), 0.0)
    norm = -0.5 * jnp.sum(f * f, axis=1, keepdims=True)
    if is_left:
        norm = norm + 1.5 * math.log2(8.0)
    out = None
    for part, pick in zip(thirds(f), picks):
        moved = jnp.dot(part.astype(BF16), pick, preferred_element_type=F32)
        out = moved if out is None else out + moved
    first = 6 * FEAT + (0 if is_left else 3)
    ones = 6 * FEAT + (3 if is_left else 0)
    for k, part in enumerate(thirds(norm)):
        out = jnp.where(lane == first + k, part, out)
    return jnp.where((lane >= ones) & (lane < ones + 3), 1.0, out)


def own_body(idx_ref, code_ref, step_ref, tab_ref, b_ref, table, left, steps, vec, small, scale, rows_a, rows_b):
    n = left.shape[0]
    groups = tab_ref.shape[1] // LANES
    for t in range(groups // PACK):
        tiles = [tab_ref[:, (PACK * t + g) * LANES : (PACK * t + g + 1) * LANES] for g in range(PACK)]
        table[t * LANES : (t + 1) * LANES, :] = jnp.transpose(jnp.concatenate(tiles, axis=0))
    picks = [selector(blocks) for blocks in LEFT]

    def make(t, rows):
        o = pl.ds(pl.multiple_of(t * LANES, LANES), LANES)
        left[o, :] = operand(rows[...], code_ref[pl.ds(t, 1), :], picks, True).astype(BF16)
        step = step_ref[pl.ds(t, 1), :].astype(F32) + 8.0
        steps[o, :] = jnp.transpose(jnp.broadcast_to(step, (LANES, LANES)))

    by_groups(lambda g, p: idx_ref[g, p], table, rows_a, rows_b, make, n // LANES)
    vec[...], small[...], factor = factors(b_ref[...])
    scale[...] = jnp.concatenate([jnp.broadcast_to(factor, (PROBES, LANES)), jnp.zeros((ROWS - PROBES, LANES), F32)], axis=0)


def own(code, step, table, b):
    n = b.shape[1]
    packed = table.shape[1] // PACK
    return pl.pallas_call(
        own_body,
        out_shape=(
            VMEM((packed, LANES), F32),
            VMEM((n, LANES), BF16),
            VMEM((n, LANES), F32),
            VMEM((2 * ROWS, n), BF16),
            VMEM((2 * ROWS, n), F8),
            VMEM((ROWS, LANES), F32),
        ),
        in_specs=[sspec()] + [vspec()] * 4,
        out_specs=(vspec(),) * 6,
        scratch_shapes=[VMEM((LANES, LANES), F32), VMEM((LANES, LANES), F32)],
        compiler_params=params(4),
        cost_estimate=pl.CostEstimate(flops=n * 6000, bytes_accessed=4 * table.size, transcendentals=0),
        name="own",
    )(code, code, step, table, b)


def build_body(idx_ref, other_ref, table, left, steps, vec, small, scale, b_ref, noise_ref, flag_ref,
               khi_ref, klo_ref, out_ref, rows_a, rows_b, right, right_steps, acc, acc8, *, pt, qt):
    n, m = khi_ref.shape
    tiles = m // LANES
    picks = [selector(blocks) for blocks in RIGHT]

    def make(t, rows):
        o = pl.ds(pl.multiple_of(t * LANES, LANES), LANES)
        part = operand(rows[...], other_ref[0, pl.ds(t, 1), :], picks, False)
        right[:, o] = jnp.transpose(part).astype(BF16)
        right_steps[0:1, o] = other_ref[1, pl.ds(t, 1), :].astype(F32)

    by_groups(lambda g, p: idx_ref[0, g, p], table, rows_a, rows_b, make, tiles)

    def column(jq, _):
        oq = pl.ds(pl.multiple_of(jq * qt, qt), qt)
        right_tile = right[:, oq]
        right_step = right_steps[0:1, oq]
        acc[...] = jnp.zeros_like(acc)
        acc8[...] = jnp.zeros_like(acc8)

        def row(ip, _):
            op = pl.ds(pl.multiple_of(ip * pt, pt), pt)
            power = jnp.dot(left[op, :], right_tile, preferred_element_type=F32)
            spread = jnp.concatenate([steps[op, :]] * (qt // LANES), axis=1) + right_step
            root = lax.rsqrt(spread)
            k = jnp.exp2(power) * (root * (root * root))
            high = k.astype(BF16)
            low = ((k - high.astype(F32)) * LIFT).astype(F8)
            khi_ref[op, oq] = high
            klo_ref[op, oq] = low
            acc[...] += jnp.dot(vec[:, op], high, preferred_element_type=F32)
            acc8[...] += jnp.dot(small[:, op], low, preferred_element_type=F32)
            return 0

        lax.fori_loop(0, n // pt, row, 0, unroll=n // pt)
        res = acc[0:ROWS, :] + acc[ROWS:, :] + scale[:, 0:1] * (acc8[0:ROWS, :] + acc8[ROWS:, :])
        res = res[0:PROBES] + flag_ref[0] * (noise_ref[:, oq] * b_ref[:, oq])
        for t in range(qt // LANES):
            pack_tile(out_ref, res[:, t * LANES : (t + 1) * LANES], jq * (qt // LANES) + t, tiles)
        return 0

    clear_rest(out_ref, tiles)
    lax.fori_loop(0, m // qt, column, 0)


def build(other, table, left, steps, vec, small, scale, b, noise, flag, pt=3072, qt=256):
    n = b.shape[1]
    m = other.shape[1] * LANES
    return pl.pallas_call(
        functools.partial(build_body, pt=pt, qt=qt),
        out_shape=(VMEM((n, m), BF16), VMEM((n, m), F8), jax.ShapeDtypeStruct((SIDE, ROWS, LANES), F32)),
        in_specs=[sspec()] + [vspec()] * 9 + [sspec()],
        out_specs=(vspec(),) * 3,
        scratch_shapes=[
            VMEM((LANES, LANES), F32),
            VMEM((LANES, LANES), F32),
            VMEM((DEPTH, m), BF16),
            VMEM((8, m), F32),
            VMEM((2 * ROWS, qt), F32),
            VMEM((2 * ROWS, qt), F32),
        ],
        compiler_params=params(BUILD),
        cost_estimate=pl.CostEstimate(flops=n * m * 1000, bytes_accessed=n * m * 3, transcendentals=2 * n * m),
        name="build",
    )(other, other, table, left, steps, vec, small, scale, b, noise.reshape(1, n), flag)


def apply_body(khi_ref, klo_ref, w_ref, noise_ref, flag_ref, out_ref, nat, vec, small, *, pt):
    n, m = khi_ref.shape
    unpack(w_ref, nat, m // LANES)
    vec[...], small[...], scale = factors(nat[0:PROBES, :])
    clear_rest(out_ref, n // LANES)
    dims = (((1,), (1,)), ((), ()))

    def row(ip, _):
        op = pl.ds(pl.multiple_of(ip * pt, pt), pt)
        y = lax.dot_general(vec[...], khi_ref[op, :], dims, preferred_element_type=F32)
        z = lax.dot_general(small[...], klo_ref[op, :], dims, preferred_element_type=F32)
        res = (y[0:ROWS] + y[ROWS:])[0:PROBES] + scale * (z[0:ROWS] + z[ROWS:])[0:PROBES]
        res = res + flag_ref[0] * (noise_ref[:, op] * nat[0:PROBES, op])
        for t in range(pt // LANES):
            pack_tile(out_ref, res[:, t * LANES : (t + 1) * LANES], ip * (pt // LANES) + t, n // LANES)
        return 0

    lax.fori_loop(0, n // pt, row, 0)


def apply(khi, klo, w, noise, flag, pt=512):
    n, m = khi.shape
    khi = pltpu.with_memory_space_constraint(khi, VMEM)
    klo = pltpu.with_memory_space_constraint(klo, VMEM)
    return pl.pallas_call(
        functools.partial(apply_body, pt=pt),
        out_shape=jax.ShapeDtypeStruct((SIDE, ROWS, LANES), F32),
        in_specs=[vspec()] * 4 + [sspec()],
        out_specs=vspec(),
        scratch_shapes=[VMEM((ROWS, m), F32), VMEM((2 * ROWS, m), BF16), VMEM((2 * ROWS, m), F8)],
        compiler_params=params(4),
        cost_estimate=pl.CostEstimate(flops=n * m * 600, bytes_accessed=n * m * 3, transcendentals=0),
        name="apply",
    )(khi, klo, w, noise.reshape(1, n), flag)


def first_sum_body(in_ref, out_ref):
    total = jnp.sum(in_ref[...], axis=0)
    for s in range(SIDE):
        out_ref[s] = total


def first_sum(got):
    return pl.pallas_call(
        first_sum_body,
        out_shape=jax.ShapeDtypeStruct((SIDE, ROWS, LANES), F32),
        in_specs=[vspec()],
        out_specs=vspec(),
        compiler_params=params(),
        name="first_sum",
    )(got)


def scalar_body(b_ref, w_ref, z_ref, out_ref, nw, nz):
    tiles = b_ref.shape[1] // LANES
    unpack(w_ref, nw, tiles)
    unpack(z_ref, nz, tiles)
    b, w, z = b_ref[...], nw[0:PROBES, :], nz[0:PROBES, :]

    def dot(x, y):
        return jnp.sum(x * y, axis=1, keepdims=True)

    ww, bw = dot(w, w), dot(b, w)
    near = jnp.where(ww > 0.0, bw / ww, 0.0)
    r = b - near * w
    line = jnp.zeros((1, LANES), F32)
    for k, value in enumerate((dot(b, b), bw, ww, near, dot(r, r), dot(r, w), dot(r, z), dot(w, z))):
        line = line + to_lanes(value, ROWS * k)
    for s in range(SIDE):
        out_ref[s] = jnp.broadcast_to(line, (MORE - ROWS, LANES))


def scalars(b, w, z):
    n = b.shape[1]
    return pl.pallas_call(
        scalar_body,
        out_shape=jax.ShapeDtypeStruct((SIDE, MORE - ROWS, LANES), F32),
        in_specs=[vspec()] * 3,
        out_specs=vspec(),
        scratch_shapes=[VMEM((ROWS, n), F32), VMEM((ROWS, n), F32)],
        compiler_params=params(),
        name="scalars",
    )(b, w, z)


def second_sum_body(in_ref, line_ref, out_ref):
    total = jnp.sum(in_ref[...], axis=0)
    blocks = jnp.concatenate([line_ref[s, 0:1, :] for s in range(SIDE)], axis=0)

    def part(k):
        return blocks if k == 0 else pltpu.roll(blocks, LANES - ROWS * k, 1)

    def over(x):
        return jnp.sum(x, axis=0, keepdims=True)

    bb, bw, ww, near, rr, rw, rz, wz = (part(k) for k in range(8))
    all_bb, all_bw = over(bb), over(bw)
    shift = near - all_bb / all_bw
    lines = [over(rz + shift * wz), over(rr + shift * (2.0 * rw + shift * ww)), over(rw + shift * ww), all_bb, all_bw]
    lines = jnp.concatenate(lines + [jnp.zeros((3, LANES), F32)], axis=0)
    for s in range(SIDE):
        out_ref[s, 0:ROWS, :] = total
        out_ref[s, ROWS:MORE, :] = lines


def second_sum(got, line):
    return pl.pallas_call(
        second_sum_body,
        out_shape=jax.ShapeDtypeStruct((SIDE, MORE, LANES), F32),
        in_specs=[vspec(), vspec()],
        out_specs=vspec(),
        compiler_params=params(),
        name="second_sum",
    )(got, line)


def finish_body(b_ref, w_ref, a_ref, x_ref, r_ref, nw, na):
    tiles = b_ref.shape[1] // LANES
    unpack(w_ref, nw, tiles)
    unpack(a_ref, na, tiles)
    rz = to_column(jnp.sum(a_ref[:, ROWS:MORE, :], axis=0)[0:1], 0)
    rr, rw, bb, bw = (to_column(a_ref[0, ROWS + k : ROWS + k + 1, :], 0) for k in range(1, 5))
    first = bb / bw
    beta = rr / bb
    second = rr / ((rw - first * rz) + 2.0 * beta * rw + beta * beta * bw)
    b = b_ref[...]
    w = nw[0:PROBES, :]
    r = b - first * w
    x_ref[...] = first * b + second * (r + beta * b)
    r_ref[...] = r - second * ((w - first * na[0:PROBES, :]) + beta * w)


def finish(b, w, a):
    n = b.shape[1]
    out = jax.ShapeDtypeStruct((PROBES, n), F32)
    return pl.pallas_call(
        finish_body,
        out_shape=(out, out),
        in_specs=[vspec()] * 3,
        out_specs=(vspec(), vspec()),
        scratch_shapes=[VMEM((ROWS, n), F32), VMEM((ROWS, n), F32)],
        compiler_params=params(),
        name="finish",
    )(b, w, a)


def on_device(right_side, noise_level, run_index, step_index, run_features):
    swap = [(i * SIDE + j, j * SIDE + i) for i in range(SIDE) for j in range(SIDE)]

    def swapped(x):
        return lax.ppermute(x, ("row", "col"), swap)

    def exchange(x, axis):
        return lax.all_to_all(x, axis, 0, 0)

    flag = (lax.axis_index("row") == lax.axis_index("col")).astype(F32).reshape(1)
    tiles = run_index.shape[0] // LANES
    code = codes(run_index).reshape(tiles, LANES)
    step = step_index.reshape(tiles, LANES)
    other = swapped(jnp.stack([code, step]))
    mine = own(code, step, run_features, right_side)
    khi, klo, part = build(other, *mine, right_side, noise_level, flag)
    product = exchange(first_sum(exchange(part, "row")), "row")
    own_product = swapped(product)
    part = apply(khi, klo, product, noise_level, flag)
    summed = exchange(part, "col")
    line = exchange(scalars(right_side, own_product, part), "row")
    again = exchange(second_sum(summed, line), "col")
    return finish(right_side, own_product, again)


def solution(mesh):
    return jax.shard_map(
        on_device,
        mesh=mesh,
        in_specs=(P(None, "row"), P("row"), P("row"), P("row"), P()),
        out_specs=(P(None, "row"), P(None, "row")),
        check_vma=False,
    )
```

```python
import functools
import math

import jax
import jax.numpy as jnp
from jax import lax
from jax.experimental import pallas as pl
from jax.experimental.pallas import tpu as pltpu
from jax.sharding import PartitionSpec as P

LANES = 128
SIDE = 16
FEAT = 16
PROBES = 9
ROWS = 16
BUILD = 8
BOTH = 32
MORE = 40
LINES = 8
GROUP = 4096
DEPTH = 128
LOG2E = 1.4426950408889634
F32 = jnp.float32
BF16 = jnp.bfloat16
F8 = jnp.float8_e4m3fn
TOP = 240.0
LIFT = 65536.0
VMEM = pltpu.VMEM
MIB = 1024 * 1024


def vspec():
    return pl.BlockSpec(memory_space=VMEM)


def sspec():
    return pl.BlockSpec(memory_space=pltpu.SMEM)


def params(mib=2):
    return pltpu.CompilerParams(vmem_limit_bytes=mib * MIB)


def thirds(x):
    a = x.astype(BF16).astype(F32)
    b = (x - a).astype(BF16).astype(F32)
    return a, b, x - a - b


def to_column(row, first):
    lane = lax.broadcasted_iota(jnp.int32, (PROBES, LANES), 1)
    sub = lax.broadcasted_iota(jnp.int32, (PROBES, LANES), 0)
    return jnp.sum(jnp.where(lane == sub + first, row, 0.0), axis=1, keepdims=True)


def unpack(v_ref, nat, tiles, first=0):
    for t in range(tiles):
        lanes = slice(t * LANES, (t + 1) * LANES)
        row = first + 8 * (t % 2)
        nat[0:8, lanes] = v_ref[t // 2, row : row + 8, :]
        m = 8 * tiles + t
        row = first + m % ROWS
        nat[8:9, lanes] = v_ref[m // ROWS, row : row + 1, :]


def pack_tile(out_ref, res, tile, tiles):
    out_ref[tile // 2, pl.ds(pl.multiple_of(8 * (tile % 2), 8), 8), :] = res[0:8]
    m = 8 * tiles + tile
    out_ref[m // ROWS, pl.ds(m % ROWS, 1), :] = res[8:9]


def clear_rest(out_ref, tiles):
    m = 9 * tiles
    out_ref[m // ROWS, m % ROWS : ROWS, :] = jnp.zeros((ROWS - m % ROWS, LANES), F32)
    for s in range(m // ROWS + 1, SIDE):
        out_ref[s, 0:ROWS, :] = jnp.zeros((ROWS, LANES), F32)


def factors(v):
    zero = jnp.zeros((ROWS - PROBES, v.shape[1]), F32)
    high = v.astype(BF16).astype(F32)
    halves = jnp.concatenate([high, zero, v - high, zero], axis=0).astype(BF16)
    top = jnp.max(jnp.abs(v), axis=1, keepdims=True)
    top = jnp.where(top > 0.0, top, 1.0)
    u = v * (TOP / top)
    coarse = u.astype(F8).astype(F32)
    small = jnp.concatenate([coarse, zero, (u - coarse), zero], axis=0).astype(F8)
    return halves, small, top * (1.0 / (TOP * LIFT))


def own_body(idx_ref, run_ref, step_ref, tab_ref, out_ref, tab, table, runs, steps, rows_a, rows_b, sems):
    tiles = out_ref.shape[0] // (FEAT + 1)
    groups = tab_ref.shape[1] // GROUP
    width = GROUP // 4
    loads = [pltpu.make_async_copy(run_ref, runs, sems.at[0]), pltpu.make_async_copy(step_ref, steps, sems.at[1])]
    for load in loads:
        load.start()
    parts = []
    for c in range(4):
        for g in range(groups):
            at = pl.ds(g * GROUP + c * width, width)
            parts.append(pltpu.make_async_copy(tab_ref.at[:, at], tab.at[:, at], sems.at[2 + c * groups + g]))
    for part in parts:
        part.start()
    blank = jnp.zeros((LANES - groups * FEAT, LANES), F32)
    for c in range(4):
        for part in parts[c * groups : (c + 1) * groups]:
            part.wait()
        for t in range(c * (width // LANES), (c + 1) * (width // LANES)):
            pieces = [tab[:, g * GROUP + t * LANES : g * GROUP + (t + 1) * LANES] for g in range(groups)]
            table[t * LANES : (t + 1) * LANES, :] = jnp.transpose(jnp.concatenate(pieces + [blank], axis=0))
    for load in loads:
        load.wait()
    out_ref[FEAT * tiles :, :] = steps[...].astype(F32)
    lane = (lax.broadcasted_iota(jnp.int32, (LANES, LANES), 1) >> 4).astype(F32)
    pick = lax.broadcasted_iota(jnp.int32, (FEAT, LANES), 1) & (FEAT - 1)
    pick = jnp.where(pick == lax.broadcasted_iota(jnp.int32, (FEAT, LANES), 0), 1.0, 0.0).astype(BF16)

    def fetch(t, rows):
        for p in range(LANES):
            rows[p : p + 1, :] = table[pl.ds(idx_ref[t, p] & (GROUP - 1), 1), :]

    def make(t, rows):
        group = (runs[pl.ds(t, 1), :] >> 12).astype(F32)
        group = jnp.transpose(jnp.broadcast_to(group, (LANES, LANES)))
        mine = jnp.where(lane == group, rows[...], 0.0)
        got = None
        for part in thirds(mine):
            moved = lax.dot_general(pick, part.astype(BF16), (((1,), (1,)), ((), ())), preferred_element_type=F32)
            got = moved if got is None else got + moved
        out_ref[pl.ds(t, FEAT, stride=tiles), :] = got

    def pair(h, _):
        fetch(2 * h + 1, rows_b)
        make(2 * h, rows_a)
        fetch(jnp.minimum(2 * h + 2, tiles - 1), rows_a)
        make(2 * h + 1, rows_b)
        return 0

    fetch(0, rows_a)
    lax.fori_loop(0, tiles // 2, pair, 0)


def hbm(x):
    return pltpu.with_memory_space_constraint(x, pltpu.HBM)


def own(run, step, table):
    tiles = run.shape[0]
    ids = VMEM((tiles, LANES), jnp.int32)
    rows = VMEM((LANES, LANES), F32)
    anywhere = pl.BlockSpec(memory_space=pl.ANY)
    return pl.pallas_call(
        own_body,
        out_shape=jax.ShapeDtypeStruct(((FEAT + 1) * tiles, LANES), F32),
        in_specs=[sspec()] + [anywhere] * 3,
        out_specs=vspec(),
        scratch_shapes=[
            VMEM(table.shape, F32),
            VMEM((GROUP, LANES), F32),
            ids,
            ids,
            rows,
            rows,
            pltpu.SemaphoreType.DMA((2 + 4 * (table.shape[1] // GROUP),)),
        ],
        compiler_params=params(8),
        cost_estimate=pl.CostEstimate(flops=tiles * 800000, bytes_accessed=4 * table.size, transcendentals=0),
        name="own",
    )(run, hbm(run), hbm(step), hbm(table))


def operand(f, is_left):
    f = f * math.sqrt(LOG2E)
    a, b, c = thirds(f)
    norm = -0.5 * jnp.sum(f * f, axis=0, keepdims=True)
    if is_left:
        norm = norm + 1.5 * math.log2(8.0)
    na, nb, nc = thirds(norm)
    one = jnp.ones_like(norm)
    if is_left:
        parts = [a, a, b, b, a, c, na, nb, nc, one, one, one]
    else:
        parts = [a, b, a, b, c, a, one, one, one, na, nb, nc]
    return jnp.concatenate(parts + [jnp.zeros((DEPTH - 6 * FEAT - 6, f.shape[1]), F32)], axis=0)


def pack(out_ref, v, tiles):
    clear_rest(out_ref, tiles)
    for t in range(tiles):
        pack_tile(out_ref, v[:, t * LANES : (t + 1) * LANES], t, tiles)


def left_body(feat, b_ref, left, steps, vec, small, scale, packed):
    tiles = feat.shape[0] // (FEAT + 1)
    for t in range(tiles):
        o = slice(t * LANES, (t + 1) * LANES)
        left[o, :] = jnp.transpose(operand(feat[pl.ds(t, FEAT, stride=tiles), :], True)).astype(BF16)
        step = feat[FEAT * tiles + t : FEAT * tiles + t + 1, :] + 8.0
        steps[o, :] = jnp.transpose(jnp.broadcast_to(step, (LANES, LANES)))
    vec[...], small[...], factor = factors(b_ref[...])
    scale[...] = jnp.concatenate([jnp.broadcast_to(factor, (PROBES, LANES)), jnp.zeros((ROWS - PROBES, LANES), F32)], axis=0)
    pack(packed, b_ref[...], tiles)


def left_side(feat, b):
    n = b.shape[1]
    return pl.pallas_call(
        left_body,
        out_shape=(
            VMEM((n, LANES), BF16),
            VMEM((n, LANES), F32),
            VMEM((2 * ROWS, n), BF16),
            VMEM((2 * ROWS, n), F8),
            VMEM((ROWS, LANES), F32),
            jax.ShapeDtypeStruct((SIDE, ROWS, LANES), F32),
        ),
        in_specs=[vspec()] * 2,
        out_specs=(vspec(),) * 6,
        compiler_params=params(4),
        cost_estimate=pl.CostEstimate(flops=n * 1000, bytes_accessed=400 * n, transcendentals=0),
        name="left_side",
    )(feat, b)


def build_body(feat, left, steps, vec, small, scale, b_ref, noise_ref, flag_ref,
               khi_ref, klo_ref, out_ref, right, right_steps, acc, acc8, *, pt, qt):
    n, m = khi_ref.shape
    tiles = m // LANES
    for t in range(tiles):
        o = slice(t * LANES, (t + 1) * LANES)
        right[:, o] = operand(feat[pl.ds(t, FEAT, stride=tiles), :], False).astype(BF16)
        right_steps[0:1, o] = feat[FEAT * tiles + t : FEAT * tiles + t + 1, :]

    def column(jq, _):
        oq = pl.ds(pl.multiple_of(jq * qt, qt), qt)
        right_tile = right[:, oq]
        right_step = right_steps[0:1, oq]
        acc[...] = jnp.zeros_like(acc)
        acc8[...] = jnp.zeros_like(acc8)

        def row(ip, _):
            op = pl.ds(pl.multiple_of(ip * pt, pt), pt)
            power = jnp.dot(left[op, :], right_tile, preferred_element_type=F32)
            spread = jnp.concatenate([steps[op, :]] * (qt // LANES), axis=1) + right_step
            root = lax.rsqrt(spread)
            k = jnp.exp2(power) * (root * (root * root))
            high = k.astype(BF16)
            low = ((k - high.astype(F32)) * LIFT).astype(F8)
            khi_ref[op, oq] = high
            klo_ref[op, oq] = low
            acc[...] += jnp.dot(vec[:, op], high, preferred_element_type=F32)
            acc8[...] += jnp.dot(small[:, op], low, preferred_element_type=F32)
            return 0

        lax.fori_loop(0, n // pt, row, 0, unroll=n // pt)
        res = acc[0:ROWS, :] + acc[ROWS:, :] + scale[:, 0:1] * (acc8[0:ROWS, :] + acc8[ROWS:, :])
        res = res[0:PROBES] + flag_ref[0] * (noise_ref[:, oq] * b_ref[:, oq])
        for t in range(qt // LANES):
            pack_tile(out_ref, res[:, t * LANES : (t + 1) * LANES], jq * (qt // LANES) + t, tiles)
        return 0

    clear_rest(out_ref, tiles)
    lax.fori_loop(0, m // qt, column, 0)


def build(feat, left, steps, vec, small, scale, b, noise, flag, pt=3072, qt=256):
    n = b.shape[1]
    m = feat.shape[0] // (FEAT + 1) * LANES
    return pl.pallas_call(
        functools.partial(build_body, pt=pt, qt=qt),
        out_shape=(VMEM((n, m), BF16), VMEM((n, m), F8), jax.ShapeDtypeStruct((SIDE, ROWS, LANES), F32)),
        in_specs=[vspec()] * 8 + [sspec()],
        out_specs=(vspec(),) * 3,
        scratch_shapes=[
            VMEM((DEPTH, m), BF16),
            VMEM((8, m), F32),
            VMEM((2 * ROWS, qt), F32),
            VMEM((2 * ROWS, qt), F32),
        ],
        compiler_params=params(BUILD),
        cost_estimate=pl.CostEstimate(flops=n * m * 1000, bytes_accessed=n * m * 3, transcendentals=2 * n * m),
        name="build",
    )(feat, left, steps, vec, small, scale, b, noise.reshape(1, n), flag)


def apply_body(khi_ref, klo_ref, w_ref, noise_ref, flag_ref, out_ref, nat, vec, small, *, pt):
    n, m = khi_ref.shape
    unpack(w_ref, nat, m // LANES)
    vec[...], small[...], scale = factors(nat[0:PROBES, :])
    clear_rest(out_ref, n // LANES)
    for s in range(SIDE):
        out_ref[s, ROWS:BOTH, :] = flag_ref[0] * w_ref[s]
    dims = (((1,), (1,)), ((), ()))

    def row(ip, _):
        op = pl.ds(pl.multiple_of(ip * pt, pt), pt)
        y = lax.dot_general(vec[...], khi_ref[op, :], dims, preferred_element_type=F32)
        z = lax.dot_general(small[...], klo_ref[op, :], dims, preferred_element_type=F32)
        res = (y[0:ROWS] + y[ROWS:])[0:PROBES] + scale * (z[0:ROWS] + z[ROWS:])[0:PROBES]
        res = res + flag_ref[0] * (noise_ref[:, op] * nat[0:PROBES, op])
        for t in range(pt // LANES):
            pack_tile(out_ref, res[:, t * LANES : (t + 1) * LANES], ip * (pt // LANES) + t, n // LANES)
        return 0

    lax.fori_loop(0, n // pt, row, 0)


def apply(khi, klo, w, noise, flag, pt=512):
    n, m = khi.shape
    khi = pltpu.with_memory_space_constraint(khi, VMEM)
    klo = pltpu.with_memory_space_constraint(klo, VMEM)
    return pl.pallas_call(
        functools.partial(apply_body, pt=pt),
        out_shape=jax.ShapeDtypeStruct((SIDE, BOTH, LANES), F32),
        in_specs=[vspec()] * 4 + [sspec()],
        out_specs=vspec(),
        scratch_shapes=[VMEM((ROWS, m), F32), VMEM((2 * ROWS, m), BF16), VMEM((2 * ROWS, m), F8)],
        compiler_params=params(4),
        cost_estimate=pl.CostEstimate(flops=n * m * 600, bytes_accessed=n * m * 3, transcendentals=0),
        name="apply",
    )(khi, klo, w, noise.reshape(1, n), flag)


def first_sum_body(in_ref, out_ref):
    total = jnp.sum(in_ref[...], axis=0)
    for s in range(SIDE):
        out_ref[s] = total


def first_sum(got):
    return pl.pallas_call(
        first_sum_body,
        out_shape=jax.ShapeDtypeStruct((SIDE, ROWS, LANES), F32),
        in_specs=[vspec()],
        out_specs=vspec(),
        compiler_params=params(),
        name="first_sum",
    )(got)


def places(which):
    lane = lax.broadcasted_iota(jnp.int32, (ROWS, LANES), 1)
    row = lax.broadcasted_iota(jnp.int32, (ROWS, LANES), 0)
    return lane == jnp.where(which < 8 * 24 // ROWS, row & 7, 8)


def joined(blocks, first):
    def part(k):
        return blocks if k == 0 else pltpu.roll(blocks, LANES - ROWS * k, 1)

    def over(x):
        return jnp.sum(x, axis=0, keepdims=True)

    bb, bw, ww, near, rr, rw, rz, wz = (part(k) for k in range(8))
    all_bb, all_bw, all_ww = over(bb), over(bw), over(ww)
    middle = all_bb / all_bw if first else jnp.where(all_ww > 0.0, all_bw / all_ww, 0.0)
    shift = near - middle
    return (all_bb, all_bw, all_ww, middle, over(rr + shift * (2.0 * rw + shift * ww)), over(rw + shift * ww),
            over(rz + shift * wz), over(wz))


def put(lines):
    lane = lax.broadcasted_iota(jnp.int32, (1, LANES), 1)
    out = jnp.zeros((1, LANES), F32)
    for k, line in enumerate(lines):
        line = jnp.where(lane < PROBES, line, 0.0)
        out = out + (line if k == 0 else pltpu.roll(line, ROWS * k, 1))
    return out


def chunk_body(in_ref, b_ref, which_ref, chunk_ref, line_ref):
    total = jnp.sum(in_ref[...], axis=0)
    chunk_ref[...] = total
    which = which_ref[0]
    b, z, w = b_ref[which], total[0:ROWS], total[ROWS:BOTH]
    here = places(which)

    def dot(x, y):
        return jnp.sum(jnp.where(here, jnp.sum(x * y, axis=1, keepdims=True), 0.0), axis=0, keepdims=True)

    ww, bw = dot(w, w), dot(b, w)
    near = jnp.where(ww > 0.0, bw / ww, 0.0)
    r = b - jnp.sum(jnp.where(here, near, 0.0), axis=1, keepdims=True) * w
    line = put((dot(b, b), bw, ww, near, dot(r, r), dot(r, w), dot(r, z), dot(w, z)))
    for s in range(SIDE):
        line_ref[s] = jnp.broadcast_to(line, (LINES, LANES))


def chunk_sums(got, b, which):
    return pl.pallas_call(
        chunk_body,
        out_shape=(jax.ShapeDtypeStruct((BOTH, LANES), F32), jax.ShapeDtypeStruct((SIDE, LINES, LANES), F32)),
        in_specs=[vspec(), vspec(), sspec()],
        out_specs=(vspec(), vspec()),
        compiler_params=params(),
        name="chunk_sums",
    )(got, b, which)


def join_body(chunk_ref, line_ref, out_ref):
    line = put(joined(jnp.concatenate([line_ref[s, 0:1, :] for s in range(SIDE)], axis=0), False))
    for s in range(SIDE):
        out_ref[s, 0:BOTH, :] = chunk_ref[...]
        out_ref[s, BOTH:MORE, :] = jnp.broadcast_to(line, (MORE - BOTH, LANES))


def join(chunk, line):
    return pl.pallas_call(
        join_body,
        out_shape=jax.ShapeDtypeStruct((SIDE, MORE, LANES), F32),
        in_specs=[vspec(), vspec()],
        out_specs=vspec(),
        compiler_params=params(),
        name="join",
    )(chunk, line)


def finish_body(b_ref, a_ref, x_ref, r_ref, nw, na):
    tiles = b_ref.shape[1] // LANES
    unpack(a_ref, na, tiles)
    unpack(a_ref, nw, tiles, ROWS)
    lines = joined(jnp.concatenate([a_ref[s, BOTH : BOTH + 1, :] for s in range(SIDE)], axis=0), True)
    bb, bw, _, first, rr, rw, rz, _ = (to_column(line, 0) for line in lines)
    beta = rr / bb
    second = rr / ((rw - first * rz) + 2.0 * beta * rw + beta * beta * bw)
    b = b_ref[...]
    w = nw[0:PROBES, :]
    r = b - first * w
    x_ref[...] = first * b + second * (r + beta * b)
    r_ref[...] = r - second * ((w - first * na[0:PROBES, :]) + beta * w)


def finish(b, a):
    n = b.shape[1]
    out = jax.ShapeDtypeStruct((PROBES, n), F32)
    return pl.pallas_call(
        finish_body,
        out_shape=(out, out),
        in_specs=[vspec()] * 2,
        out_specs=(vspec(), vspec()),
        scratch_shapes=[VMEM((ROWS, n), F32), VMEM((ROWS, n), F32)],
        compiler_params=params(),
        name="finish",
    )(b, a)


def on_device(right_side, noise_level, run_index, step_index, run_features):
    swap = [(i * SIDE + j, j * SIDE + i) for i in range(SIDE) for j in range(SIDE)]

    def exchange(x, axis):
        return lax.all_to_all(x, axis, 0, 0)

    flag = (lax.axis_index("row") == lax.axis_index("col")).astype(F32).reshape(1)
    which = lax.axis_index("col").reshape(1)
    tiles = run_index.shape[0] // LANES
    feat = own(run_index.reshape(tiles, LANES), step_index.reshape(tiles, LANES), run_features)
    other = lax.ppermute(feat, ("row", "col"), swap)
    *mine, packed = left_side(feat, right_side)
    khi, klo, part = build(other, *mine, right_side, noise_level, flag)
    product = exchange(first_sum(exchange(part, "row")), "row")
    both = exchange(apply(khi, klo, product, noise_level, flag), "col")
    chunk, line = chunk_sums(both, packed, which)
    again = exchange(join(chunk, exchange(line, "row")), "col")
    return finish(right_side, again)


def solution(mesh):
    return jax.shard_map(
        on_device,
        mesh=mesh,
        in_specs=(P(None, "row"), P("row"), P("row"), P("row"), P()),
        out_specs=(P(None, "row"), P(None, "row")),
        check_vma=False,
    )
```

```python
import functools
import math

import jax
import jax.numpy as jnp
from jax import lax
from jax.experimental import pallas as pl
from jax.experimental.pallas import tpu as pltpu
from jax.sharding import PartitionSpec as P

LANES = 128
SIDE = 16
FEAT = 16
PROBES = 9
ROWS = 16
BUILD = 8
BOTH = 32
MORE = 40
LINES = 8
GROUP = 4096
DEPTH = 128
LOG2E = 1.4426950408889634
F32 = jnp.float32
BF16 = jnp.bfloat16
F8 = jnp.float8_e4m3fn
TOP = 240.0
LIFT = 65536.0
VMEM = pltpu.VMEM
MIB = 1024 * 1024


def vspec():
    return pl.BlockSpec(memory_space=VMEM)


def sspec():
    return pl.BlockSpec(memory_space=pltpu.SMEM)


def params(mib=2):
    return pltpu.CompilerParams(vmem_limit_bytes=mib * MIB)


def thirds(x):
    a = x.astype(BF16).astype(F32)
    b = (x - a).astype(BF16).astype(F32)
    return a, b, x - a - b


def to_column(row, first):
    lane = lax.broadcasted_iota(jnp.int32, (PROBES, LANES), 1)
    sub = lax.broadcasted_iota(jnp.int32, (PROBES, LANES), 0)
    return jnp.sum(jnp.where(lane == sub + first, row, 0.0), axis=1, keepdims=True)


def unpack(v_ref, nat, tiles, first=0):
    for t in range(tiles):
        lanes = slice(t * LANES, (t + 1) * LANES)
        row = first + 8 * (t % 2)
        nat[0:8, lanes] = v_ref[t // 2, row : row + 8, :]
        m = 8 * tiles + t
        row = first + m % ROWS
        nat[8:9, lanes] = v_ref[m // ROWS, row : row + 1, :]


def pack_tile(out_ref, res, tile, tiles):
    out_ref[tile // 2, pl.ds(pl.multiple_of(8 * (tile % 2), 8), 8), :] = res[0:8]
    m = 8 * tiles + tile
    out_ref[m // ROWS, pl.ds(m % ROWS, 1), :] = res[8:9]


def clear_rest(out_ref, tiles):
    m = 9 * tiles
    out_ref[m // ROWS, m % ROWS : ROWS, :] = jnp.zeros((ROWS - m % ROWS, LANES), F32)
    for s in range(m // ROWS + 1, SIDE):
        out_ref[s, 0:ROWS, :] = jnp.zeros((ROWS, LANES), F32)


def factors(v):
    zero = jnp.zeros((ROWS - PROBES, v.shape[1]), F32)
    high = v.astype(BF16).astype(F32)
    halves = jnp.concatenate([high, zero, v - high, zero], axis=0).astype(BF16)
    top = jnp.max(jnp.abs(v), axis=1, keepdims=True)
    top = jnp.where(top > 0.0, top, 1.0)
    u = v * (TOP / top)
    coarse = u.astype(F8).astype(F32)
    small = jnp.concatenate([coarse, zero, (u - coarse), zero], axis=0).astype(F8)
    return halves, small, top * (1.0 / (TOP * LIFT))


def fetch_features(read, table, runs, rows, use):
    tiles = rows.shape[0] // LANES

    def fetch(t, _):
        base = pl.multiple_of(t * LANES, LANES)
        for p in range(LANES):
            rows[pl.ds(base + p, 1), :] = table[pl.ds(read(t, p) & (GROUP - 1), 1), :]
        return 0

    lax.fori_loop(0, tiles, fetch, 0)
    for t in range(tiles):
        turned = jnp.transpose(rows[t * LANES : (t + 1) * LANES, :])
        group = runs[t : t + 1, :] >> 12
        f = turned[0:FEAT]
        for g in range(1, LANES // FEAT):
            f = jnp.where(group == g, turned[g * FEAT : (g + 1) * FEAT], f)
        use(t, f)


def pack(out_ref, v, tiles):
    clear_rest(out_ref, tiles)
    for t in range(tiles):
        pack_tile(out_ref, v[:, t * LANES : (t + 1) * LANES], t, tiles)


def operand(f, is_left):
    f = f * math.sqrt(LOG2E)
    a, b, c = thirds(f)
    norm = -0.5 * jnp.sum(f * f, axis=0, keepdims=True)
    if is_left:
        norm = norm + 1.5 * math.log2(8.0)
    na, nb, nc = thirds(norm)
    one = jnp.ones_like(norm)
    if is_left:
        parts = [a, a, b, b, a, c, na, nb, nc, one, one, one]
    else:
        parts = [a, b, a, b, c, a, one, one, one, na, nb, nc]
    return jnp.concatenate(parts + [jnp.zeros((DEPTH - 6 * FEAT - 6, f.shape[1]), F32)], axis=0)


def own_body(idx_ref, run_ref, step_ref, tab_ref, b_ref, table, left, steps, vec, small, scale, packed,
             tab, runs, own_steps, b, rows, sems):
    groups = tab_ref.shape[1] // GROUP
    width = GROUP // 4
    loads = [
        pltpu.make_async_copy(run_ref, runs, sems.at[0]),
        pltpu.make_async_copy(step_ref, own_steps, sems.at[1]),
        pltpu.make_async_copy(b_ref, b, sems.at[2]),
    ]
    parts = []
    for c in range(4):
        for g in range(groups):
            at = pl.ds(g * GROUP + c * width, width)
            parts.append(pltpu.make_async_copy(tab_ref.at[:, at], tab.at[:, at], sems.at[3 + c * groups + g]))
    for part in parts + loads:
        part.start()
    blank = jnp.zeros((LANES - groups * FEAT, LANES), F32)
    for c in range(4):
        for part in parts[c * groups : (c + 1) * groups]:
            part.wait()
        for t in range(c * (width // LANES), (c + 1) * (width // LANES)):
            pieces = [tab[:, g * GROUP + t * LANES : g * GROUP + (t + 1) * LANES] for g in range(groups)]
            table[t * LANES : (t + 1) * LANES, :] = jnp.transpose(jnp.concatenate(pieces + [blank], axis=0))
    for load in loads:
        load.wait()

    def use(t, f):
        o = slice(t * LANES, (t + 1) * LANES)
        left[o, :] = jnp.transpose(operand(f, True)).astype(BF16)
        step = own_steps[t : t + 1, :].astype(F32) + 8.0
        steps[o, :] = jnp.transpose(jnp.broadcast_to(step, (LANES, LANES)))

    fetch_features(lambda t, p: idx_ref[t, p], table, runs, rows, use)
    vec[...], small[...], factor = factors(b[...])
    scale[...] = jnp.concatenate([jnp.broadcast_to(factor, (PROBES, LANES)), jnp.zeros((ROWS - PROBES, LANES), F32)], axis=0)
    pack(packed, b[...], runs.shape[0])


def hbm(x):
    return pltpu.with_memory_space_constraint(x, pltpu.HBM)


def own(run, step, table, b):
    n = b.shape[1]
    ids = VMEM(run.shape, jnp.int32)
    return pl.pallas_call(
        own_body,
        out_shape=(
            VMEM((GROUP, LANES), F32),
            VMEM((n, LANES), BF16),
            VMEM((n, LANES), F32),
            VMEM((2 * ROWS, n), BF16),
            VMEM((2 * ROWS, n), F8),
            VMEM((ROWS, LANES), F32),
            jax.ShapeDtypeStruct((SIDE, ROWS, LANES), F32),
        ),
        in_specs=[sspec()] + [pl.BlockSpec(memory_space=pl.ANY)] * 4,
        out_specs=(vspec(),) * 7,
        scratch_shapes=[
            VMEM(table.shape, F32),
            ids,
            ids,
            VMEM(b.shape, F32),
            VMEM((n, LANES), F32),
            pltpu.SemaphoreType.DMA((3 + 4 * (table.shape[1] // GROUP),)),
        ],
        compiler_params=params(12),
        cost_estimate=pl.CostEstimate(flops=n * 6000, bytes_accessed=4 * table.size, transcendentals=0),
        name="own",
    )(run, hbm(run), hbm(step), hbm(table), hbm(b))


def build_body(idx_ref, other, table, left, steps, vec, small, scale, b_ref, noise_ref, flag_ref,
               khi_ref, klo_ref, out_ref, rows, right, right_steps, acc, acc8, *, pt, qt):
    n, m = khi_ref.shape
    tiles = m // LANES

    def use(t, f):
        o = slice(t * LANES, (t + 1) * LANES)
        right[:, o] = operand(f, False).astype(BF16)
        right_steps[0:1, o] = other[1, t : t + 1, :].astype(F32)

    fetch_features(lambda t, p: idx_ref[0, t, p], table, other.at[0], rows, use)

    def column(jq, _):
        oq = pl.ds(pl.multiple_of(jq * qt, qt), qt)
        right_tile = right[:, oq]
        right_step = right_steps[0:1, oq]
        acc[...] = jnp.zeros_like(acc)
        acc8[...] = jnp.zeros_like(acc8)

        def row(ip, _):
            op = pl.ds(pl.multiple_of(ip * pt, pt), pt)
            power = jnp.dot(left[op, :], right_tile, preferred_element_type=F32)
            spread = jnp.concatenate([steps[op, :]] * (qt // LANES), axis=1) + right_step
            root = lax.rsqrt(spread)
            k = jnp.exp2(power) * (root * (root * root))
            high = k.astype(BF16)
            low = ((k - high.astype(F32)) * LIFT).astype(F8)
            khi_ref[op, oq] = high
            klo_ref[op, oq] = low
            acc[...] += jnp.dot(vec[:, op], high, preferred_element_type=F32)
            acc8[...] += jnp.dot(small[:, op], low, preferred_element_type=F32)
            return 0

        lax.fori_loop(0, n // pt, row, 0, unroll=n // pt)
        res = acc[0:ROWS, :] + acc[ROWS:, :] + scale[:, 0:1] * (acc8[0:ROWS, :] + acc8[ROWS:, :])
        res = res[0:PROBES] + flag_ref[0] * (noise_ref[:, oq] * b_ref[:, oq])
        for t in range(qt // LANES):
            pack_tile(out_ref, res[:, t * LANES : (t + 1) * LANES], jq * (qt // LANES) + t, tiles)
        return 0

    clear_rest(out_ref, tiles)
    lax.fori_loop(0, m // qt, column, 0)


def build(other, table, left, steps, vec, small, scale, b, noise, flag, pt=3072, qt=256):
    n = b.shape[1]
    m = other.shape[1] * LANES
    return pl.pallas_call(
        functools.partial(build_body, pt=pt, qt=qt),
        out_shape=(VMEM((n, m), BF16), VMEM((n, m), F8), jax.ShapeDtypeStruct((SIDE, ROWS, LANES), F32)),
        in_specs=[sspec()] + [vspec()] * 9 + [sspec()],
        out_specs=(vspec(),) * 3,
        scratch_shapes=[
            VMEM((m, LANES), F32),
            VMEM((DEPTH, m), BF16),
            VMEM((8, m), F32),
            VMEM((2 * ROWS, qt), F32),
            VMEM((2 * ROWS, qt), F32),
        ],
        compiler_params=params(BUILD),
        cost_estimate=pl.CostEstimate(flops=n * m * 1000, bytes_accessed=n * m * 3, transcendentals=2 * n * m),
        name="build",
    )(other, other, table, left, steps, vec, small, scale, b, noise.reshape(1, n), flag)


def apply_body(khi_ref, klo_ref, w_ref, noise_ref, flag_ref, out_ref, nat, vec, small, *, pt):
    n, m = khi_ref.shape
    unpack(w_ref, nat, m // LANES)
    vec[...], small[...], scale = factors(nat[0:PROBES, :])
    clear_rest(out_ref, n // LANES)
    for s in range(SIDE):
        out_ref[s, ROWS:BOTH, :] = flag_ref[0] * w_ref[s]
    dims = (((1,), (1,)), ((), ()))

    def row(ip, _):
        op = pl.ds(pl.multiple_of(ip * pt, pt), pt)
        y = lax.dot_general(vec[...], khi_ref[op, :], dims, preferred_element_type=F32)
        z = lax.dot_general(small[...], klo_ref[op, :], dims, preferred_element_type=F32)
        res = (y[0:ROWS] + y[ROWS:])[0:PROBES] + scale * (z[0:ROWS] + z[ROWS:])[0:PROBES]
        res = res + flag_ref[0] * (noise_ref[:, op] * nat[0:PROBES, op])
        for t in range(pt // LANES):
            pack_tile(out_ref, res[:, t * LANES : (t + 1) * LANES], ip * (pt // LANES) + t, n // LANES)
        return 0

    lax.fori_loop(0, n // pt, row, 0)


def apply(khi, klo, w, noise, flag, pt=512):
    n, m = khi.shape
    khi = pltpu.with_memory_space_constraint(khi, VMEM)
    klo = pltpu.with_memory_space_constraint(klo, VMEM)
    return pl.pallas_call(
        functools.partial(apply_body, pt=pt),
        out_shape=jax.ShapeDtypeStruct((SIDE, BOTH, LANES), F32),
        in_specs=[vspec()] * 4 + [sspec()],
        out_specs=vspec(),
        scratch_shapes=[VMEM((ROWS, m), F32), VMEM((2 * ROWS, m), BF16), VMEM((2 * ROWS, m), F8)],
        compiler_params=params(4),
        cost_estimate=pl.CostEstimate(flops=n * m * 600, bytes_accessed=n * m * 3, transcendentals=0),
        name="apply",
    )(khi, klo, w, noise.reshape(1, n), flag)


def first_sum_body(in_ref, out_ref):
    total = jnp.sum(in_ref[...], axis=0)
    for s in range(SIDE):
        out_ref[s] = total


def first_sum(got):
    return pl.pallas_call(
        first_sum_body,
        out_shape=jax.ShapeDtypeStruct((SIDE, ROWS, LANES), F32),
        in_specs=[vspec()],
        out_specs=vspec(),
        compiler_params=params(),
        name="first_sum",
    )(got)


def places(which):
    lane = lax.broadcasted_iota(jnp.int32, (ROWS, LANES), 1)
    row = lax.broadcasted_iota(jnp.int32, (ROWS, LANES), 0)
    return lane == jnp.where(which < 8 * 24 // ROWS, row & 7, 8)


def joined(blocks, first):
    def part(k):
        return blocks if k == 0 else pltpu.roll(blocks, LANES - ROWS * k, 1)

    def over(x):
        return jnp.sum(x, axis=0, keepdims=True)

    bb, bw, ww, near, rr, rw, rz, wz = (part(k) for k in range(8))
    all_bb, all_bw, all_ww = over(bb), over(bw), over(ww)
    middle = all_bb / all_bw if first else jnp.where(all_ww > 0.0, all_bw / all_ww, 0.0)
    shift = near - middle
    return (all_bb, all_bw, all_ww, middle, over(rr + shift * (2.0 * rw + shift * ww)), over(rw + shift * ww),
            over(rz + shift * wz), over(wz))


def put(lines):
    lane = lax.broadcasted_iota(jnp.int32, (1, LANES), 1)
    out = jnp.zeros((1, LANES), F32)
    for k, line in enumerate(lines):
        line = jnp.where(lane < PROBES, line, 0.0)
        out = out + (line if k == 0 else pltpu.roll(line, ROWS * k, 1))
    return out


def chunk_body(in_ref, b_ref, which_ref, chunk_ref, line_ref):
    total = jnp.sum(in_ref[...], axis=0)
    chunk_ref[...] = total
    which = which_ref[0]
    b, z, w = b_ref[which], total[0:ROWS], total[ROWS:BOTH]
    here = places(which)

    def dot(x, y):
        return jnp.sum(jnp.where(here, jnp.sum(x * y, axis=1, keepdims=True), 0.0), axis=0, keepdims=True)

    ww, bw = dot(w, w), dot(b, w)
    near = jnp.where(ww > 0.0, bw / ww, 0.0)
    r = b - jnp.sum(jnp.where(here, near, 0.0), axis=1, keepdims=True) * w
    line = put((dot(b, b), bw, ww, near, dot(r, r), dot(r, w), dot(r, z), dot(w, z)))
    for s in range(SIDE):
        line_ref[s] = jnp.broadcast_to(line, (LINES, LANES))


def chunk_sums(got, b, which):
    return pl.pallas_call(
        chunk_body,
        out_shape=(jax.ShapeDtypeStruct((BOTH, LANES), F32), jax.ShapeDtypeStruct((SIDE, LINES, LANES), F32)),
        in_specs=[vspec(), vspec(), sspec()],
        out_specs=(vspec(), vspec()),
        compiler_params=params(),
        name="chunk_sums",
    )(got, b, which)


def join_body(chunk_ref, line_ref, out_ref):
    line = put(joined(jnp.concatenate([line_ref[s, 0:1, :] for s in range(SIDE)], axis=0), False))
    for s in range(SIDE):
        out_ref[s, 0:BOTH, :] = chunk_ref[...]
        out_ref[s, BOTH:MORE, :] = jnp.broadcast_to(line, (MORE - BOTH, LANES))


def join(chunk, line):
    return pl.pallas_call(
        join_body,
        out_shape=jax.ShapeDtypeStruct((SIDE, MORE, LANES), F32),
        in_specs=[vspec(), vspec()],
        out_specs=vspec(),
        compiler_params=params(),
        name="join",
    )(chunk, line)


def finish_body(b_ref, a_ref, x_ref, r_ref, nw, na):
    tiles = b_ref.shape[1] // LANES
    unpack(a_ref, na, tiles)
    unpack(a_ref, nw, tiles, ROWS)
    lines = joined(jnp.concatenate([a_ref[s, BOTH : BOTH + 1, :] for s in range(SIDE)], axis=0), True)
    bb, bw, _, first, rr, rw, rz, _ = (to_column(line, 0) for line in lines)
    beta = rr / bb
    second = rr / ((rw - first * rz) + 2.0 * beta * rw + beta * beta * bw)
    b = b_ref[...]
    w = nw[0:PROBES, :]
    r = b - first * w
    x_ref[...] = first * b + second * (r + beta * b)
    r_ref[...] = r - second * ((w - first * na[0:PROBES, :]) + beta * w)


def finish(b, a):
    n = b.shape[1]
    out = jax.ShapeDtypeStruct((PROBES, n), F32)
    return pl.pallas_call(
        finish_body,
        out_shape=(out, out),
        in_specs=[vspec()] * 2,
        out_specs=(vspec(), vspec()),
        scratch_shapes=[VMEM((ROWS, n), F32), VMEM((ROWS, n), F32)],
        compiler_params=params(),
        name="finish",
    )(b, a)


def on_device(right_side, noise_level, run_index, step_index, run_features):
    swap = [(i * SIDE + j, j * SIDE + i) for i in range(SIDE) for j in range(SIDE)]

    def exchange(x, axis):
        return lax.all_to_all(x, axis, 0, 0)

    flag = (lax.axis_index("row") == lax.axis_index("col")).astype(F32).reshape(1)
    which = lax.axis_index("col").reshape(1)
    tiles = run_index.shape[0] // LANES
    run = run_index.reshape(tiles, LANES)
    step = step_index.reshape(tiles, LANES)
    other = lax.ppermute(jnp.stack([run, step]), ("row", "col"), swap)
    *mine, packed = own(run, step, run_features, right_side)
    khi, klo, part = build(other, *mine, right_side, noise_level, flag)
    product = exchange(first_sum(exchange(part, "row")), "row")
    both = exchange(apply(khi, klo, product, noise_level, flag), "col")
    chunk, line = chunk_sums(both, packed, which)
    again = exchange(join(chunk, exchange(line, "row")), "col")
    return finish(right_side, again)


def solution(mesh):
    return jax.shard_map(
        on_device,
        mesh=mesh,
        in_specs=(P(None, "row"), P("row"), P("row"), P("row"), P()),
        out_specs=(P(None, "row"), P(None, "row")),
        check_vma=False,
    )
```

```python
import functools
import math

import jax
import jax.numpy as jnp
import numpy as np
from jax import lax
from jax.experimental import pallas as pl
from jax.experimental.pallas import tpu as pltpu
from jax.sharding import PartitionSpec as P

LANES = 128
SIDE = 16
FEAT = 16
PROBES = 9
ROWS = 16
BUILD = 8
BOTH = 32
MORE = 40
LINES = 8
GROUP = 4096
DEPTH = 256
RANK = 24
STEPS = 128
LOG2E = 1.4426950408889634
F32 = jnp.float32
BF16 = jnp.bfloat16
F8 = jnp.float8_e4m3fn
TOP = 240.0
LIFT = 65536.0
VMEM = pltpu.VMEM
MIB = 1024 * 1024


def vspec():
    return pl.BlockSpec(memory_space=VMEM)


def sspec():
    return pl.BlockSpec(memory_space=pltpu.SMEM)


def params(mib=2):
    return pltpu.CompilerParams(vmem_limit_bytes=mib * MIB)


def thirds(x):
    a = x.astype(BF16).astype(F32)
    b = (x - a).astype(BF16).astype(F32)
    return a, b, x - a - b


def to_column(row, first):
    lane = lax.broadcasted_iota(jnp.int32, (PROBES, LANES), 1)
    sub = lax.broadcasted_iota(jnp.int32, (PROBES, LANES), 0)
    return jnp.sum(jnp.where(lane == sub + first, row, 0.0), axis=1, keepdims=True)


def unpack(v_ref, nat, tiles, first=0):
    for t in range(tiles):
        lanes = slice(t * LANES, (t + 1) * LANES)
        row = first + 8 * (t % 2)
        nat[0:8, lanes] = v_ref[t // 2, row : row + 8, :]
        m = 8 * tiles + t
        row = first + m % ROWS
        nat[8:9, lanes] = v_ref[m // ROWS, row : row + 1, :]


def pack_tile(out_ref, res, tile, tiles):
    out_ref[tile // 2, pl.ds(pl.multiple_of(8 * (tile % 2), 8), 8), :] = res[0:8]
    m = 8 * tiles + tile
    out_ref[m // ROWS, pl.ds(m % ROWS, 1), :] = res[8:9]


def clear_rest(out_ref, tiles):
    m = 9 * tiles
    out_ref[m // ROWS, m % ROWS : ROWS, :] = jnp.zeros((ROWS - m % ROWS, LANES), F32)
    for s in range(m // ROWS + 1, SIDE):
        out_ref[s, 0:ROWS, :] = jnp.zeros((ROWS, LANES), F32)


def factors(v):
    zero = jnp.zeros((ROWS - PROBES, v.shape[1]), F32)
    high = v.astype(BF16).astype(F32)
    halves = jnp.concatenate([high, zero, v - high, zero], axis=0).astype(BF16)
    top = jnp.max(jnp.abs(v), axis=1, keepdims=True)
    top = jnp.where(top > 0.0, top, 1.0)
    u = v * (TOP / top)
    coarse = u.astype(F8).astype(F32)
    small = jnp.concatenate([coarse, zero, (u - coarse), zero], axis=0).astype(F8)
    return halves, small, top * (1.0 / (TOP * LIFT))


def fetch(read, table, rows, t, at):
    for p in range(LANES):
        rows[pl.ds(at + p, 1), :] = table[pl.ds(read(t, p) & (GROUP - 1), 1), :]


def turn(rows, run):
    turned = jnp.transpose(rows)
    group = run >> 12
    f = turned[0:FEAT]
    for g in range(1, LANES // FEAT):
        f = jnp.where(group == g, turned[g * FEAT : (g + 1) * FEAT], f)
    return f


def pack(out_ref, v, tiles):
    clear_rest(out_ref, tiles)
    for t in range(tiles):
        pack_tile(out_ref, v[:, t * LANES : (t + 1) * LANES], t, tiles)


def operand(f, is_left):
    f = f * math.sqrt(LOG2E)
    a, b, c = thirds(f)
    norm = -0.5 * jnp.sum(f * f, axis=0, keepdims=True)
    if is_left:
        norm = norm + math.log2(LIFT)
    na, nb, nc = thirds(norm)
    one = jnp.ones_like(norm)
    if is_left:
        parts = [a, a, b, b, a, c, na, nb, nc, one, one, one]
    else:
        parts = [a, b, a, b, c, a, one, one, one, na, nb, nc]
    return jnp.concatenate(parts + [jnp.zeros((2, f.shape[1]), F32)], axis=0)


def own_body(idx_ref, flag_ref, run_ref, step_ref, tab_ref, b_ref, noise_ref, decay_ref, right_ref,
             right_decay, table, left, vec, small, scale, extra_b, extra, packed,
             tab, runs, own_steps, b, noise, decay, rows, sems):
    groups = tab_ref.shape[1] // GROUP
    width = GROUP // 4
    loads = [
        pltpu.make_async_copy(run_ref, runs, sems.at[0]),
        pltpu.make_async_copy(step_ref, own_steps, sems.at[1]),
        pltpu.make_async_copy(b_ref, b, sems.at[2]),
        pltpu.make_async_copy(noise_ref, noise, sems.at[3]),
        pltpu.make_async_copy(decay_ref, decay, sems.at[4]),
        pltpu.make_async_copy(right_ref, right_decay, sems.at[5]),
    ]
    parts = []
    for c in range(4):
        for g in range(groups):
            at = pl.ds(g * GROUP + c * width, width)
            parts.append(pltpu.make_async_copy(tab_ref.at[:, at], tab.at[:, at], sems.at[6 + c * groups + g]))
    for part in parts + loads:
        part.start()
    blank = jnp.zeros((LANES - groups * FEAT, LANES), F32)
    for c in range(4):
        for part in parts[c * groups : (c + 1) * groups]:
            part.wait()
        for t in range(c * (width // LANES), (c + 1) * (width // LANES)):
            pieces = [tab[:, g * GROUP + t * LANES : g * GROUP + (t + 1) * LANES] for g in range(groups)]
            table[t * LANES : (t + 1) * LANES, :] = jnp.transpose(jnp.concatenate(pieces + [blank], axis=0))
    for load in loads:
        load.wait()

    tiles = runs.shape[0]

    def get(t, _):
        fetch(lambda t, p: idx_ref[t, p], table, rows, t, pl.multiple_of(t * LANES, LANES))
        return 0

    lax.fori_loop(0, tiles, get, 0)
    for t in range(tiles):
        o = slice(t * LANES, (t + 1) * LANES)
        f = turn(rows[o, :], runs[t : t + 1, :])
        hot = one_hot(own_steps[t : t + 1, :])
        terms = jnp.dot(decay[...].astype(BF16), hot, preferred_element_type=F32)
        left[o, 0:LANES] = jnp.transpose(jnp.concatenate([operand(f, True), terms], axis=0)).astype(BF16)
        left[o, LANES:] = jnp.transpose(hot.astype(F32)).astype(BF16)
    vec[...], small[...], factor = factors(b[...])
    scale[...] = jnp.concatenate([jnp.broadcast_to(factor, (PROBES, LANES)), jnp.zeros((ROWS - PROBES, LANES), F32)], axis=0)
    pack(packed, b[...], tiles)
    extra[...] = flag_ref[0] * noise[...]
    extra_b[...] = flag_ref[0] * noise[...] * b[...]


def decay_tables():
    rest = np.array([[-1.5 * math.log2((s + t + 8.0) / 8.0) for t in range(STEPS)] for s in range(STEPS)])

    def rounded(x):
        return x.astype(BF16).astype(np.float64)

    left, right = [], []
    for _ in range(RANK):
        s, t = divmod(int(np.argmax(np.abs(rest))), STEPS)
        a, b = rounded(rest[:, t] / rest[s, t]), rounded(rest[s, :])
        left.append(a)
        right.append(b)
        rest = rest - np.outer(a, b)
    return np.array(left).astype(np.float32), np.concatenate([np.array(right), rounded(rest)]).astype(np.float32)


def one_hot(step):
    row = lax.broadcasted_iota(jnp.int32, (STEPS, LANES), 0)
    return jnp.where(row == step, 1.0, 0.0).astype(BF16)


def hbm(x):
    return pltpu.with_memory_space_constraint(x, pltpu.HBM)


def own(run, step, table, b, noise, flag, decay, right_decay):
    n = b.shape[1]
    ids = VMEM(run.shape, jnp.int32)
    return pl.pallas_call(
        own_body,
        out_shape=(
            VMEM(right_decay.shape, F32),
            VMEM((GROUP, LANES), F32),
            VMEM((n, DEPTH), BF16),
            VMEM((2 * ROWS, n), BF16),
            VMEM((2 * ROWS, n), F8),
            VMEM((ROWS, LANES), F32),
            VMEM((PROBES, n), F32),
            VMEM((1, n), F32),
            jax.ShapeDtypeStruct((SIDE, ROWS, LANES), F32),
        ),
        in_specs=[sspec()] * 2 + [pl.BlockSpec(memory_space=pl.ANY)] * 7,
        out_specs=(vspec(),) * 9,
        scratch_shapes=[
            VMEM(table.shape, F32),
            ids,
            ids,
            VMEM(b.shape, F32),
            VMEM((1, n), F32),
            VMEM(decay.shape, F32),
            VMEM((n, LANES), F32),
            pltpu.SemaphoreType.DMA((6 + 4 * (table.shape[1] // GROUP),)),
        ],
        compiler_params=params(12),
        cost_estimate=pl.CostEstimate(flops=n * 6000, bytes_accessed=4 * table.size, transcendentals=0),
        name="own",
    )(run, flag, *(hbm(x) for x in (run, step, table, b, noise.reshape(1, n), decay, right_decay)))


def build_body(idx_ref, other, decay, table, left, vec, small, scale, extra_b,
               khi_ref, klo_ref, out_ref, rows, right, acc, acc8, *, pt, qt):
    n, m = khi_ref.shape
    tiles = m // LANES
    per = qt // LANES

    def ready(jq, slot):
        for k in range(per):
            t = jq * per + k
            o = slice(k * LANES, (k + 1) * LANES)
            fetch(lambda t, p: idx_ref[0, t, p], table, rows, t, k * LANES)
            f = turn(rows[o, :], other[0, pl.ds(t, 1), :])
            terms = jnp.dot(decay[...].astype(BF16), one_hot(other[1, pl.ds(t, 1), :]), preferred_element_type=F32)
            right[slot, :, o] = jnp.concatenate([operand(f, False), terms], axis=0).astype(BF16)

    def column(jq, _):
        oq = pl.ds(pl.multiple_of(jq * qt, qt), qt)
        right_tile = right[jq % 2]
        acc[...] = jnp.zeros_like(acc)
        acc8[...] = jnp.zeros_like(acc8)

        def row(ip, _):
            op = pl.ds(pl.multiple_of(ip * pt, pt), pt)
            power = jnp.dot(left[op, :], right_tile, preferred_element_type=F32)
            k = jnp.exp2(power)
            high = k.astype(BF16)
            low = (k - high.astype(F32)).astype(BF16).astype(F8)
            khi_ref[op, oq] = high
            klo_ref[op, oq] = low
            acc[...] += jnp.dot(vec[:, op], high, preferred_element_type=F32)
            acc8[...] += jnp.dot(small[:, op], low, preferred_element_type=F32)
            return 0

        lax.fori_loop(0, n // pt, row, 0, unroll=n // pt)
        res = (acc[0:ROWS, :] + acc[ROWS:, :]) * (1.0 / LIFT) + scale[:, 0:1] * (acc8[0:ROWS, :] + acc8[ROWS:, :])
        res = res[0:PROBES] + extra_b[:, oq]
        for t in range(qt // LANES):
            pack_tile(out_ref, res[:, t * LANES : (t + 1) * LANES], jq * (qt // LANES) + t, tiles)
        ready(jnp.minimum(jq + 1, m // qt - 1), (jq + 1) % 2)
        return 0

    clear_rest(out_ref, tiles)
    ready(0, 0)
    lax.fori_loop(0, m // qt, column, 0)


def build(other, decay, table, left, vec, small, scale, extra_b, pt=3072, qt=256):
    n = left.shape[0]
    m = other.shape[1] * LANES
    return pl.pallas_call(
        functools.partial(build_body, pt=pt, qt=qt),
        out_shape=(VMEM((n, m), BF16), VMEM((n, m), F8), jax.ShapeDtypeStruct((SIDE, ROWS, LANES), F32)),
        in_specs=[sspec()] + [vspec()] * 8,
        out_specs=(vspec(),) * 3,
        scratch_shapes=[
            VMEM((qt, LANES), F32),
            VMEM((2, DEPTH, qt), BF16),
            VMEM((2 * ROWS, qt), F32),
            VMEM((2 * ROWS, qt), F32),
        ],
        compiler_params=params(BUILD),
        cost_estimate=pl.CostEstimate(flops=n * m * 1000, bytes_accessed=n * m * 3, transcendentals=2 * n * m),
        name="build",
    )(other, other, decay, table, left, vec, small, scale, extra_b)


def apply_body(khi_ref, klo_ref, w_ref, extra, flag_ref, out_ref, nat, vec, small, *, pt):
    n, m = khi_ref.shape
    unpack(w_ref, nat, m // LANES)
    vec[...], small[...], scale = factors(nat[0:PROBES, :])
    clear_rest(out_ref, n // LANES)
    for s in range(SIDE):
        out_ref[s, ROWS:BOTH, :] = flag_ref[0] * w_ref[s]
    dims = (((1,), (1,)), ((), ()))

    def row(ip, _):
        op = pl.ds(pl.multiple_of(ip * pt, pt), pt)
        y = lax.dot_general(vec[...], khi_ref[op, :], dims, preferred_element_type=F32)
        z = lax.dot_general(small[...], klo_ref[op, :], dims, preferred_element_type=F32)
        res = (y[0:ROWS] + y[ROWS:])[0:PROBES] * (1.0 / LIFT) + scale * (z[0:ROWS] + z[ROWS:])[0:PROBES]
        res = res + extra[:, op] * nat[0:PROBES, op]
        for t in range(pt // LANES):
            pack_tile(out_ref, res[:, t * LANES : (t + 1) * LANES], ip * (pt // LANES) + t, n // LANES)
        return 0

    lax.fori_loop(0, n // pt, row, 0)


def apply(khi, klo, w, extra, flag, pt=512):
    n, m = khi.shape
    khi = pltpu.with_memory_space_constraint(khi, VMEM)
    klo = pltpu.with_memory_space_constraint(klo, VMEM)
    return pl.pallas_call(
        functools.partial(apply_body, pt=pt),
        out_shape=jax.ShapeDtypeStruct((SIDE, BOTH, LANES), F32),
        in_specs=[vspec()] * 4 + [sspec()],
        out_specs=vspec(),
        scratch_shapes=[VMEM((ROWS, m), F32), VMEM((2 * ROWS, m), BF16), VMEM((2 * ROWS, m), F8)],
        compiler_params=params(4),
        cost_estimate=pl.CostEstimate(flops=n * m * 600, bytes_accessed=n * m * 3, transcendentals=0),
        name="apply",
    )(khi, klo, w, extra, flag)


def first_sum_body(in_ref, out_ref):
    total = jnp.sum(in_ref[...], axis=0)
    for s in range(SIDE):
        out_ref[s] = total


def first_sum(got):
    return pl.pallas_call(
        first_sum_body,
        out_shape=jax.ShapeDtypeStruct((SIDE, ROWS, LANES), F32),
        in_specs=[vspec()],
        out_specs=vspec(),
        compiler_params=params(),
        name="first_sum",
    )(got)


def places(which):
    lane = lax.broadcasted_iota(jnp.int32, (ROWS, LANES), 1)
    row = lax.broadcasted_iota(jnp.int32, (ROWS, LANES), 0)
    return lane == jnp.where(which < 8 * 24 // ROWS, row & 7, 8)


def joined(blocks, first):
    def part(k):
        return blocks if k == 0 else pltpu.roll(blocks, LANES - ROWS * k, 1)

    def over(x):
        return jnp.sum(x, axis=0, keepdims=True)

    bb, bw, ww, near, rr, rw, rz, wz = (part(k) for k in range(8))
    all_bb, all_bw, all_ww = over(bb), over(bw), over(ww)
    middle = all_bb / all_bw if first else jnp.where(all_ww > 0.0, all_bw / all_ww, 0.0)
    shift = near - middle
    return (all_bb, all_bw, all_ww, middle, over(rr + shift * (2.0 * rw + shift * ww)), over(rw + shift * ww),
            over(rz + shift * wz), over(wz))


def put(lines):
    lane = lax.broadcasted_iota(jnp.int32, (1, LANES), 1)
    out = jnp.zeros((1, LANES), F32)
    for k, line in enumerate(lines):
        line = jnp.where(lane < PROBES, line, 0.0)
        out = out + (line if k == 0 else pltpu.roll(line, ROWS * k, 1))
    return out


def chunk_body(in_ref, b_ref, which_ref, chunk_ref, line_ref):
    total = jnp.sum(in_ref[...], axis=0)
    chunk_ref[...] = total
    which = which_ref[0]
    b, z, w = b_ref[which], total[0:ROWS], total[ROWS:BOTH]
    here = places(which)

    def dot(x, y):
        return jnp.sum(jnp.where(here, jnp.sum(x * y, axis=1, keepdims=True), 0.0), axis=0, keepdims=True)

    ww, bw = dot(w, w), dot(b, w)
    near = jnp.where(ww > 0.0, bw / ww, 0.0)
    r = b - jnp.sum(jnp.where(here, near, 0.0), axis=1, keepdims=True) * w
    line = put((dot(b, b), bw, ww, near, dot(r, r), dot(r, w), dot(r, z), dot(w, z)))
    for s in range(SIDE):
        line_ref[s] = jnp.broadcast_to(line, (LINES, LANES))


def chunk_sums(got, b, which):
    return pl.pallas_call(
        chunk_body,
        out_shape=(jax.ShapeDtypeStruct((BOTH, LANES), F32), jax.ShapeDtypeStruct((SIDE, LINES, LANES), F32)),
        in_specs=[vspec(), vspec(), sspec()],
        out_specs=(vspec(), vspec()),
        compiler_params=params(),
        name="chunk_sums",
    )(got, b, which)


def join_body(chunk_ref, line_ref, out_ref):
    line = put(joined(jnp.concatenate([line_ref[s, 0:1, :] for s in range(SIDE)], axis=0), False))
    for s in range(SIDE):
        out_ref[s, 0:BOTH, :] = chunk_ref[...]
        out_ref[s, BOTH:MORE, :] = jnp.broadcast_to(line, (MORE - BOTH, LANES))


def join(chunk, line):
    return pl.pallas_call(
        join_body,
        out_shape=jax.ShapeDtypeStruct((SIDE, MORE, LANES), F32),
        in_specs=[vspec(), vspec()],
        out_specs=vspec(),
        compiler_params=params(),
        name="join",
    )(chunk, line)


def finish_body(b_ref, a_ref, x_ref, r_ref, nw, na):
    tiles = b_ref.shape[1] // LANES
    unpack(a_ref, na, tiles)
    unpack(a_ref, nw, tiles, ROWS)
    lines = joined(jnp.concatenate([a_ref[s, BOTH : BOTH + 1, :] for s in range(SIDE)], axis=0), True)
    bb, bw, _, first, rr, rw, rz, _ = (to_column(line, 0) for line in lines)
    beta = rr / bb
    second = rr / ((rw - first * rz) + 2.0 * beta * rw + beta * beta * bw)
    b = b_ref[...]
    w = nw[0:PROBES, :]
    r = b - first * w
    x_ref[...] = first * b + second * (r + beta * b)
    r_ref[...] = r - second * ((w - first * na[0:PROBES, :]) + beta * w)


def finish(b, a):
    n = b.shape[1]
    out = jax.ShapeDtypeStruct((PROBES, n), F32)
    return pl.pallas_call(
        finish_body,
        out_shape=(out, out),
        in_specs=[vspec()] * 2,
        out_specs=(vspec(), vspec()),
        scratch_shapes=[VMEM((ROWS, n), F32), VMEM((ROWS, n), F32)],
        compiler_params=params(),
        name="finish",
    )(b, a)


def on_device(right_side, noise_level, run_index, step_index, run_features):
    swap = [(i * SIDE + j, j * SIDE + i) for i in range(SIDE) for j in range(SIDE)]

    def exchange(x, axis):
        return lax.all_to_all(x, axis, 0, 0)

    flag = (lax.axis_index("row") == lax.axis_index("col")).astype(F32).reshape(1)
    which = lax.axis_index("col").reshape(1)
    tiles = run_index.shape[0] // LANES
    run = run_index.reshape(tiles, LANES)
    step = step_index.reshape(tiles, LANES)
    other = lax.ppermute(jnp.stack([run, step]), ("row", "col"), swap)
    decays = (jnp.asarray(x) for x in decay_tables())
    *mine, extra, packed = own(run, step, run_features, right_side, noise_level, flag, *decays)
    khi, klo, part = build(other, *mine)
    product = exchange(first_sum(exchange(part, "row")), "row")
    both = exchange(apply(khi, klo, product, extra, flag), "col")
    chunk, line = chunk_sums(both, packed, which)
    again = exchange(join(chunk, exchange(line, "row")), "col")
    return finish(right_side, again)


def solution(mesh):
    return jax.shard_map(
        on_device,
        mesh=mesh,
        in_specs=(P(None, "row"), P("row"), P("row"), P("row"), P()),
        out_specs=(P(None, "row"), P(None, "row")),
        check_vma=False,
    )
```

```python
import functools
import math

import jax
import jax.numpy as jnp
import numpy as np
from jax import lax
from jax.experimental import pallas as pl
from jax.experimental.pallas import tpu as pltpu
from jax.sharding import PartitionSpec as P

LANES = 128
SIDE = 16
FEAT = 16
PROBES = 9
ROWS = 16
BUILD = 12
BOTH = 32
MORE = 40
LINES = 8
GROUP = 4096
DEPTH = 256
RANK = 24
STEPS = 128
LOG2E = 1.4426950408889634
F32 = jnp.float32
BF16 = jnp.bfloat16
F8 = jnp.float8_e4m3fn
TOP = 240.0
LIFT = 65536.0
VMEM = pltpu.VMEM
MIB = 1024 * 1024


def vspec():
    return pl.BlockSpec(memory_space=VMEM)


def sspec():
    return pl.BlockSpec(memory_space=pltpu.SMEM)


def params(mib=2):
    return pltpu.CompilerParams(vmem_limit_bytes=mib * MIB)


def thirds(x):
    a = x.astype(BF16).astype(F32)
    b = (x - a).astype(BF16).astype(F32)
    return a, b, x - a - b


def to_column(row, first):
    lane = lax.broadcasted_iota(jnp.int32, (PROBES, LANES), 1)
    sub = lax.broadcasted_iota(jnp.int32, (PROBES, LANES), 0)
    return jnp.sum(jnp.where(lane == sub + first, row, 0.0), axis=1, keepdims=True)


def unpack(v_ref, nat, tiles, first=0):
    for t in range(tiles):
        lanes = slice(t * LANES, (t + 1) * LANES)
        row = first + 8 * (t % 2)
        nat[0:8, lanes] = v_ref[t // 2, row : row + 8, :]
        m = 8 * tiles + t
        row = first + m % ROWS
        nat[8:9, lanes] = v_ref[m // ROWS, row : row + 1, :]


def pack_tile(out_ref, res, tile, tiles):
    out_ref[tile // 2, pl.ds(pl.multiple_of(8 * (tile % 2), 8), 8), :] = res[0:8]
    m = 8 * tiles + tile
    out_ref[m // ROWS, pl.ds(m % ROWS, 1), :] = res[8:9]


def clear_rest(out_ref, tiles):
    m = 9 * tiles
    out_ref[m // ROWS, m % ROWS : ROWS, :] = jnp.zeros((ROWS - m % ROWS, LANES), F32)
    for s in range(m // ROWS + 1, SIDE):
        out_ref[s, 0:ROWS, :] = jnp.zeros((ROWS, LANES), F32)


def factors(v):
    zero = jnp.zeros((ROWS - PROBES, v.shape[1]), F32)
    high = v.astype(BF16).astype(F32)
    halves = jnp.concatenate([high, zero, v - high, zero], axis=0).astype(BF16)
    top = jnp.max(jnp.abs(v), axis=1, keepdims=True)
    top = jnp.where(top > 0.0, top, 1.0)
    u = v * (TOP / top)
    coarse = u.astype(F8).astype(F32)
    small = jnp.concatenate([coarse, zero, (u - coarse), zero], axis=0).astype(F8)
    return halves, small, top * (1.0 / (TOP * LIFT))


def fetch(read, table, rows, t, at):
    for p in range(LANES):
        rows[pl.ds(at + p, 1), :] = table[pl.ds(read(t, p) & (GROUP - 1), 1), :]


def turn(rows, run):
    turned = jnp.transpose(rows)
    group = run >> 12
    f = turned[0:FEAT]
    for g in range(1, LANES // FEAT):
        f = jnp.where(group == g, turned[g * FEAT : (g + 1) * FEAT], f)
    return f


def pack(out_ref, v, tiles):
    clear_rest(out_ref, tiles)
    for t in range(tiles):
        pack_tile(out_ref, v[:, t * LANES : (t + 1) * LANES], t, tiles)


def operand(f, is_left):
    f = f * math.sqrt(LOG2E)
    a, b, c = thirds(f)
    norm = -0.5 * jnp.sum(f * f, axis=0, keepdims=True)
    if is_left:
        norm = norm + math.log2(LIFT)
    na, nb, nc = thirds(norm)
    one = jnp.ones_like(norm)
    if is_left:
        parts = [a, a, b, b, a, c, na, nb, nc, one, one, one]
    else:
        parts = [a, b, a, b, c, a, one, one, one, na, nb, nc]
    return jnp.concatenate(parts + [jnp.zeros((2, f.shape[1]), F32)], axis=0)


def own_body(idx_ref, flag_ref, run_ref, step_ref, tab_ref, b_ref, noise_ref, decay_ref, right_ref,
             ids, right_decay, table, left, vec, small, scale, extra_b, extra, packed,
             tab, b, noise, decay, terms, rows, sems):
    groups = tab_ref.shape[1] // GROUP
    width = GROUP // 4
    tiles = run_ref.shape[0]
    pairs = [(step_ref, ids.at[1]), (decay_ref, decay), (b_ref, b), (noise_ref, noise), (run_ref, ids.at[0])]
    pairs.append((right_ref, right_decay))
    loads = [pltpu.make_async_copy(src, dst, sems.at[k]) for k, (src, dst) in enumerate(pairs)]
    parts = []
    for c in range(4):
        for g in range(groups):
            at = pl.ds(g * GROUP + c * width, width)
            parts.append(pltpu.make_async_copy(tab_ref.at[:, at], tab.at[:, at], sems.at[6 + c * groups + g]))
    for part in loads + parts:
        part.start()
    loads[0].wait()
    loads[1].wait()
    table_left = decay[...].astype(BF16)
    for t in range(tiles):
        o = slice(t * LANES, (t + 1) * LANES)
        hot = one_hot(ids[1, t : t + 1, :])
        terms[:, o] = jnp.dot(table_left, hot, preferred_element_type=F32)
        left[o, LANES:] = jnp.transpose(hot.astype(F32)).astype(BF16)
    loads[2].wait()
    loads[3].wait()
    vec[...], small[...], factor = factors(b[...])
    scale[...] = jnp.concatenate([jnp.broadcast_to(factor, (PROBES, LANES)), jnp.zeros((ROWS - PROBES, LANES), F32)], axis=0)
    pack(packed, b[...], tiles)
    extra[...] = flag_ref[0] * noise[...]
    extra_b[...] = flag_ref[0] * noise[...] * b[...]
    blank = jnp.zeros((LANES - groups * FEAT, LANES), F32)
    for c in range(4):
        for part in parts[c * groups : (c + 1) * groups]:
            part.wait()
        for t in range(c * (width // LANES), (c + 1) * (width // LANES)):
            pieces = [tab[:, g * GROUP + t * LANES : g * GROUP + (t + 1) * LANES] for g in range(groups)]
            table[t * LANES : (t + 1) * LANES, :] = jnp.transpose(jnp.concatenate(pieces + [blank], axis=0))
    loads[4].wait()
    loads[5].wait()

    def get(t, _):
        fetch(lambda t, p: idx_ref[t, p], table, rows, t, pl.multiple_of(t * LANES, LANES))
        return 0

    lax.fori_loop(0, tiles, get, 0)
    for t in range(tiles):
        o = slice(t * LANES, (t + 1) * LANES)
        f = turn(rows[o, :], ids[0, t : t + 1, :])
        left[o, 0:LANES] = jnp.transpose(jnp.concatenate([operand(f, True), terms[:, o]], axis=0)).astype(BF16)


def decay_tables():
    rest = np.array([[-1.5 * math.log2((s + t + 8.0) / 8.0) for t in range(STEPS)] for s in range(STEPS)])

    def rounded(x):
        return x.astype(BF16).astype(np.float64)

    left, right = [], []
    for _ in range(RANK):
        s, t = divmod(int(np.argmax(np.abs(rest))), STEPS)
        a, b = rounded(rest[:, t] / rest[s, t]), rounded(rest[s, :])
        left.append(a)
        right.append(b)
        rest = rest - np.outer(a, b)
    return np.array(left).astype(np.float32), np.concatenate([np.array(right), rounded(rest)]).astype(np.float32)


def one_hot(step):
    row = lax.broadcasted_iota(jnp.int32, (STEPS, LANES), 0)
    return jnp.where(row == step, 1.0, 0.0).astype(BF16)


def hbm(x):
    return pltpu.with_memory_space_constraint(x, pltpu.HBM)


def own(run, step, table, b, noise, flag, decay, right_decay):
    n = b.shape[1]
    return pl.pallas_call(
        own_body,
        out_shape=(
            VMEM((2, *run.shape), jnp.int32),
            VMEM(right_decay.shape, F32),
            VMEM((GROUP, LANES), F32),
            VMEM((n, DEPTH), BF16),
            VMEM((2 * ROWS, n), BF16),
            VMEM((2 * ROWS, n), F8),
            VMEM((ROWS, LANES), F32),
            VMEM((PROBES, n), F32),
            VMEM((1, n), F32),
            jax.ShapeDtypeStruct((SIDE, ROWS, LANES), F32),
        ),
        in_specs=[sspec()] * 2 + [pl.BlockSpec(memory_space=pl.ANY)] * 7,
        out_specs=(vspec(),) * 10,
        scratch_shapes=[
            VMEM(table.shape, F32),
            VMEM(b.shape, F32),
            VMEM((1, n), F32),
            VMEM(decay.shape, F32),
            VMEM((RANK, n), F32),
            VMEM((n, LANES), F32),
            pltpu.SemaphoreType.DMA((6 + 4 * (table.shape[1] // GROUP),)),
        ],
        compiler_params=params(12),
        cost_estimate=pl.CostEstimate(flops=n * 6000, bytes_accessed=4 * table.size, transcendentals=0),
        name="own",
    )(run, flag, *(hbm(x) for x in (run, step, table, b, noise.reshape(1, n), decay, right_decay)))


def build_body(idx_ref, other, decay, table, left, vec, small, scale, extra_b,
               khi_ref, klo_ref, out_ref, rows, right, acc, acc8, *, pt, qt):
    n, m = khi_ref.shape
    tiles = m // LANES
    per = qt // LANES

    def ready(jq, slot):
        for k in range(per):
            t = jq * per + k
            o = slice(k * LANES, (k + 1) * LANES)
            fetch(lambda t, p: idx_ref[0, t, p], table, rows, t, k * LANES)
            f = turn(rows[o, :], other[0, pl.ds(t, 1), :])
            terms = jnp.dot(decay[...].astype(BF16), one_hot(other[1, pl.ds(t, 1), :]), preferred_element_type=F32)
            right[slot, :, o] = jnp.concatenate([operand(f, False), terms], axis=0).astype(BF16)

    def column(jq, _):
        oq = pl.ds(pl.multiple_of(jq * qt, qt), qt)
        right_tile = right[jq % 2]
        acc[...] = jnp.zeros_like(acc)
        acc8[...] = jnp.zeros_like(acc8)

        def row(ip, _):
            op = pl.ds(pl.multiple_of(ip * pt, pt), pt)
            power = jnp.dot(left[op, :], right_tile, preferred_element_type=F32)
            k = jnp.exp2(power)
            high = k.astype(BF16)
            low = (k - high.astype(F32)).astype(BF16).astype(F8)
            khi_ref[op, oq] = high
            klo_ref[op, oq] = low
            acc[...] += jnp.dot(vec[:, op], high, preferred_element_type=F32)
            acc8[...] += jnp.dot(small[:, op], low, preferred_element_type=F32)
            return 0

        lax.fori_loop(0, n // pt, row, 0, unroll=n // pt)
        res = (acc[0:ROWS, :] + acc[ROWS:, :]) * (1.0 / LIFT) + scale[:, 0:1] * (acc8[0:ROWS, :] + acc8[ROWS:, :])
        res = res[0:PROBES] + extra_b[:, oq]
        for t in range(qt // LANES):
            pack_tile(out_ref, res[:, t * LANES : (t + 1) * LANES], jq * (qt // LANES) + t, tiles)
        ready(jnp.minimum(jq + 1, m // qt - 1), (jq + 1) % 2)
        return 0

    clear_rest(out_ref, tiles)
    ready(0, 0)
    lax.fori_loop(0, m // qt, column, 0)


def build(other, decay, table, left, vec, small, scale, extra_b, pt=3072, qt=512):
    n = left.shape[0]
    m = other.shape[1] * LANES
    return pl.pallas_call(
        functools.partial(build_body, pt=pt, qt=qt),
        out_shape=(VMEM((n, m), BF16), VMEM((n, m), F8), jax.ShapeDtypeStruct((SIDE, ROWS, LANES), F32)),
        in_specs=[sspec()] + [vspec()] * 8,
        out_specs=(vspec(),) * 3,
        scratch_shapes=[
            VMEM((qt, LANES), F32),
            VMEM((2, DEPTH, qt), BF16),
            VMEM((2 * ROWS, qt), F32),
            VMEM((2 * ROWS, qt), F32),
        ],
        compiler_params=params(BUILD),
        cost_estimate=pl.CostEstimate(flops=n * m * 1000, bytes_accessed=n * m * 3, transcendentals=2 * n * m),
        name="build",
    )(other, other, decay, table, left, vec, small, scale, extra_b)


def apply_body(khi_ref, klo_ref, w_ref, extra, flag_ref, out_ref, nat, vec, small, *, pt):
    n, m = khi_ref.shape
    unpack(w_ref, nat, m // LANES)
    vec[...], small[...], scale = factors(nat[0:PROBES, :])
    clear_rest(out_ref, n // LANES)
    for s in range(SIDE):
        out_ref[s, ROWS:BOTH, :] = flag_ref[0] * w_ref[s]
    dims = (((1,), (1,)), ((), ()))

    def row(ip, _):
        op = pl.ds(pl.multiple_of(ip * pt, pt), pt)
        y = lax.dot_general(vec[...], khi_ref[op, :], dims, preferred_element_type=F32)
        z = lax.dot_general(small[...], klo_ref[op, :], dims, preferred_element_type=F32)
        res = (y[0:ROWS] + y[ROWS:])[0:PROBES] * (1.0 / LIFT) + scale * (z[0:ROWS] + z[ROWS:])[0:PROBES]
        res = res + extra[:, op] * nat[0:PROBES, op]
        for t in range(pt // LANES):
            pack_tile(out_ref, res[:, t * LANES : (t + 1) * LANES], ip * (pt // LANES) + t, n // LANES)
        return 0

    lax.fori_loop(0, n // pt, row, 0)


def apply(khi, klo, w, extra, flag, pt=512):
    n, m = khi.shape
    khi = pltpu.with_memory_space_constraint(khi, VMEM)
    klo = pltpu.with_memory_space_constraint(klo, VMEM)
    return pl.pallas_call(
        functools.partial(apply_body, pt=pt),
        out_shape=jax.ShapeDtypeStruct((SIDE, BOTH, LANES), F32),
        in_specs=[vspec()] * 4 + [sspec()],
        out_specs=vspec(),
        scratch_shapes=[VMEM((ROWS, m), F32), VMEM((2 * ROWS, m), BF16), VMEM((2 * ROWS, m), F8)],
        compiler_params=params(4),
        cost_estimate=pl.CostEstimate(flops=n * m * 600, bytes_accessed=n * m * 3, transcendentals=0),
        name="apply",
    )(khi, klo, w, extra, flag)


def first_sum_body(in_ref, out_ref):
    total = jnp.sum(in_ref[...], axis=0)
    for s in range(SIDE):
        out_ref[s] = total


def first_sum(got):
    return pl.pallas_call(
        first_sum_body,
        out_shape=jax.ShapeDtypeStruct((SIDE, ROWS, LANES), F32),
        in_specs=[vspec()],
        out_specs=vspec(),
        compiler_params=params(),
        name="first_sum",
    )(got)


def places(which):
    lane = lax.broadcasted_iota(jnp.int32, (ROWS, LANES), 1)
    row = lax.broadcasted_iota(jnp.int32, (ROWS, LANES), 0)
    return lane == jnp.where(which < 8 * 24 // ROWS, row & 7, 8)


def joined(blocks, first):
    def part(k):
        return blocks if k == 0 else pltpu.roll(blocks, LANES - ROWS * k, 1)

    def over(x):
        return jnp.sum(x, axis=0, keepdims=True)

    bb, bw, ww, near, rr, rw, rz, wz = (part(k) for k in range(8))
    all_bb, all_bw, all_ww = over(bb), over(bw), over(ww)
    middle = all_bb / all_bw if first else jnp.where(all_ww > 0.0, all_bw / all_ww, 0.0)
    shift = near - middle
    return (all_bb, all_bw, all_ww, middle, over(rr + shift * (2.0 * rw + shift * ww)), over(rw + shift * ww),
            over(rz + shift * wz), over(wz))


def put(lines):
    lane = lax.broadcasted_iota(jnp.int32, (1, LANES), 1)
    out = jnp.zeros((1, LANES), F32)
    for k, line in enumerate(lines):
        line = jnp.where(lane < PROBES, line, 0.0)
        out = out + (line if k == 0 else pltpu.roll(line, ROWS * k, 1))
    return out


def chunk_body(in_ref, b_ref, which_ref, chunk_ref, line_ref):
    total = jnp.sum(in_ref[...], axis=0)
    chunk_ref[...] = total
    which = which_ref[0]
    b, z, w = b_ref[which], total[0:ROWS], total[ROWS:BOTH]
    here = places(which)

    def dot(x, y):
        return jnp.sum(jnp.where(here, jnp.sum(x * y, axis=1, keepdims=True), 0.0), axis=0, keepdims=True)

    ww, bw = dot(w, w), dot(b, w)
    near = jnp.where(ww > 0.0, bw / ww, 0.0)
    r = b - jnp.sum(jnp.where(here, near, 0.0), axis=1, keepdims=True) * w
    line = put((dot(b, b), bw, ww, near, dot(r, r), dot(r, w), dot(r, z), dot(w, z)))
    for s in range(SIDE):
        line_ref[s] = jnp.broadcast_to(line, (LINES, LANES))


def chunk_sums(got, b, which):
    return pl.pallas_call(
        chunk_body,
        out_shape=(jax.ShapeDtypeStruct((BOTH, LANES), F32), jax.ShapeDtypeStruct((SIDE, LINES, LANES), F32)),
        in_specs=[vspec(), vspec(), sspec()],
        out_specs=(vspec(), vspec()),
        compiler_params=params(),
        name="chunk_sums",
    )(got, b, which)


def join_body(chunk_ref, line_ref, out_ref):
    line = put(joined(jnp.concatenate([line_ref[s, 0:1, :] for s in range(SIDE)], axis=0), False))
    for s in range(SIDE):
        out_ref[s, 0:BOTH, :] = chunk_ref[...]
        out_ref[s, BOTH:MORE, :] = jnp.broadcast_to(line, (MORE - BOTH, LANES))


def join(chunk, line):
    return pl.pallas_call(
        join_body,
        out_shape=jax.ShapeDtypeStruct((SIDE, MORE, LANES), F32),
        in_specs=[vspec(), vspec()],
        out_specs=vspec(),
        compiler_params=params(),
        name="join",
    )(chunk, line)


def finish_body(b_ref, a_ref, x_ref, r_ref, nw, na):
    tiles = b_ref.shape[1] // LANES
    unpack(a_ref, na, tiles)
    unpack(a_ref, nw, tiles, ROWS)
    lines = joined(jnp.concatenate([a_ref[s, BOTH : BOTH + 1, :] for s in range(SIDE)], axis=0), True)
    bb, bw, _, first, rr, rw, rz, _ = (to_column(line, 0) for line in lines)
    beta = rr / bb
    second = rr / ((rw - first * rz) + 2.0 * beta * rw + beta * beta * bw)
    b = b_ref[...]
    w = nw[0:PROBES, :]
    r = b - first * w
    x_ref[...] = first * b + second * (r + beta * b)
    r_ref[...] = r - second * ((w - first * na[0:PROBES, :]) + beta * w)


def finish(b, a):
    n = b.shape[1]
    out = jax.ShapeDtypeStruct((PROBES, n), F32)
    return pl.pallas_call(
        finish_body,
        out_shape=(out, out),
        in_specs=[vspec()] * 2,
        out_specs=(vspec(), vspec()),
        scratch_shapes=[VMEM((ROWS, n), F32), VMEM((ROWS, n), F32)],
        compiler_params=params(),
        name="finish",
    )(b, a)


def on_device(right_side, noise_level, run_index, step_index, run_features):
    swap = [(i * SIDE + j, j * SIDE + i) for i in range(SIDE) for j in range(SIDE)]

    def exchange(x, axis):
        return lax.all_to_all(x, axis, 0, 0)

    flag = (lax.axis_index("row") == lax.axis_index("col")).astype(F32).reshape(1)
    which = lax.axis_index("col").reshape(1)
    tiles = run_index.shape[0] // LANES
    run = run_index.reshape(tiles, LANES)
    step = step_index.reshape(tiles, LANES)
    decays = (jnp.asarray(x) for x in decay_tables())
    ids, *mine, extra, packed = own(run, step, run_features, right_side, noise_level, flag, *decays)
    khi, klo, part = build(lax.ppermute(ids, ("row", "col"), swap), *mine)
    product = exchange(first_sum(exchange(part, "row")), "row")
    both = exchange(apply(khi, klo, product, extra, flag), "col")
    chunk, line = chunk_sums(both, packed, which)
    again = exchange(join(chunk, exchange(line, "row")), "col")
    return finish(right_side, again)


def solution(mesh):
    return jax.shard_map(
        on_device,
        mesh=mesh,
        in_specs=(P(None, "row"), P("row"), P("row"), P("row"), P()),
        out_specs=(P(None, "row"), P(None, "row")),
        check_vma=False,
    )
```

```python
import functools
import math

import jax
import jax.numpy as jnp
import numpy as np
from jax import lax
from jax.experimental import pallas as pl
from jax.experimental.pallas import tpu as pltpu
from jax.sharding import PartitionSpec as P

LANES = 128
SIDE = 16
FEAT = 16
PROBES = 9
ROWS = 16
BUILD = 12
BOTH = 32
MORE = 40
LINES = 8
GROUP = 4096
DEPTH = 256
RANK = 24
STEPS = 128
LOG2E = 1.4426950408889634
F32 = jnp.float32
BF16 = jnp.bfloat16
F8 = jnp.float8_e4m3fn
TOP = 240.0
LIFT = 65536.0
VMEM = pltpu.VMEM
MIB = 1024 * 1024


def vspec():
    return pl.BlockSpec(memory_space=VMEM)


def sspec():
    return pl.BlockSpec(memory_space=pltpu.SMEM)


def params(mib=2):
    return pltpu.CompilerParams(vmem_limit_bytes=mib * MIB)


def thirds(x):
    a = x.astype(BF16).astype(F32)
    b = (x - a).astype(BF16).astype(F32)
    return a, b, x - a - b


def to_column(row, first):
    lane = lax.broadcasted_iota(jnp.int32, (PROBES, LANES), 1)
    sub = lax.broadcasted_iota(jnp.int32, (PROBES, LANES), 0)
    return jnp.sum(jnp.where(lane == sub + first, row, 0.0), axis=1, keepdims=True)


def unpack(v_ref, nat, tiles, first=0):
    for t in range(tiles):
        lanes = slice(t * LANES, (t + 1) * LANES)
        row = first + 8 * (t % 2)
        nat[0:8, lanes] = v_ref[t // 2, row : row + 8, :]
        m = 8 * tiles + t
        row = first + m % ROWS
        nat[8:9, lanes] = v_ref[m // ROWS, row : row + 1, :]


def pack_tile(out_ref, res, tile, tiles):
    out_ref[tile // 2, pl.ds(pl.multiple_of(8 * (tile % 2), 8), 8), :] = res[0:8]
    m = 8 * tiles + tile
    out_ref[m // ROWS, pl.ds(m % ROWS, 1), :] = res[8:9]


def clear_rest(out_ref, tiles):
    m = 9 * tiles
    out_ref[m // ROWS, m % ROWS : ROWS, :] = jnp.zeros((ROWS - m % ROWS, LANES), F32)
    for s in range(m // ROWS + 1, SIDE):
        out_ref[s, 0:ROWS, :] = jnp.zeros((ROWS, LANES), F32)


def factors(v):
    zero = jnp.zeros((ROWS - PROBES, v.shape[1]), F32)
    high = v.astype(BF16).astype(F32)
    halves = jnp.concatenate([high, zero, v - high, zero], axis=0).astype(BF16)
    top = jnp.max(jnp.abs(v), axis=1, keepdims=True)
    top = jnp.where(top > 0.0, top, 1.0)
    u = v * (TOP / top)
    coarse = u.astype(F8).astype(F32)
    small = jnp.concatenate([coarse, zero, (u - coarse), zero], axis=0).astype(F8)
    return halves, small, top * (1.0 / (TOP * LIFT))


def fetch(read, table, rows, t, at):
    for p in range(LANES):
        rows[pl.ds(at + p, 1), :] = table[pl.ds(read(t, p) & (GROUP - 1), 1), :]


def turn(rows, run):
    turned = jnp.transpose(rows)
    group = run >> 12
    f = turned[0:FEAT]
    for g in range(1, LANES // FEAT):
        f = jnp.where(group == g, turned[g * FEAT : (g + 1) * FEAT], f)
    return f


def pack(out_ref, v, tiles):
    clear_rest(out_ref, tiles)
    for t in range(tiles):
        pack_tile(out_ref, v[:, t * LANES : (t + 1) * LANES], t, tiles)


def operand(f, is_left):
    f = f * math.sqrt(LOG2E)
    a, b, c = thirds(f)
    norm = -0.5 * jnp.sum(f * f, axis=0, keepdims=True)
    if is_left:
        norm = norm + math.log2(LIFT)
    na, nb, nc = thirds(norm)
    one = jnp.ones_like(norm)
    if is_left:
        parts = [a, a, b, b, a, c, na, nb, nc, one, one, one]
    else:
        parts = [a, b, a, b, c, a, one, one, one, na, nb, nc]
    return jnp.concatenate(parts + [jnp.zeros((2, f.shape[1]), F32)], axis=0)


def own_body(idx_ref, flag_ref, run_ref, step_ref, tab_ref, b_ref, noise_ref, decay_ref, right_ref,
             right_decay, table, left, vec, small, scale, extra_b, extra, packed,
             ids, tab, b, noise, decay, terms, rows, sems):
    groups = tab_ref.shape[1] // GROUP
    width = GROUP // 4
    tiles = run_ref.shape[0]
    pairs = [(step_ref, ids.at[1]), (decay_ref, decay), (b_ref, b), (noise_ref, noise), (run_ref, ids.at[0])]
    pairs.append((right_ref, right_decay))
    loads = [pltpu.make_async_copy(src, dst, sems.at[k]) for k, (src, dst) in enumerate(pairs)]
    parts = []
    for c in range(4):
        for g in range(groups):
            at = pl.ds(g * GROUP + c * width, width)
            parts.append(pltpu.make_async_copy(tab_ref.at[:, at], tab.at[:, at], sems.at[6 + c * groups + g]))
    for part in loads + parts:
        part.start()
    loads[0].wait()
    loads[1].wait()
    table_left = decay[...].astype(BF16)
    for t in range(tiles):
        o = slice(t * LANES, (t + 1) * LANES)
        hot = one_hot(ids[1, t : t + 1, :])
        terms[:, o] = jnp.dot(table_left, hot, preferred_element_type=F32)
        left[o, LANES:] = jnp.transpose(hot.astype(F32)).astype(BF16)
    loads[2].wait()
    loads[3].wait()
    vec[...], small[...], factor = factors(b[...])
    scale[...] = jnp.concatenate([jnp.broadcast_to(factor, (PROBES, LANES)), jnp.zeros((ROWS - PROBES, LANES), F32)], axis=0)
    pack(packed, b[...], tiles)
    extra[...] = flag_ref[0] * noise[...]
    extra_b[...] = flag_ref[0] * noise[...] * b[...]
    blank = jnp.zeros((LANES - groups * FEAT, LANES), F32)
    for c in range(4):
        for part in parts[c * groups : (c + 1) * groups]:
            part.wait()
        for t in range(c * (width // LANES), (c + 1) * (width // LANES)):
            pieces = [tab[:, g * GROUP + t * LANES : g * GROUP + (t + 1) * LANES] for g in range(groups)]
            table[t * LANES : (t + 1) * LANES, :] = jnp.transpose(jnp.concatenate(pieces + [blank], axis=0))
    loads[4].wait()
    loads[5].wait()

    def get(t, _):
        fetch(lambda t, p: idx_ref[t, p], table, rows, t, pl.multiple_of(t * LANES, LANES))
        return 0

    lax.fori_loop(0, tiles, get, 0)
    for t in range(tiles):
        o = slice(t * LANES, (t + 1) * LANES)
        f = turn(rows[o, :], ids[0, t : t + 1, :])
        left[o, 0:LANES] = jnp.transpose(jnp.concatenate([operand(f, True), terms[:, o]], axis=0)).astype(BF16)


def decay_tables():
    rest = np.array([[-1.5 * math.log2((s + t + 8.0) / 8.0) for t in range(STEPS)] for s in range(STEPS)])

    def rounded(x):
        return x.astype(BF16).astype(np.float64)

    left, right = [], []
    for _ in range(RANK):
        s, t = divmod(int(np.argmax(np.abs(rest))), STEPS)
        a, b = rounded(rest[:, t] / rest[s, t]), rounded(rest[s, :])
        left.append(a)
        right.append(b)
        rest = rest - np.outer(a, b)
    return np.array(left).astype(np.float32), np.concatenate([np.array(right), rounded(rest)]).astype(np.float32)


def one_hot(step):
    row = lax.broadcasted_iota(jnp.int32, (STEPS, LANES), 0)
    return jnp.where(row == step, 1.0, 0.0).astype(BF16)


def hbm(x):
    return pltpu.with_memory_space_constraint(x, pltpu.HBM)


def own(run, step, table, b, noise, flag, decay, right_decay):
    n = b.shape[1]
    return pl.pallas_call(
        own_body,
        out_shape=(
            VMEM(right_decay.shape, F32),
            VMEM((GROUP, LANES), F32),
            VMEM((n, DEPTH), BF16),
            VMEM((2 * ROWS, n), BF16),
            VMEM((2 * ROWS, n), F8),
            VMEM((ROWS, LANES), F32),
            VMEM((PROBES, n), F32),
            VMEM((1, n), F32),
            jax.ShapeDtypeStruct((SIDE, ROWS, LANES), F32),
        ),
        in_specs=[sspec()] * 2 + [pl.BlockSpec(memory_space=pl.ANY)] * 7,
        out_specs=(vspec(),) * 9,
        scratch_shapes=[
            VMEM((2, *run.shape), jnp.int32),
            VMEM(table.shape, F32),
            VMEM(b.shape, F32),
            VMEM((1, n), F32),
            VMEM(decay.shape, F32),
            VMEM((RANK, n), F32),
            VMEM((n, LANES), F32),
            pltpu.SemaphoreType.DMA((6 + 4 * (table.shape[1] // GROUP),)),
        ],
        compiler_params=params(12),
        cost_estimate=pl.CostEstimate(flops=n * 6000, bytes_accessed=4 * table.size, transcendentals=0),
        name="own",
    )(run, flag, *(hbm(x) for x in (run, step, table, b, noise.reshape(1, n), decay, right_decay)))


def build_body(idx_ref, other, decay, table, left, vec, small, scale, extra_b,
               khi_ref, klo_ref, out_ref, rows, right, acc, acc8, *, pt, qt):
    n, m = khi_ref.shape
    tiles = m // LANES
    per = qt // LANES

    def ready(jq, slot):
        for k in range(per):
            t = jq * per + k
            o = slice(k * LANES, (k + 1) * LANES)
            fetch(lambda t, p: idx_ref[0, t, p], table, rows, t, k * LANES)
            f = turn(rows[o, :], other[0, pl.ds(t, 1), :])
            terms = jnp.dot(decay[...].astype(BF16), one_hot(other[1, pl.ds(t, 1), :]), preferred_element_type=F32)
            right[slot, :, o] = jnp.concatenate([operand(f, False), terms], axis=0).astype(BF16)

    def column(jq, _):
        oq = pl.ds(pl.multiple_of(jq * qt, qt), qt)
        right_tile = right[jq % 2]
        acc[...] = jnp.zeros_like(acc)
        acc8[...] = jnp.zeros_like(acc8)

        def row(ip, _):
            op = pl.ds(pl.multiple_of(ip * pt, pt), pt)
            power = jnp.dot(left[op, :], right_tile, preferred_element_type=F32)
            k = jnp.exp2(power)
            high = k.astype(BF16)
            low = (k - high.astype(F32)).astype(BF16).astype(F8)
            khi_ref[op, oq] = high
            klo_ref[op, oq] = low
            acc[...] += jnp.dot(vec[:, op], high, preferred_element_type=F32)
            acc8[...] += jnp.dot(small[:, op], low, preferred_element_type=F32)
            return 0

        lax.fori_loop(0, n // pt, row, 0, unroll=n // pt)
        res = (acc[0:ROWS, :] + acc[ROWS:, :]) * (1.0 / LIFT) + scale[:, 0:1] * (acc8[0:ROWS, :] + acc8[ROWS:, :])
        res = res[0:PROBES] + extra_b[:, oq]
        for t in range(qt // LANES):
            pack_tile(out_ref, res[:, t * LANES : (t + 1) * LANES], jq * (qt // LANES) + t, tiles)
        ready(jnp.minimum(jq + 1, m // qt - 1), (jq + 1) % 2)
        return 0

    clear_rest(out_ref, tiles)
    ready(0, 0)
    lax.fori_loop(0, m // qt, column, 0)


def build(other, decay, table, left, vec, small, scale, extra_b, pt=3072, qt=512):
    n = left.shape[0]
    m = other.shape[1] * LANES
    return pl.pallas_call(
        functools.partial(build_body, pt=pt, qt=qt),
        out_shape=(VMEM((n, m), BF16), VMEM((n, m), F8), jax.ShapeDtypeStruct((SIDE, ROWS, LANES), F32)),
        in_specs=[sspec()] + [vspec()] * 8,
        out_specs=(vspec(),) * 3,
        scratch_shapes=[
            VMEM((qt, LANES), F32),
            VMEM((2, DEPTH, qt), BF16),
            VMEM((2 * ROWS, qt), F32),
            VMEM((2 * ROWS, qt), F32),
        ],
        compiler_params=params(BUILD),
        cost_estimate=pl.CostEstimate(flops=n * m * 1000, bytes_accessed=n * m * 3, transcendentals=2 * n * m),
        name="build",
    )(other, other, decay, table, left, vec, small, scale, extra_b)


def apply_body(khi_ref, klo_ref, w_ref, extra, flag_ref, out_ref, nat, vec, small, *, pt):
    n, m = khi_ref.shape
    unpack(w_ref, nat, m // LANES)
    vec[...], small[...], scale = factors(nat[0:PROBES, :])
    clear_rest(out_ref, n // LANES)
    for s in range(SIDE):
        out_ref[s, ROWS:BOTH, :] = flag_ref[0] * w_ref[s]
    dims = (((1,), (1,)), ((), ()))

    def row(ip, _):
        op = pl.ds(pl.multiple_of(ip * pt, pt), pt)
        y = lax.dot_general(vec[...], khi_ref[op, :], dims, preferred_element_type=F32)
        z = lax.dot_general(small[...], klo_ref[op, :], dims, preferred_element_type=F32)
        res = (y[0:ROWS] + y[ROWS:])[0:PROBES] * (1.0 / LIFT) + scale * (z[0:ROWS] + z[ROWS:])[0:PROBES]
        res = res + extra[:, op] * nat[0:PROBES, op]
        for t in range(pt // LANES):
            pack_tile(out_ref, res[:, t * LANES : (t + 1) * LANES], ip * (pt // LANES) + t, n // LANES)
        return 0

    lax.fori_loop(0, n // pt, row, 0)


def apply(khi, klo, w, extra, flag, pt=512):
    n, m = khi.shape
    khi = pltpu.with_memory_space_constraint(khi, VMEM)
    klo = pltpu.with_memory_space_constraint(klo, VMEM)
    return pl.pallas_call(
        functools.partial(apply_body, pt=pt),
        out_shape=jax.ShapeDtypeStruct((SIDE, BOTH, LANES), F32),
        in_specs=[vspec()] * 4 + [sspec()],
        out_specs=vspec(),
        scratch_shapes=[VMEM((ROWS, m), F32), VMEM((2 * ROWS, m), BF16), VMEM((2 * ROWS, m), F8)],
        compiler_params=params(4),
        cost_estimate=pl.CostEstimate(flops=n * m * 600, bytes_accessed=n * m * 3, transcendentals=0),
        name="apply",
    )(khi, klo, w, extra, flag)


def first_sum_body(in_ref, out_ref):
    total = jnp.sum(in_ref[...], axis=0)
    for s in range(SIDE):
        out_ref[s] = total


def first_sum(got):
    return pl.pallas_call(
        first_sum_body,
        out_shape=jax.ShapeDtypeStruct((SIDE, ROWS, LANES), F32),
        in_specs=[vspec()],
        out_specs=vspec(),
        compiler_params=params(),
        name="first_sum",
    )(got)


def places(which):
    lane = lax.broadcasted_iota(jnp.int32, (ROWS, LANES), 1)
    row = lax.broadcasted_iota(jnp.int32, (ROWS, LANES), 0)
    return lane == jnp.where(which < 8 * 24 // ROWS, row & 7, 8)


def joined(blocks, first):
    def part(k):
        return blocks if k == 0 else pltpu.roll(blocks, LANES - ROWS * k, 1)

    def over(x):
        return jnp.sum(x, axis=0, keepdims=True)

    bb, bw, ww, near, rr, rw, rz, wz = (part(k) for k in range(8))
    all_bb, all_bw, all_ww = over(bb), over(bw), over(ww)
    middle = all_bb / all_bw if first else jnp.where(all_ww > 0.0, all_bw / all_ww, 0.0)
    shift = near - middle
    return (all_bb, all_bw, all_ww, middle, over(rr + shift * (2.0 * rw + shift * ww)), over(rw + shift * ww),
            over(rz + shift * wz), over(wz))


def put(lines):
    lane = lax.broadcasted_iota(jnp.int32, (1, LANES), 1)
    out = jnp.zeros((1, LANES), F32)
    for k, line in enumerate(lines):
        line = jnp.where(lane < PROBES, line, 0.0)
        out = out + (line if k == 0 else pltpu.roll(line, ROWS * k, 1))
    return out


def chunk_body(in_ref, b_ref, which_ref, chunk_ref, line_ref):
    total = jnp.sum(in_ref[...], axis=0)
    chunk_ref[...] = total
    which = which_ref[0]
    b, z, w = b_ref[which], total[0:ROWS], total[ROWS:BOTH]
    here = places(which)

    def dot(x, y):
        return jnp.sum(jnp.where(here, jnp.sum(x * y, axis=1, keepdims=True), 0.0), axis=0, keepdims=True)

    ww, bw = dot(w, w), dot(b, w)
    near = jnp.where(ww > 0.0, bw / ww, 0.0)
    r = b - jnp.sum(jnp.where(here, near, 0.0), axis=1, keepdims=True) * w
    line = put((dot(b, b), bw, ww, near, dot(r, r), dot(r, w), dot(r, z), dot(w, z)))
    for s in range(SIDE):
        line_ref[s] = jnp.broadcast_to(line, (LINES, LANES))


def chunk_sums(got, b, which):
    return pl.pallas_call(
        chunk_body,
        out_shape=(jax.ShapeDtypeStruct((BOTH, LANES), F32), jax.ShapeDtypeStruct((SIDE, LINES, LANES), F32)),
        in_specs=[vspec(), vspec(), sspec()],
        out_specs=(vspec(), vspec()),
        compiler_params=params(),
        name="chunk_sums",
    )(got, b, which)


def join_body(chunk_ref, line_ref, out_ref):
    line = put(joined(jnp.concatenate([line_ref[s, 0:1, :] for s in range(SIDE)], axis=0), False))
    for s in range(SIDE):
        out_ref[s, 0:BOTH, :] = chunk_ref[...]
        out_ref[s, BOTH:MORE, :] = jnp.broadcast_to(line, (MORE - BOTH, LANES))


def join(chunk, line):
    return pl.pallas_call(
        join_body,
        out_shape=jax.ShapeDtypeStruct((SIDE, MORE, LANES), F32),
        in_specs=[vspec(), vspec()],
        out_specs=vspec(),
        compiler_params=params(),
        name="join",
    )(chunk, line)


def finish_body(b_ref, a_ref, x_ref, r_ref, nw, na):
    tiles = b_ref.shape[1] // LANES
    unpack(a_ref, na, tiles)
    unpack(a_ref, nw, tiles, ROWS)
    lines = joined(jnp.concatenate([a_ref[s, BOTH : BOTH + 1, :] for s in range(SIDE)], axis=0), True)
    bb, bw, _, first, rr, rw, rz, _ = (to_column(line, 0) for line in lines)
    beta = rr / bb
    second = rr / ((rw - first * rz) + 2.0 * beta * rw + beta * beta * bw)
    b = b_ref[...]
    w = nw[0:PROBES, :]
    r = b - first * w
    x_ref[...] = first * b + second * (r + beta * b)
    r_ref[...] = r - second * ((w - first * na[0:PROBES, :]) + beta * w)


def finish(b, a):
    n = b.shape[1]
    out = jax.ShapeDtypeStruct((PROBES, n), F32)
    return pl.pallas_call(
        finish_body,
        out_shape=(out, out),
        in_specs=[vspec()] * 2,
        out_specs=(vspec(), vspec()),
        scratch_shapes=[VMEM((ROWS, n), F32), VMEM((ROWS, n), F32)],
        compiler_params=params(),
        name="finish",
    )(b, a)


def on_device(right_side, noise_level, run_index, step_index, run_features):
    swap = [(i * SIDE + j, j * SIDE + i) for i in range(SIDE) for j in range(SIDE)]

    def exchange(x, axis):
        return lax.all_to_all(x, axis, 0, 0)

    flag = (lax.axis_index("row") == lax.axis_index("col")).astype(F32).reshape(1)
    which = lax.axis_index("col").reshape(1)
    tiles = run_index.shape[0] // LANES
    run = run_index.reshape(tiles, LANES)
    step = step_index.reshape(tiles, LANES)
    decays = (jnp.asarray(x) for x in decay_tables())
    other = lax.ppermute(jnp.stack([run, step]), ("row", "col"), swap)
    *mine, extra, packed = own(run, step, run_features, right_side, noise_level, flag, *decays)
    khi, klo, part = build(other, *mine)
    product = exchange(first_sum(exchange(part, "row")), "row")
    both = exchange(apply(khi, klo, product, extra, flag), "col")
    chunk, line = chunk_sums(both, packed, which)
    again = exchange(join(chunk, exchange(line, "row")), "col")
    return finish(right_side, again)


def solution(mesh):
    return jax.shard_map(
        on_device,
        mesh=mesh,
        in_specs=(P(None, "row"), P("row"), P("row"), P("row"), P()),
        out_specs=(P(None, "row"), P(None, "row")),
        check_vma=False,
    )
```

```python
import functools
import math

import jax
import jax.numpy as jnp
import numpy as np
from jax import lax
from jax.experimental import pallas as pl
from jax.experimental.pallas import tpu as pltpu
from jax.sharding import PartitionSpec as P

LANES = 128
SIDE = 16
FEAT = 16
PROBES = 9
ROWS = 16
BUILD = 12
BOTH = 32
MORE = 40
LINES = 8
GROUP = 4096
DEPTH = 256
RANK = 24
STEPS = 128
LOG2E = 1.4426950408889634
F32 = jnp.float32
BF16 = jnp.bfloat16
F8 = jnp.float8_e4m3fn
TOP = 240.0
LIFT = 65536.0
VMEM = pltpu.VMEM
MIB = 1024 * 1024


def vspec():
    return pl.BlockSpec(memory_space=VMEM)


def sspec():
    return pl.BlockSpec(memory_space=pltpu.SMEM)


def params(mib=2):
    return pltpu.CompilerParams(vmem_limit_bytes=mib * MIB)


def thirds(x):
    a = x.astype(BF16).astype(F32)
    b = (x - a).astype(BF16).astype(F32)
    return a, b, x - a - b


def to_column(row, first):
    lane = lax.broadcasted_iota(jnp.int32, (PROBES, LANES), 1)
    sub = lax.broadcasted_iota(jnp.int32, (PROBES, LANES), 0)
    return jnp.sum(jnp.where(lane == sub + first, row, 0.0), axis=1, keepdims=True)


def unpack(v_ref, nat, tiles, first=0):
    for t in range(tiles):
        lanes = slice(t * LANES, (t + 1) * LANES)
        row = first + 8 * (t % 2)
        nat[0:8, lanes] = v_ref[t // 2, row : row + 8, :]
        m = 8 * tiles + t
        row = first + m % ROWS
        nat[8:9, lanes] = v_ref[m // ROWS, row : row + 1, :]


def pack_tile(out_ref, res, tile, tiles):
    out_ref[tile // 2, pl.ds(pl.multiple_of(8 * (tile % 2), 8), 8), :] = res[0:8]
    m = 8 * tiles + tile
    out_ref[m // ROWS, pl.ds(m % ROWS, 1), :] = res[8:9]


def clear_rest(out_ref, tiles):
    m = 9 * tiles
    out_ref[m // ROWS, m % ROWS : ROWS, :] = jnp.zeros((ROWS - m % ROWS, LANES), F32)
    for s in range(m // ROWS + 1, SIDE):
        out_ref[s, 0:ROWS, :] = jnp.zeros((ROWS, LANES), F32)


def factors(v):
    zero = jnp.zeros((ROWS - PROBES, v.shape[1]), F32)
    high = v.astype(BF16).astype(F32)
    halves = jnp.concatenate([high, zero, v - high, zero], axis=0).astype(BF16)
    top = jnp.max(jnp.abs(v), axis=1, keepdims=True)
    top = jnp.where(top > 0.0, top, 1.0)
    u = v * (TOP / top)
    coarse = u.astype(F8).astype(F32)
    small = jnp.concatenate([coarse, zero, (u - coarse), zero], axis=0).astype(F8)
    return halves, small, top * (1.0 / (TOP * LIFT))


def fetch(read, table, rows, t, at):
    for p in range(LANES):
        rows[pl.ds(at + p, 1), :] = table[pl.ds(read(t, p), 1), :]


def turn(rows, group):
    turned = jnp.transpose(rows)
    f = turned[0:FEAT]
    for g in range(1, LANES // FEAT):
        f = jnp.where(group == g, turned[g * FEAT : (g + 1) * FEAT], f)
    return f


def pack(out_ref, v, tiles):
    clear_rest(out_ref, tiles)
    for t in range(tiles):
        pack_tile(out_ref, v[:, t * LANES : (t + 1) * LANES], t, tiles)


def operand(f, is_left):
    f = f * math.sqrt(LOG2E)
    a, b, c = thirds(f)
    norm = -0.5 * jnp.sum(f * f, axis=0, keepdims=True)
    if is_left:
        norm = norm + math.log2(LIFT)
    na, nb, nc = thirds(norm)
    one = jnp.ones_like(norm)
    if is_left:
        parts = [a, a, b, b, a, c, na, nb, nc, one, one, one]
    else:
        parts = [a, b, a, b, c, a, one, one, one, na, nb, nc]
    return jnp.concatenate(parts + [jnp.zeros((2, f.shape[1]), F32)], axis=0)


def own_body(idx_ref, flag_ref, ids_ref, tab_ref, b_ref, noise_ref, decay_ref, right_ref,
             right_decay, table, left, vec, small, scale, extra_b, extra, packed,
             ids, tab, b, noise, decay, terms, rows, sems):
    groups = tab_ref.shape[1] // GROUP
    width = GROUP // 4
    tiles = ids_ref.shape[1]
    pairs = [(ids_ref, ids), (decay_ref, decay), (b_ref, b), (noise_ref, noise), (right_ref, right_decay)]
    loads = [pltpu.make_async_copy(src, dst, sems.at[k]) for k, (src, dst) in enumerate(pairs)]
    parts = []
    for c in range(4):
        for g in range(groups):
            at = pl.ds(g * GROUP + c * width, width)
            parts.append(pltpu.make_async_copy(tab_ref.at[:, at], tab.at[:, at], sems.at[5 + c * groups + g]))
    for part in loads + parts:
        part.start()
    loads[0].wait()
    loads[1].wait()
    table_left = decay[...].astype(BF16)
    for t in range(tiles):
        o = slice(t * LANES, (t + 1) * LANES)
        hot = one_hot(ids[2, t : t + 1, :])
        terms[:, o] = jnp.dot(table_left, hot, preferred_element_type=F32)
        left[o, LANES:] = jnp.transpose(hot.astype(F32)).astype(BF16)
    loads[2].wait()
    loads[3].wait()
    vec[...], small[...], factor = factors(b[...])
    scale[...] = jnp.concatenate([jnp.broadcast_to(factor, (PROBES, LANES)), jnp.zeros((ROWS - PROBES, LANES), F32)], axis=0)
    pack(packed, b[...], tiles)
    extra[...] = flag_ref[0] * noise[...]
    extra_b[...] = flag_ref[0] * noise[...] * b[...]
    blank = jnp.zeros((LANES - groups * FEAT, LANES), F32)
    for c in range(4):
        for part in parts[c * groups : (c + 1) * groups]:
            part.wait()
        for t in range(c * (width // LANES), (c + 1) * (width // LANES)):
            pieces = [tab[:, g * GROUP + t * LANES : g * GROUP + (t + 1) * LANES] for g in range(groups)]
            table[t * LANES : (t + 1) * LANES, :] = jnp.transpose(jnp.concatenate(pieces + [blank], axis=0))
    loads[4].wait()

    def get(t, _):
        fetch(lambda t, p: idx_ref[0, t, p], table, rows, t, pl.multiple_of(t * LANES, LANES))
        return 0

    lax.fori_loop(0, tiles, get, 0)
    for t in range(tiles):
        o = slice(t * LANES, (t + 1) * LANES)
        f = turn(rows[o, :], ids[1, t : t + 1, :])
        left[o, 0:LANES] = jnp.transpose(jnp.concatenate([operand(f, True), terms[:, o]], axis=0)).astype(BF16)


def decay_tables():
    rest = np.array([[-1.5 * math.log2((s + t + 8.0) / 8.0) for t in range(STEPS)] for s in range(STEPS)])

    def rounded(x):
        return x.astype(BF16).astype(np.float64)

    left, right = [], []
    for _ in range(RANK):
        s, t = divmod(int(np.argmax(np.abs(rest))), STEPS)
        a, b = rounded(rest[:, t] / rest[s, t]), rounded(rest[s, :])
        left.append(a)
        right.append(b)
        rest = rest - np.outer(a, b)
    return np.array(left).astype(np.float32), np.concatenate([np.array(right), rounded(rest)]).astype(np.float32)


def one_hot(step):
    row = lax.broadcasted_iota(jnp.int32, (STEPS, LANES), 0)
    return jnp.where(row == step, 1.0, 0.0).astype(BF16)


def hbm(x):
    return pltpu.with_memory_space_constraint(x, pltpu.HBM)


def own(ids, table, b, noise, flag, decay, right_decay):
    n = b.shape[1]
    return pl.pallas_call(
        own_body,
        out_shape=(
            VMEM(right_decay.shape, F32),
            VMEM((GROUP, LANES), F32),
            VMEM((n, DEPTH), BF16),
            VMEM((2 * ROWS, n), BF16),
            VMEM((2 * ROWS, n), F8),
            VMEM((ROWS, LANES), F32),
            VMEM((PROBES, n), F32),
            VMEM((1, n), F32),
            jax.ShapeDtypeStruct((SIDE, ROWS, LANES), F32),
        ),
        in_specs=[sspec()] * 2 + [pl.BlockSpec(memory_space=pl.ANY)] * 6,
        out_specs=(vspec(),) * 9,
        scratch_shapes=[
            VMEM(ids.shape, jnp.int32),
            VMEM(table.shape, F32),
            VMEM(b.shape, F32),
            VMEM((1, n), F32),
            VMEM(decay.shape, F32),
            VMEM((RANK, n), F32),
            VMEM((n, LANES), F32),
            pltpu.SemaphoreType.DMA((5 + 4 * (table.shape[1] // GROUP),)),
        ],
        compiler_params=params(12),
        cost_estimate=pl.CostEstimate(flops=n * 6000, bytes_accessed=4 * table.size, transcendentals=0),
        name="own",
    )(ids, flag, ids, *(hbm(x) for x in (table, b, noise.reshape(1, n), decay, right_decay)))


def build_body(idx_ref, other, decay, table, left, vec, small, scale, extra_b,
               khi_ref, klo_ref, out_ref, rows, right, acc, acc8, *, pt, qt):
    n, m = khi_ref.shape
    tiles = m // LANES
    per = qt // LANES

    def ready(jq, slot):
        for k in range(per):
            t = jq * per + k
            o = slice(k * LANES, (k + 1) * LANES)
            fetch(lambda t, p: idx_ref[0, t, p], table, rows, t, k * LANES)
            f = turn(rows[o, :], other[1, pl.ds(t, 1), :])
            terms = jnp.dot(decay[...].astype(BF16), one_hot(other[2, pl.ds(t, 1), :]), preferred_element_type=F32)
            right[slot, :, o] = jnp.concatenate([operand(f, False), terms], axis=0).astype(BF16)

    def column(jq, _):
        oq = pl.ds(pl.multiple_of(jq * qt, qt), qt)
        right_tile = right[jq % 2]
        acc[...] = jnp.zeros_like(acc)
        acc8[...] = jnp.zeros_like(acc8)

        def row(ip, _):
            op = pl.ds(pl.multiple_of(ip * pt, pt), pt)
            power = jnp.dot(left[op, :], right_tile, preferred_element_type=F32)
            k = jnp.exp2(power)
            high = k.astype(BF16)
            low = (k - high.astype(F32)).astype(BF16).astype(F8)
            khi_ref[op, oq] = high
            klo_ref[op, oq] = low
            acc[...] += jnp.dot(vec[:, op], high, preferred_element_type=F32)
            acc8[...] += jnp.dot(small[:, op], low, preferred_element_type=F32)
            return 0

        lax.fori_loop(0, n // pt, row, 0, unroll=n // pt)
        res = (acc[0:ROWS, :] + acc[ROWS:, :]) * (1.0 / LIFT) + scale[:, 0:1] * (acc8[0:ROWS, :] + acc8[ROWS:, :])
        res = res[0:PROBES] + extra_b[:, oq]
        for t in range(qt // LANES):
            pack_tile(out_ref, res[:, t * LANES : (t + 1) * LANES], jq * (qt // LANES) + t, tiles)
        ready(jnp.minimum(jq + 1, m // qt - 1), (jq + 1) % 2)
        return 0

    clear_rest(out_ref, tiles)
    ready(0, 0)
    lax.fori_loop(0, m // qt, column, 0)


def build(other, decay, table, left, vec, small, scale, extra_b, pt=3072, qt=512):
    n = left.shape[0]
    m = other.shape[1] * LANES
    return pl.pallas_call(
        functools.partial(build_body, pt=pt, qt=qt),
        out_shape=(VMEM((n, m), BF16), VMEM((n, m), F8), jax.ShapeDtypeStruct((SIDE, ROWS, LANES), F32)),
        in_specs=[sspec()] + [vspec()] * 8,
        out_specs=(vspec(),) * 3,
        scratch_shapes=[
            VMEM((qt, LANES), F32),
            VMEM((2, DEPTH, qt), BF16),
            VMEM((2 * ROWS, qt), F32),
            VMEM((2 * ROWS, qt), F32),
        ],
        compiler_params=params(BUILD),
        cost_estimate=pl.CostEstimate(flops=n * m * 1000, bytes_accessed=n * m * 3, transcendentals=2 * n * m),
        name="build",
    )(other, other, decay, table, left, vec, small, scale, extra_b)


def apply_body(khi_ref, klo_ref, w_ref, extra, flag_ref, out_ref, nat, vec, small, *, pt):
    n, m = khi_ref.shape
    unpack(w_ref, nat, m // LANES)
    vec[...], small[...], scale = factors(nat[0:PROBES, :])
    clear_rest(out_ref, n // LANES)
    for s in range(SIDE):
        out_ref[s, ROWS:BOTH, :] = flag_ref[0] * w_ref[s]
    dims = (((1,), (1,)), ((), ()))

    def row(ip, _):
        op = pl.ds(pl.multiple_of(ip * pt, pt), pt)
        y = lax.dot_general(vec[...], khi_ref[op, :], dims, preferred_element_type=F32)
        z = lax.dot_general(small[...], klo_ref[op, :], dims, preferred_element_type=F32)
        res = (y[0:ROWS] + y[ROWS:])[0:PROBES] * (1.0 / LIFT) + scale * (z[0:ROWS] + z[ROWS:])[0:PROBES]
        res = res + extra[:, op] * nat[0:PROBES, op]
        for t in range(pt // LANES):
            pack_tile(out_ref, res[:, t * LANES : (t + 1) * LANES], ip * (pt // LANES) + t, n // LANES)
        return 0

    lax.fori_loop(0, n // pt, row, 0)


def apply(khi, klo, w, extra, flag, pt=512):
    n, m = khi.shape
    khi = pltpu.with_memory_space_constraint(khi, VMEM)
    klo = pltpu.with_memory_space_constraint(klo, VMEM)
    return pl.pallas_call(
        functools.partial(apply_body, pt=pt),
        out_shape=jax.ShapeDtypeStruct((SIDE, BOTH, LANES), F32),
        in_specs=[vspec()] * 4 + [sspec()],
        out_specs=vspec(),
        scratch_shapes=[VMEM((ROWS, m), F32), VMEM((2 * ROWS, m), BF16), VMEM((2 * ROWS, m), F8)],
        compiler_params=params(4),
        cost_estimate=pl.CostEstimate(flops=n * m * 600, bytes_accessed=n * m * 3, transcendentals=0),
        name="apply",
    )(khi, klo, w, extra, flag)


def first_sum_body(in_ref, out_ref):
    total = jnp.sum(in_ref[...], axis=0)
    for s in range(SIDE):
        out_ref[s] = total


def first_sum(got):
    return pl.pallas_call(
        first_sum_body,
        out_shape=jax.ShapeDtypeStruct((SIDE, ROWS, LANES), F32),
        in_specs=[vspec()],
        out_specs=vspec(),
        compiler_params=params(),
        name="first_sum",
    )(got)


def places(which):
    lane = lax.broadcasted_iota(jnp.int32, (ROWS, LANES), 1)
    row = lax.broadcasted_iota(jnp.int32, (ROWS, LANES), 0)
    return lane == jnp.where(which < 8 * 24 // ROWS, row & 7, 8)


def joined(blocks, first):
    def part(k):
        return blocks if k == 0 else pltpu.roll(blocks, LANES - ROWS * k, 1)

    def over(x):
        return jnp.sum(x, axis=0, keepdims=True)

    bb, bw, ww, near, rr, rw, rz, wz = (part(k) for k in range(8))
    all_bb, all_bw, all_ww = over(bb), over(bw), over(ww)
    middle = all_bb / all_bw if first else jnp.where(all_ww > 0.0, all_bw / all_ww, 0.0)
    shift = near - middle
    return (all_bb, all_bw, all_ww, middle, over(rr + shift * (2.0 * rw + shift * ww)), over(rw + shift * ww),
            over(rz + shift * wz), over(wz))


def put(lines):
    lane = lax.broadcasted_iota(jnp.int32, (1, LANES), 1)
    out = jnp.zeros((1, LANES), F32)
    for k, line in enumerate(lines):
        line = jnp.where(lane < PROBES, line, 0.0)
        out = out + (line if k == 0 else pltpu.roll(line, ROWS * k, 1))
    return out


def chunk_body(in_ref, b_ref, which_ref, chunk_ref, line_ref):
    total = jnp.sum(in_ref[...], axis=0)
    chunk_ref[...] = total
    which = which_ref[0]
    b, z, w = b_ref[which], total[0:ROWS], total[ROWS:BOTH]
    here = places(which)

    def dot(x, y):
        return jnp.sum(jnp.where(here, jnp.sum(x * y, axis=1, keepdims=True), 0.0), axis=0, keepdims=True)

    ww, bw = dot(w, w), dot(b, w)
    near = jnp.where(ww > 0.0, bw / ww, 0.0)
    r = b - jnp.sum(jnp.where(here, near, 0.0), axis=1, keepdims=True) * w
    line = put((dot(b, b), bw, ww, near, dot(r, r), dot(r, w), dot(r, z), dot(w, z)))
    for s in range(SIDE):
        line_ref[s] = jnp.broadcast_to(line, (LINES, LANES))


def chunk_sums(got, b, which):
    return pl.pallas_call(
        chunk_body,
        out_shape=(jax.ShapeDtypeStruct((BOTH, LANES), F32), jax.ShapeDtypeStruct((SIDE, LINES, LANES), F32)),
        in_specs=[vspec(), vspec(), sspec()],
        out_specs=(vspec(), vspec()),
        compiler_params=params(),
        name="chunk_sums",
    )(got, b, which)


def join_body(chunk_ref, line_ref, out_ref):
    line = put(joined(jnp.concatenate([line_ref[s, 0:1, :] for s in range(SIDE)], axis=0), False))
    for s in range(SIDE):
        out_ref[s, 0:BOTH, :] = chunk_ref[...]
        out_ref[s, BOTH:MORE, :] = jnp.broadcast_to(line, (MORE - BOTH, LANES))


def join(chunk, line):
    return pl.pallas_call(
        join_body,
        out_shape=jax.ShapeDtypeStruct((SIDE, MORE, LANES), F32),
        in_specs=[vspec(), vspec()],
        out_specs=vspec(),
        compiler_params=params(),
        name="join",
    )(chunk, line)


def finish_body(b_ref, a_ref, x_ref, r_ref, nw, na):
    tiles = b_ref.shape[1] // LANES
    unpack(a_ref, na, tiles)
    unpack(a_ref, nw, tiles, ROWS)
    lines = joined(jnp.concatenate([a_ref[s, BOTH : BOTH + 1, :] for s in range(SIDE)], axis=0), True)
    bb, bw, _, first, rr, rw, rz, _ = (to_column(line, 0) for line in lines)
    beta = rr / bb
    second = rr / ((rw - first * rz) + 2.0 * beta * rw + beta * beta * bw)
    b = b_ref[...]
    w = nw[0:PROBES, :]
    r = b - first * w
    x_ref[...] = first * b + second * (r + beta * b)
    r_ref[...] = r - second * ((w - first * na[0:PROBES, :]) + beta * w)


def finish(b, a):
    n = b.shape[1]
    out = jax.ShapeDtypeStruct((PROBES, n), F32)
    return pl.pallas_call(
        finish_body,
        out_shape=(out, out),
        in_specs=[vspec()] * 2,
        out_specs=(vspec(), vspec()),
        scratch_shapes=[VMEM((ROWS, n), F32), VMEM((ROWS, n), F32)],
        compiler_params=params(),
        name="finish",
    )(b, a)


def on_device(right_side, noise_level, run_index, step_index, run_features):
    swap = [(i * SIDE + j, j * SIDE + i) for i in range(SIDE) for j in range(SIDE)]

    def exchange(x, axis):
        return lax.all_to_all(x, axis, 0, 0)

    flag = (lax.axis_index("row") == lax.axis_index("col")).astype(F32).reshape(1)
    which = lax.axis_index("col").reshape(1)
    tiles = run_index.shape[0] // LANES
    run = run_index.reshape(tiles, LANES)
    step = step_index.reshape(tiles, LANES)
    decays = (jnp.asarray(x) for x in decay_tables())
    plane = lax.broadcasted_iota(jnp.int32, (3, tiles, LANES), 0)
    ids = jnp.where(plane == 0, run & (GROUP - 1), jnp.where(plane == 1, run >> 12, step))
    other = lax.ppermute(ids, ("row", "col"), swap)
    *mine, extra, packed = own(ids, run_features, right_side, noise_level, flag, *decays)
    khi, klo, part = build(other, *mine)
    product = exchange(first_sum(exchange(part, "row")), "row")
    both = exchange(apply(khi, klo, product, extra, flag), "col")
    chunk, line = chunk_sums(both, packed, which)
    again = exchange(join(chunk, exchange(line, "row")), "col")
    return finish(right_side, again)


def solution(mesh):
    return jax.shard_map(
        on_device,
        mesh=mesh,
        in_specs=(P(None, "row"), P("row"), P("row"), P("row"), P()),
        out_specs=(P(None, "row"), P(None, "row")),
        check_vma=False,
    )
```

```python
import functools
import math

import jax
import jax.numpy as jnp
import numpy as np
from jax import lax
from jax.experimental import pallas as pl
from jax.experimental.pallas import tpu as pltpu
from jax.sharding import PartitionSpec as P

LANES = 128
SIDE = 16
FEAT = 16
PROBES = 9
ROWS = 16
BUILD = 12
BOTH = 32
MORE = 40
LINES = 8
GROUP = 4096
DEPTH = 256
RANK = 24
STEPS = 128
LOG2E = 1.4426950408889634
F32 = jnp.float32
BF16 = jnp.bfloat16
F8 = jnp.float8_e4m3fn
TOP = 240.0
LIFT = 65536.0
VMEM = pltpu.VMEM
MIB = 1024 * 1024


def vspec():
    return pl.BlockSpec(memory_space=VMEM)


def sspec():
    return pl.BlockSpec(memory_space=pltpu.SMEM)


def params(mib=2):
    return pltpu.CompilerParams(vmem_limit_bytes=mib * MIB)


def thirds(x):
    a = x.astype(BF16).astype(F32)
    b = (x - a).astype(BF16).astype(F32)
    return a, b, x - a - b


def to_column(row, first):
    lane = lax.broadcasted_iota(jnp.int32, (PROBES, LANES), 1)
    sub = lax.broadcasted_iota(jnp.int32, (PROBES, LANES), 0)
    return jnp.sum(jnp.where(lane == sub + first, row, 0.0), axis=1, keepdims=True)


def unpack(v_ref, nat, tiles, first=0):
    for t in range(tiles):
        lanes = slice(t * LANES, (t + 1) * LANES)
        row = first + 8 * (t % 2)
        nat[0:8, lanes] = v_ref[t // 2, row : row + 8, :]
        m = 8 * tiles + t
        row = first + m % ROWS
        nat[8:9, lanes] = v_ref[m // ROWS, row : row + 1, :]


def pack_tile(out_ref, res, tile, tiles):
    out_ref[tile // 2, pl.ds(pl.multiple_of(8 * (tile % 2), 8), 8), :] = res[0:8]
    m = 8 * tiles + tile
    out_ref[m // ROWS, pl.ds(m % ROWS, 1), :] = res[8:9]


def clear_rest(out_ref, tiles):
    m = 9 * tiles
    out_ref[m // ROWS, m % ROWS : ROWS, :] = jnp.zeros((ROWS - m % ROWS, LANES), F32)
    for s in range(m // ROWS + 1, SIDE):
        out_ref[s, 0:ROWS, :] = jnp.zeros((ROWS, LANES), F32)


def factors(v):
    zero = jnp.zeros((ROWS - PROBES, v.shape[1]), F32)
    high = v.astype(BF16).astype(F32)
    halves = jnp.concatenate([high, zero, v - high, zero], axis=0).astype(BF16)
    top = jnp.max(jnp.abs(v), axis=1, keepdims=True)
    top = jnp.where(top > 0.0, top, 1.0)
    u = v * (TOP / top)
    coarse = u.astype(F8).astype(F32)
    small = jnp.concatenate([coarse, zero, (u - coarse), zero], axis=0).astype(F8)
    return halves, small, top * (1.0 / (TOP * LIFT))


def fetch(read, table, rows, t, at):
    for p in range(LANES):
        rows[pl.ds(at + p, 1), :] = table[pl.ds(read(t, p), 1), :]


def turn(rows, group):
    turned = jnp.transpose(rows)
    f = turned[0:FEAT]
    for g in range(1, LANES // FEAT):
        f = jnp.where(group == g, turned[g * FEAT : (g + 1) * FEAT], f)
    return f


def pack(out_ref, v, tiles):
    clear_rest(out_ref, tiles)
    for t in range(tiles):
        pack_tile(out_ref, v[:, t * LANES : (t + 1) * LANES], t, tiles)


def operand(f, is_left):
    f = f * math.sqrt(LOG2E)
    a, b, c = thirds(f)
    norm = -0.5 * jnp.sum(f * f, axis=0, keepdims=True)
    if is_left:
        norm = norm + math.log2(LIFT)
    na, nb, nc = thirds(norm)
    one = jnp.ones_like(norm)
    if is_left:
        parts = [a, a, b, b, a, c, na, nb, nc, one, one, one]
    else:
        parts = [a, b, a, b, c, a, one, one, one, na, nb, nc]
    return jnp.concatenate(parts + [jnp.zeros((2, f.shape[1]), F32)], axis=0)


def own_body(idx_ref, flag_ref, ids_ref, tab_ref, b_ref, noise_ref, decay_ref, right_ref,
             right_decay, table, left, vec, small, scale, extra_b, extra, packed,
             ids, tab, b, noise, decay, terms, rows, sems):
    groups = tab_ref.shape[1] // GROUP
    width = GROUP // 4
    tiles = ids_ref.shape[1]
    pairs = [(ids_ref, ids), (decay_ref, decay), (b_ref, b), (noise_ref, noise), (right_ref, right_decay)]
    loads = [pltpu.make_async_copy(src, dst, sems.at[k]) for k, (src, dst) in enumerate(pairs)]
    parts = []
    for c in range(4):
        for g in range(groups):
            at = pl.ds(g * GROUP + c * width, width)
            parts.append(pltpu.make_async_copy(tab_ref.at[:, at], tab.at[:, at], sems.at[5 + c * groups + g]))
    for part in loads + parts:
        part.start()
    loads[0].wait()
    loads[1].wait()
    table_left = decay[...].astype(BF16)
    for t in range(tiles):
        o = slice(t * LANES, (t + 1) * LANES)
        hot = one_hot(ids[2, t : t + 1, :])
        terms[:, o] = jnp.dot(table_left, hot, preferred_element_type=F32)
        left[o, LANES:] = jnp.transpose(hot.astype(F32)).astype(BF16)
    loads[2].wait()
    loads[3].wait()
    vec[...], small[...], factor = factors(b[...])
    scale[...] = jnp.concatenate([jnp.broadcast_to(factor, (PROBES, LANES)), jnp.zeros((ROWS - PROBES, LANES), F32)], axis=0)
    pack(packed, b[...], tiles)
    extra[...] = flag_ref[0] * noise[...]
    extra_b[...] = flag_ref[0] * noise[...] * b[...]
    blank = jnp.zeros((LANES - groups * FEAT, LANES), F32)
    for c in range(4):
        for part in parts[c * groups : (c + 1) * groups]:
            part.wait()
        for t in range(c * (width // LANES), (c + 1) * (width // LANES)):
            pieces = [tab[:, g * GROUP + t * LANES : g * GROUP + (t + 1) * LANES] for g in range(groups)]
            table[t * LANES : (t + 1) * LANES, :] = jnp.transpose(jnp.concatenate(pieces + [blank], axis=0))
    loads[4].wait()

    def get(t, _):
        fetch(lambda t, p: idx_ref[0, t, p], table, rows, t, pl.multiple_of(t * LANES, LANES))
        return 0

    lax.fori_loop(0, tiles, get, 0)
    for t in range(tiles):
        o = slice(t * LANES, (t + 1) * LANES)
        f = turn(rows[o, :], ids[1, t : t + 1, :])
        left[o, 0:LANES] = jnp.transpose(jnp.concatenate([operand(f, True), terms[:, o]], axis=0)).astype(BF16)


def decay_tables():
    rest = np.array([[-1.5 * math.log2((s + t + 8.0) / 8.0) for t in range(STEPS)] for s in range(STEPS)])

    def rounded(x):
        return x.astype(BF16).astype(np.float64)

    left, right = [], []
    for _ in range(RANK):
        s, t = divmod(int(np.argmax(np.abs(rest))), STEPS)
        a, b = rounded(rest[:, t] / rest[s, t]), rounded(rest[s, :])
        left.append(a)
        right.append(b)
        rest = rest - np.outer(a, b)
    return np.array(left).astype(np.float32), np.concatenate([np.array(right), rounded(rest)]).astype(np.float32)


def one_hot(step):
    row = lax.broadcasted_iota(jnp.int32, (STEPS, LANES), 0)
    return jnp.where(row == step, 1.0, 0.0).astype(BF16)


def hbm(x):
    return pltpu.with_memory_space_constraint(x, pltpu.HBM)


def own(ids, table, b, noise, flag, decay, right_decay):
    n = b.shape[1]
    return pl.pallas_call(
        own_body,
        out_shape=(
            VMEM(right_decay.shape, F32),
            VMEM((GROUP, LANES), F32),
            VMEM((n, DEPTH), BF16),
            VMEM((2 * ROWS, n), BF16),
            VMEM((2 * ROWS, n), F8),
            VMEM((ROWS, LANES), F32),
            VMEM((PROBES, n), F32),
            VMEM((1, n), F32),
            jax.ShapeDtypeStruct((SIDE, ROWS, LANES), F32),
        ),
        in_specs=[sspec()] * 2 + [pl.BlockSpec(memory_space=pl.ANY)] * 6,
        out_specs=(vspec(),) * 9,
        scratch_shapes=[
            VMEM(ids.shape, jnp.int32),
            VMEM(table.shape, F32),
            VMEM(b.shape, F32),
            VMEM((1, n), F32),
            VMEM(decay.shape, F32),
            VMEM((RANK, n), F32),
            VMEM((n, LANES), F32),
            pltpu.SemaphoreType.DMA((5 + 4 * (table.shape[1] // GROUP),)),
        ],
        compiler_params=params(12),
        cost_estimate=pl.CostEstimate(flops=n * 6000, bytes_accessed=4 * table.size, transcendentals=0),
        name="own",
    )(ids, flag, ids, *(hbm(x) for x in (table, b, noise.reshape(1, n), decay, right_decay)))


def build_body(idx_ref, other, decay, table, left, vec, small, scale, extra_b,
               khi_ref, klo_ref, out_ref, rows, right, acc, acc8, *, pt, qt):
    n, m = khi_ref.shape
    tiles = m // LANES
    per = qt // LANES

    def ready(jq, slot):
        for k in range(per):
            t = jq * per + k
            o = slice(k * LANES, (k + 1) * LANES)
            fetch(lambda t, p: idx_ref[0, t, p], table, rows, t, k * LANES)
            f = turn(rows[o, :], other[1, pl.ds(t, 1), :])
            terms = jnp.dot(decay[...].astype(BF16), one_hot(other[2, pl.ds(t, 1), :]), preferred_element_type=F32)
            right[slot, :, o] = jnp.concatenate([operand(f, False), terms], axis=0).astype(BF16)

    def column(jq, _):
        oq = pl.ds(pl.multiple_of(jq * qt, qt), qt)
        right_tile = right[jq % 2]
        acc[...] = jnp.zeros_like(acc)
        acc8[...] = jnp.zeros_like(acc8)

        def row(ip, _):
            op = pl.ds(pl.multiple_of(ip * pt, pt), pt)
            power = jnp.dot(left[op, :], right_tile, preferred_element_type=F32)
            k = jnp.exp2(power)
            high = k.astype(BF16)
            low = (k - high.astype(F32)).astype(BF16).astype(F8)
            khi_ref[op, oq] = high
            klo_ref[op, oq] = low
            acc[...] += jnp.dot(vec[:, op], high, preferred_element_type=F32)
            acc8[...] += jnp.dot(small[:, op], low, preferred_element_type=F32)
            return 0

        lax.fori_loop(0, n // pt, row, 0, unroll=n // pt)
        res = (acc[0:ROWS, :] + acc[ROWS:, :]) * (1.0 / LIFT) + scale[:, 0:1] * (acc8[0:ROWS, :] + acc8[ROWS:, :])
        res = res[0:PROBES] + extra_b[:, oq]
        for t in range(qt // LANES):
            pack_tile(out_ref, res[:, t * LANES : (t + 1) * LANES], jq * (qt // LANES) + t, tiles)
        ready(jnp.minimum(jq + 1, m // qt - 1), (jq + 1) % 2)
        return 0

    clear_rest(out_ref, tiles)
    ready(0, 0)
    lax.fori_loop(0, m // qt, column, 0)


def build(other, decay, table, left, vec, small, scale, extra_b, pt=3072, qt=512):
    n = left.shape[0]
    m = other.shape[1] * LANES
    return pl.pallas_call(
        functools.partial(build_body, pt=pt, qt=qt),
        out_shape=(VMEM((n, m), BF16), VMEM((n, m), F8), jax.ShapeDtypeStruct((SIDE, ROWS, LANES), F32)),
        in_specs=[sspec()] + [vspec()] * 8,
        out_specs=(vspec(),) * 3,
        scratch_shapes=[
            VMEM((qt, LANES), F32),
            VMEM((2, DEPTH, qt), BF16),
            VMEM((2 * ROWS, qt), F32),
            VMEM((2 * ROWS, qt), F32),
        ],
        compiler_params=params(BUILD),
        cost_estimate=pl.CostEstimate(flops=n * m * 1000, bytes_accessed=n * m * 3, transcendentals=2 * n * m),
        name="build",
    )(other, other, decay, table, left, vec, small, scale, extra_b)


def apply_body(khi_ref, klo_ref, w_ref, extra, flag_ref, out_ref, nat, vec, small, *, pt):
    n, m = khi_ref.shape
    unpack(w_ref, nat, m // LANES)
    vec[...], small[...], scale = factors(nat[0:PROBES, :])
    clear_rest(out_ref, n // LANES)
    for s in range(SIDE):
        out_ref[s, ROWS:BOTH, :] = flag_ref[0] * w_ref[s]
    dims = (((1,), (1,)), ((), ()))

    def row(ip, _):
        op = pl.ds(pl.multiple_of(ip * pt, pt), pt)
        y = lax.dot_general(vec[...], khi_ref[op, :], dims, preferred_element_type=F32)
        z = lax.dot_general(small[...], klo_ref[op, :], dims, preferred_element_type=F32)
        res = (y[0:ROWS] + y[ROWS:])[0:PROBES] * (1.0 / LIFT) + scale * (z[0:ROWS] + z[ROWS:])[0:PROBES]
        res = res + extra[:, op] * nat[0:PROBES, op]
        for t in range(pt // LANES):
            pack_tile(out_ref, res[:, t * LANES : (t + 1) * LANES], ip * (pt // LANES) + t, n // LANES)
        return 0

    lax.fori_loop(0, n // pt, row, 0)


def apply(khi, klo, w, extra, flag, pt=512):
    n, m = khi.shape
    khi = pltpu.with_memory_space_constraint(khi, VMEM)
    klo = pltpu.with_memory_space_constraint(klo, VMEM)
    return pl.pallas_call(
        functools.partial(apply_body, pt=pt),
        out_shape=jax.ShapeDtypeStruct((SIDE, BOTH, LANES), F32),
        in_specs=[vspec()] * 4 + [sspec()],
        out_specs=vspec(),
        scratch_shapes=[VMEM((ROWS, m), F32), VMEM((2 * ROWS, m), BF16), VMEM((2 * ROWS, m), F8)],
        compiler_params=params(4),
        cost_estimate=pl.CostEstimate(flops=n * m * 600, bytes_accessed=n * m * 3, transcendentals=0),
        name="apply",
    )(khi, klo, w, extra, flag)


def first_sum_body(in_ref, out_ref):
    total = jnp.sum(in_ref[...], axis=0)
    for s in range(SIDE):
        out_ref[s] = total


def first_sum(got):
    return pl.pallas_call(
        first_sum_body,
        out_shape=jax.ShapeDtypeStruct((SIDE, ROWS, LANES), F32),
        in_specs=[vspec()],
        out_specs=vspec(),
        compiler_params=params(),
        name="first_sum",
    )(got)


def places(which):
    lane = lax.broadcasted_iota(jnp.int32, (ROWS, LANES), 1)
    row = lax.broadcasted_iota(jnp.int32, (ROWS, LANES), 0)
    return lane == jnp.where(which < 8 * 24 // ROWS, row & 7, 8)


def joined(blocks, first):
    def part(k):
        return blocks if k == 0 else pltpu.roll(blocks, LANES - ROWS * k, 1)

    def over(x):
        return jnp.sum(x, axis=0, keepdims=True)

    bb, bw, ww, near, rr, rw, rz, wz = (part(k) for k in range(8))
    all_bb, all_bw, all_ww = over(bb), over(bw), over(ww)
    middle = all_bb / all_bw if first else jnp.where(all_ww > 0.0, all_bw / all_ww, 0.0)
    shift = near - middle
    return (all_bb, all_bw, all_ww, middle, over(rr + shift * (2.0 * rw + shift * ww)), over(rw + shift * ww),
            over(rz + shift * wz), over(wz))


def put(lines):
    lane = lax.broadcasted_iota(jnp.int32, (1, LANES), 1)
    out = jnp.zeros((1, LANES), F32)
    for k, line in enumerate(lines):
        line = jnp.where(lane < PROBES, line, 0.0)
        out = out + (line if k == 0 else pltpu.roll(line, ROWS * k, 1))
    return out


def chunk_body(in_ref, b_ref, which_ref, chunk_ref, line_ref):
    total = jnp.sum(in_ref[...], axis=0)
    chunk_ref[...] = total
    which = which_ref[0]
    b, z, w = b_ref[which], total[0:ROWS], total[ROWS:BOTH]
    here = places(which)

    def dot(x, y):
        return jnp.sum(jnp.where(here, jnp.sum(x * y, axis=1, keepdims=True), 0.0), axis=0, keepdims=True)

    ww, bw = dot(w, w), dot(b, w)
    near = jnp.where(ww > 0.0, bw / ww, 0.0)
    r = b - jnp.sum(jnp.where(here, near, 0.0), axis=1, keepdims=True) * w
    line = put((dot(b, b), bw, ww, near, dot(r, r), dot(r, w), dot(r, z), dot(w, z)))
    for s in range(SIDE):
        line_ref[s] = jnp.broadcast_to(line, (LINES, LANES))


def chunk_sums(got, b, which):
    return pl.pallas_call(
        chunk_body,
        out_shape=(jax.ShapeDtypeStruct((BOTH, LANES), F32), jax.ShapeDtypeStruct((SIDE, LINES, LANES), F32)),
        in_specs=[vspec(), vspec(), sspec()],
        out_specs=(vspec(), vspec()),
        compiler_params=params(),
        name="chunk_sums",
    )(got, b, which)


def join_body(chunk_ref, line_ref, out_ref):
    line = put(joined(jnp.concatenate([line_ref[s, 0:1, :] for s in range(SIDE)], axis=0), False))
    for s in range(SIDE):
        out_ref[s, 0:BOTH, :] = chunk_ref[...]
        out_ref[s, BOTH:MORE, :] = jnp.broadcast_to(line, (MORE - BOTH, LANES))


def join(chunk, line):
    return pl.pallas_call(
        join_body,
        out_shape=jax.ShapeDtypeStruct((SIDE, MORE, LANES), F32),
        in_specs=[vspec(), vspec()],
        out_specs=vspec(),
        compiler_params=params(),
        name="join",
    )(chunk, line)


def finish_body(b_ref, a_ref, x_ref, r_ref, nw, na):
    tiles = b_ref.shape[1] // LANES
    unpack(a_ref, na, tiles)
    unpack(a_ref, nw, tiles, ROWS)
    lines = joined(jnp.concatenate([a_ref[s, BOTH : BOTH + 1, :] for s in range(SIDE)], axis=0), True)
    bb, bw, _, first, rr, rw, rz, _ = (to_column(line, 0) for line in lines)
    beta = rr / bb
    second = rr / ((rw - first * rz) + 2.0 * beta * rw + beta * beta * bw)
    b = b_ref[...]
    w = nw[0:PROBES, :]
    r = b - first * w
    x_ref[...] = first * b + second * (r + beta * b)
    r_ref[...] = r - second * ((w - first * na[0:PROBES, :]) + beta * w)


def finish(b, a):
    n = b.shape[1]
    out = jax.ShapeDtypeStruct((PROBES, n), F32)
    return pl.pallas_call(
        finish_body,
        out_shape=(out, out),
        in_specs=[vspec()] * 2,
        out_specs=(vspec(), vspec()),
        scratch_shapes=[VMEM((ROWS, n), F32), VMEM((ROWS, n), F32)],
        compiler_params=params(),
        name="finish",
    )(b, a)


def on_device(right_side, noise_level, run_index, step_index, run_features):
    swap = [(i * SIDE + j, j * SIDE + i) for i in range(SIDE) for j in range(SIDE)]

    def exchange(x, axis):
        return lax.all_to_all(x, axis, 0, 0)

    flag = (lax.axis_index("row") == lax.axis_index("col")).astype(F32).reshape(1)
    which = lax.axis_index("col").reshape(1)
    tiles = run_index.shape[0] // LANES
    run = run_index.reshape(tiles, LANES)
    step = step_index.reshape(tiles, LANES)
    decays = (jnp.asarray(x) for x in decay_tables())
    plane = lax.broadcasted_iota(jnp.int32, (3, tiles, LANES), 0)
    ids = jnp.where(plane == 2, step, run)
    ids = (ids >> jnp.where(plane == 1, 12, 0)) & jnp.where(plane == 0, GROUP - 1, -1)
    other = lax.ppermute(ids, ("row", "col"), swap)
    *mine, extra, packed = own(ids, run_features, right_side, noise_level, flag, *decays)
    khi, klo, part = build(other, *mine)
    product = exchange(first_sum(exchange(part, "row")), "row")
    both = exchange(apply(khi, klo, product, extra, flag), "col")
    chunk, line = chunk_sums(both, packed, which)
    again = exchange(join(chunk, exchange(line, "row")), "col")
    return finish(right_side, again)


def solution(mesh):
    return jax.shard_map(
        on_device,
        mesh=mesh,
        in_specs=(P(None, "row"), P("row"), P("row"), P("row"), P()),
        out_specs=(P(None, "row"), P(None, "row")),
        check_vma=False,
    )
```

```python
import functools
import math

import jax
import jax.numpy as jnp
import numpy as np
from jax import lax
from jax.experimental import pallas as pl
from jax.experimental.pallas import tpu as pltpu
from jax.sharding import PartitionSpec as P

LANES = 128
SIDE = 16
FEAT = 16
PROBES = 9
ROWS = 16
BUILD = 12
BOTH = 32
MORE = 40
LINES = 8
GROUP = 4096
DEPTH = 256
RANK = 24
STEPS = 128
LOG2E = 1.4426950408889634
F32 = jnp.float32
BF16 = jnp.bfloat16
F8 = jnp.float8_e4m3fn
TOP = 240.0
LIFT = 65536.0
VMEM = pltpu.VMEM
MIB = 1024 * 1024


def vspec():
    return pl.BlockSpec(memory_space=VMEM)


def sspec():
    return pl.BlockSpec(memory_space=pltpu.SMEM)


def params(mib=2):
    return pltpu.CompilerParams(vmem_limit_bytes=mib * MIB)


def thirds(x):
    a = x.astype(BF16).astype(F32)
    b = (x - a).astype(BF16).astype(F32)
    return a, b, x - a - b


def to_column(row, first):
    lane = lax.broadcasted_iota(jnp.int32, (PROBES, LANES), 1)
    sub = lax.broadcasted_iota(jnp.int32, (PROBES, LANES), 0)
    return jnp.sum(jnp.where(lane == sub + first, row, 0.0), axis=1, keepdims=True)


def unpack(v_ref, nat, tiles, first=0):
    for t in range(tiles):
        lanes = slice(t * LANES, (t + 1) * LANES)
        row = first + 8 * (t % 2)
        nat[0:8, lanes] = v_ref[t // 2, row : row + 8, :]
        m = 8 * tiles + t
        row = first + m % ROWS
        nat[8:9, lanes] = v_ref[m // ROWS, row : row + 1, :]


def pack_tile(out_ref, res, tile, tiles):
    out_ref[tile // 2, pl.ds(pl.multiple_of(8 * (tile % 2), 8), 8), :] = res[0:8]
    m = 8 * tiles + tile
    out_ref[m // ROWS, pl.ds(m % ROWS, 1), :] = res[8:9]


def clear_rest(out_ref, tiles):
    m = 9 * tiles
    out_ref[m // ROWS, m % ROWS : ROWS, :] = jnp.zeros((ROWS - m % ROWS, LANES), F32)
    for s in range(m // ROWS + 1, SIDE):
        out_ref[s, 0:ROWS, :] = jnp.zeros((ROWS, LANES), F32)


def factors(v):
    zero = jnp.zeros((ROWS - PROBES, v.shape[1]), F32)
    high = v.astype(BF16).astype(F32)
    halves = jnp.concatenate([high, zero, v - high, zero], axis=0).astype(BF16)
    top = jnp.max(jnp.abs(v), axis=1, keepdims=True)
    top = jnp.where(top > 0.0, top, 1.0)
    u = v * (TOP / top)
    coarse = u.astype(F8).astype(F32)
    small = jnp.concatenate([coarse, zero, (u - coarse), zero], axis=0).astype(F8)
    return halves, small, top * (1.0 / (TOP * LIFT))


def fetch(read, table, rows, t, at):
    for p in range(LANES):
        rows[pl.ds(at + p, 1), :] = table[pl.ds(read(t, p), 1), :]


def turn(rows, group):
    turned = jnp.transpose(rows)
    f = turned[0:FEAT]
    for g in range(1, LANES // FEAT):
        f = jnp.where(group == g, turned[g * FEAT : (g + 1) * FEAT], f)
    return f


def pack(out_ref, v, tiles):
    clear_rest(out_ref, tiles)
    for t in range(tiles):
        pack_tile(out_ref, v[:, t * LANES : (t + 1) * LANES], t, tiles)


def operand(f, is_left):
    f = f * math.sqrt(LOG2E)
    a, b, c = thirds(f)
    norm = -0.5 * jnp.sum(f * f, axis=0, keepdims=True)
    if is_left:
        norm = norm + math.log2(LIFT)
    na, nb, nc = thirds(norm)
    one = jnp.ones_like(norm)
    if is_left:
        parts = [a, a, b, b, a, c, na, nb, nc, one, one, one]
    else:
        parts = [a, b, a, b, c, a, one, one, one, na, nb, nc]
    return jnp.concatenate(parts + [jnp.zeros((2, f.shape[1]), F32)], axis=0)


def own_body(idx_ref, flag_ref, ids_ref, tab_ref, b_ref, noise_ref, decay_ref, right_ref,
             right_decay, table, left, vec, small, scale, extra_b, extra, packed,
             ids, tab, b, noise, decay, terms, rows, sems):
    groups = tab_ref.shape[1] // GROUP
    width = GROUP // 4
    tiles = ids_ref.shape[1]
    pairs = [(ids_ref, ids), (decay_ref, decay), (b_ref, b), (noise_ref, noise), (right_ref, right_decay)]
    loads = [pltpu.make_async_copy(src, dst, sems.at[k]) for k, (src, dst) in enumerate(pairs)]
    parts = []
    for c in range(4):
        for g in range(groups):
            at = pl.ds(g * GROUP + c * width, width)
            parts.append(pltpu.make_async_copy(tab_ref.at[:, at], tab.at[:, at], sems.at[5 + c * groups + g]))
    for part in loads + parts:
        part.start()
    loads[0].wait()
    loads[1].wait()
    table_left = decay[...].astype(BF16)
    for t in range(tiles):
        o = slice(t * LANES, (t + 1) * LANES)
        hot = one_hot(ids[2, t : t + 1, :])
        terms[:, o] = jnp.dot(table_left, hot, preferred_element_type=F32)
        left[o, LANES:] = jnp.transpose(hot.astype(F32)).astype(BF16)
    loads[2].wait()
    loads[3].wait()
    vec[...], small[...], factor = factors(b[...])
    scale[...] = jnp.concatenate([jnp.broadcast_to(factor, (PROBES, LANES)), jnp.zeros((ROWS - PROBES, LANES), F32)], axis=0)
    pack(packed, b[...], tiles)
    extra[...] = flag_ref[0] * noise[...]
    extra_b[...] = flag_ref[0] * noise[...] * b[...]
    blank = jnp.zeros((LANES - groups * FEAT, LANES), F32)
    for c in range(4):
        for part in parts[c * groups : (c + 1) * groups]:
            part.wait()
        for t in range(c * (width // LANES), (c + 1) * (width // LANES)):
            pieces = [tab[:, g * GROUP + t * LANES : g * GROUP + (t + 1) * LANES] for g in range(groups)]
            table[t * LANES : (t + 1) * LANES, :] = jnp.transpose(jnp.concatenate(pieces + [blank], axis=0))
    loads[4].wait()

    def get(t, _):
        fetch(lambda t, p: idx_ref[0, t, p], table, rows, t, pl.multiple_of(t * LANES, LANES))
        return 0

    lax.fori_loop(0, tiles, get, 0)
    for t in range(tiles):
        o = slice(t * LANES, (t + 1) * LANES)
        f = turn(rows[o, :], ids[1, t : t + 1, :])
        left[o, 0:LANES] = jnp.transpose(jnp.concatenate([operand(f, True), terms[:, o]], axis=0)).astype(BF16)


def decay_tables():
    rest = np.array([[-1.5 * math.log2((s + t + 8.0) / 8.0) for t in range(STEPS)] for s in range(STEPS)])

    def rounded(x):
        return x.astype(BF16).astype(np.float64)

    left, right = [], []
    for _ in range(RANK):
        s, t = divmod(int(np.argmax(np.abs(rest))), STEPS)
        a, b = rounded(rest[:, t] / rest[s, t]), rounded(rest[s, :])
        left.append(a)
        right.append(b)
        rest = rest - np.outer(a, b)
    return np.array(left).astype(np.float32), np.concatenate([np.array(right), rounded(rest)]).astype(np.float32)


def one_hot(step):
    row = lax.broadcasted_iota(jnp.int32, (STEPS, LANES), 0)
    return jnp.where(row == step, 1.0, 0.0).astype(BF16)


def hbm(x):
    return pltpu.with_memory_space_constraint(x, pltpu.HBM)


def own(ids, table, b, noise, flag, decay, right_decay):
    n = b.shape[1]
    return pl.pallas_call(
        own_body,
        out_shape=(
            VMEM(right_decay.shape, F32),
            VMEM((GROUP, LANES), F32),
            VMEM((n, DEPTH), BF16),
            VMEM((2 * ROWS, n), BF16),
            VMEM((2 * ROWS, n), F8),
            VMEM((ROWS, LANES), F32),
            VMEM((PROBES, n), F32),
            VMEM((1, n), F32),
            jax.ShapeDtypeStruct((SIDE, ROWS, LANES), F32),
        ),
        in_specs=[sspec()] * 2 + [pl.BlockSpec(memory_space=pl.ANY)] * 6,
        out_specs=(vspec(),) * 9,
        scratch_shapes=[
            VMEM(ids.shape, jnp.int32),
            VMEM(table.shape, F32),
            VMEM(b.shape, F32),
            VMEM((1, n), F32),
            VMEM(decay.shape, F32),
            VMEM((RANK, n), F32),
            VMEM((n, LANES), F32),
            pltpu.SemaphoreType.DMA((5 + 4 * (table.shape[1] // GROUP),)),
        ],
        compiler_params=params(12),
        cost_estimate=pl.CostEstimate(flops=n * 6000, bytes_accessed=4 * table.size, transcendentals=0),
        name="own",
    )(ids, flag, ids, *(hbm(x) for x in (table, b, noise.reshape(1, n), decay, right_decay)))


def build_body(idx_ref, other, decay, table, left, vec, small, scale, extra_b,
               khi_ref, klo_ref, out_ref, rows, right, acc, acc8, *, pt, qt):
    n, m = khi_ref.shape
    tiles = m // LANES
    per = qt // LANES

    def ready(jq, slot):
        for k in range(per):
            t = jq * per + k
            o = slice(k * LANES, (k + 1) * LANES)
            fetch(lambda t, p: idx_ref[0, t, p], table, rows, t, k * LANES)
            f = turn(rows[o, :], other[1, pl.ds(t, 1), :])
            terms = jnp.dot(decay[...].astype(BF16), one_hot(other[2, pl.ds(t, 1), :]), preferred_element_type=F32)
            right[slot, :, o] = jnp.concatenate([operand(f, False), terms], axis=0).astype(BF16)

    def column(jq, _):
        oq = pl.ds(pl.multiple_of(jq * qt, qt), qt)
        right_tile = right[jq % 2]
        acc[...] = jnp.zeros_like(acc)
        acc8[...] = jnp.zeros_like(acc8)

        def row(ip, _):
            op = pl.ds(pl.multiple_of(ip * pt, pt), pt)
            power = jnp.dot(left[op, :], right_tile, preferred_element_type=F32)
            k = jnp.exp2(power)
            high = k.astype(BF16)
            low = (k - high.astype(F32)).astype(BF16).astype(F8)
            khi_ref[op, oq] = high
            klo_ref[op, oq] = low
            acc[...] += jnp.dot(vec[:, op], high, preferred_element_type=F32)
            acc8[...] += jnp.dot(small[:, op], low, preferred_element_type=F32)
            return 0

        lax.fori_loop(0, n // pt, row, 0, unroll=n // pt)
        res = (acc[0:ROWS, :] + acc[ROWS:, :]) * (1.0 / LIFT) + scale[:, 0:1] * (acc8[0:ROWS, :] + acc8[ROWS:, :])
        res = res[0:PROBES] + extra_b[:, oq]
        for t in range(qt // LANES):
            pack_tile(out_ref, res[:, t * LANES : (t + 1) * LANES], jq * (qt // LANES) + t, tiles)
        ready(jnp.minimum(jq + 1, m // qt - 1), (jq + 1) % 2)
        return 0

    clear_rest(out_ref, tiles)
    ready(0, 0)
    lax.fori_loop(0, m // qt, column, 0)


def build(other, decay, table, left, vec, small, scale, extra_b, pt=3072, qt=512):
    n = left.shape[0]
    m = other.shape[1] * LANES
    return pl.pallas_call(
        functools.partial(build_body, pt=pt, qt=qt),
        out_shape=(VMEM((n, m), BF16), VMEM((n, m), F8), jax.ShapeDtypeStruct((SIDE, ROWS, LANES), F32)),
        in_specs=[sspec()] + [vspec()] * 8,
        out_specs=(vspec(),) * 3,
        scratch_shapes=[
            VMEM((qt, LANES), F32),
            VMEM((2, DEPTH, qt), BF16),
            VMEM((2 * ROWS, qt), F32),
            VMEM((2 * ROWS, qt), F32),
        ],
        compiler_params=params(BUILD),
        cost_estimate=pl.CostEstimate(flops=n * m * 1000, bytes_accessed=n * m * 3, transcendentals=2 * n * m),
        name="build",
    )(other, other, decay, table, left, vec, small, scale, extra_b)


def apply_body(khi_ref, klo_ref, w_ref, extra, flag_ref, out_ref, nat, vec, small, *, pt):
    n, m = khi_ref.shape
    unpack(w_ref, nat, m // LANES)
    vec[...], small[...], scale = factors(nat[0:PROBES, :])
    clear_rest(out_ref, n // LANES)
    for s in range(SIDE):
        out_ref[s, ROWS:BOTH, :] = flag_ref[0] * w_ref[s]
    dims = (((1,), (1,)), ((), ()))

    def row(ip, _):
        op = pl.ds(pl.multiple_of(ip * pt, pt), pt)
        y = lax.dot_general(vec[...], khi_ref[op, :], dims, preferred_element_type=F32)
        z = lax.dot_general(small[...], klo_ref[op, :], dims, preferred_element_type=F32)
        res = (y[0:ROWS] + y[ROWS:])[0:PROBES] * (1.0 / LIFT) + scale * (z[0:ROWS] + z[ROWS:])[0:PROBES]
        res = res + extra[:, op] * nat[0:PROBES, op]
        for t in range(pt // LANES):
            pack_tile(out_ref, res[:, t * LANES : (t + 1) * LANES], ip * (pt // LANES) + t, n // LANES)
        return 0

    lax.fori_loop(0, n // pt, row, 0)


def apply(khi, klo, w, extra, flag, pt=512):
    n, m = khi.shape
    khi = pltpu.with_memory_space_constraint(khi, VMEM)
    klo = pltpu.with_memory_space_constraint(klo, VMEM)
    return pl.pallas_call(
        functools.partial(apply_body, pt=pt),
        out_shape=jax.ShapeDtypeStruct((SIDE, BOTH, LANES), F32),
        in_specs=[vspec()] * 4 + [sspec()],
        out_specs=vspec(),
        scratch_shapes=[VMEM((ROWS, m), F32), VMEM((2 * ROWS, m), BF16), VMEM((2 * ROWS, m), F8)],
        compiler_params=params(4),
        cost_estimate=pl.CostEstimate(flops=n * m * 600, bytes_accessed=n * m * 3, transcendentals=0),
        name="apply",
    )(khi, klo, w, extra, flag)


def first_sum_body(in_ref, out_ref):
    total = jnp.sum(in_ref[...], axis=0)
    for s in range(SIDE):
        out_ref[s] = total


def first_sum(got):
    return pl.pallas_call(
        first_sum_body,
        out_shape=jax.ShapeDtypeStruct((SIDE, ROWS, LANES), F32),
        in_specs=[vspec()],
        out_specs=vspec(),
        compiler_params=params(),
        name="first_sum",
    )(got)


def places(which):
    lane = lax.broadcasted_iota(jnp.int32, (ROWS, LANES), 1)
    row = lax.broadcasted_iota(jnp.int32, (ROWS, LANES), 0)
    return lane == jnp.where(which < 8 * 24 // ROWS, row & 7, 8)


def joined(blocks, first):
    def part(k):
        return blocks if k == 0 else pltpu.roll(blocks, LANES - ROWS * k, 1)

    def over(x):
        return jnp.sum(x, axis=0, keepdims=True)

    bb, bw, ww, near, rr, rw, rz, wz = (part(k) for k in range(8))
    all_bb, all_bw, all_ww = over(bb), over(bw), over(ww)
    middle = all_bb / all_bw if first else jnp.where(all_ww > 0.0, all_bw / all_ww, 0.0)
    shift = near - middle
    return (all_bb, all_bw, all_ww, middle, over(rr + shift * (2.0 * rw + shift * ww)), over(rw + shift * ww),
            over(rz + shift * wz), over(wz))


def put(lines):
    lane = lax.broadcasted_iota(jnp.int32, (1, LANES), 1)
    out = jnp.zeros((1, LANES), F32)
    for k, line in enumerate(lines):
        line = jnp.where(lane < PROBES, line, 0.0)
        out = out + (line if k == 0 else pltpu.roll(line, ROWS * k, 1))
    return out


def chunk_body(in_ref, b_ref, which_ref, chunk_ref, line_ref):
    total = jnp.sum(in_ref[...], axis=0)
    chunk_ref[...] = total
    which = which_ref[0]
    b, z, w = b_ref[which], total[0:ROWS], total[ROWS:BOTH]
    here = places(which)

    def dot(x, y):
        return jnp.sum(jnp.where(here, jnp.sum(x * y, axis=1, keepdims=True), 0.0), axis=0, keepdims=True)

    ww, bw = dot(w, w), dot(b, w)
    near = jnp.where(ww > 0.0, bw / ww, 0.0)
    r = b - jnp.sum(jnp.where(here, near, 0.0), axis=1, keepdims=True) * w
    line = put((dot(b, b), bw, ww, near, dot(r, r), dot(r, w), dot(r, z), dot(w, z)))
    for s in range(SIDE):
        line_ref[s] = jnp.broadcast_to(line, (LINES, LANES))


def chunk_sums(got, b, which):
    return pl.pallas_call(
        chunk_body,
        out_shape=(jax.ShapeDtypeStruct((BOTH, LANES), F32), jax.ShapeDtypeStruct((SIDE, LINES, LANES), F32)),
        in_specs=[vspec(), vspec(), sspec()],
        out_specs=(vspec(), vspec()),
        compiler_params=params(),
        name="chunk_sums",
    )(got, b, which)


def join_body(chunk_ref, line_ref, out_ref):
    line = put(joined(jnp.concatenate([line_ref[s, 0:1, :] for s in range(SIDE)], axis=0), False))
    for s in range(SIDE // 2):
        out_ref[s, 0:BOTH, :] = chunk_ref[...]
        out_ref[s, BOTH:MORE, :] = jnp.broadcast_to(line, (MORE - BOTH, LANES))


def join(chunk, line):
    return pl.pallas_call(
        join_body,
        out_shape=jax.ShapeDtypeStruct((SIDE // 2, MORE, LANES), F32),
        in_specs=[vspec(), vspec()],
        out_specs=vspec(),
        compiler_params=params(),
        name="join",
    )(chunk, line)


def finish_body(b_ref, mine, other, core_ref, x_ref, r_ref, a_ref, nw, na):
    core = core_ref[0]
    for h in range(SIDE // 2):
        a_ref[2 * h + core] = mine[h]
        a_ref[2 * h + 1 - core] = other[h]
    tiles = b_ref.shape[1] // LANES
    unpack(a_ref, na, tiles)
    unpack(a_ref, nw, tiles, ROWS)
    lines = joined(jnp.concatenate([a_ref[s, BOTH : BOTH + 1, :] for s in range(SIDE)], axis=0), True)
    bb, bw, _, first, rr, rw, rz, _ = (to_column(line, 0) for line in lines)
    beta = rr / bb
    second = rr / ((rw - first * rz) + 2.0 * beta * rw + beta * beta * bw)
    b = b_ref[...]
    w = nw[0:PROBES, :]
    r = b - first * w
    x_ref[...] = first * b + second * (r + beta * b)
    r_ref[...] = r - second * ((w - first * na[0:PROBES, :]) + beta * w)


def finish(b, mine, other, core):
    n = b.shape[1]
    out = jax.ShapeDtypeStruct((PROBES, n), F32)
    return pl.pallas_call(
        finish_body,
        out_shape=(out, out),
        in_specs=[vspec()] * 3 + [sspec()],
        out_specs=(vspec(), vspec()),
        scratch_shapes=[VMEM((SIDE, MORE, LANES), F32), VMEM((ROWS, n), F32), VMEM((ROWS, n), F32)],
        compiler_params=params(4),
        name="finish",
    )(b, mine, other, core)


def on_device(right_side, noise_level, run_index, step_index, run_features):
    swap = [(i * SIDE + j, j * SIDE + i) for i in range(SIDE) for j in range(SIDE)]

    def exchange(x, axis):
        return lax.all_to_all(x, axis, 0, 0)

    flag = (lax.axis_index("row") == lax.axis_index("col")).astype(F32).reshape(1)
    which = lax.axis_index("col").reshape(1)
    tiles = run_index.shape[0] // LANES
    run = run_index.reshape(tiles, LANES)
    step = step_index.reshape(tiles, LANES)
    decays = (jnp.asarray(x) for x in decay_tables())
    plane = lax.broadcasted_iota(jnp.int32, (3, tiles, LANES), 0)
    ids = jnp.where(plane == 2, step, run)
    ids = (ids >> jnp.where(plane == 1, 12, 0)) & jnp.where(plane == 0, GROUP - 1, -1)
    other = lax.ppermute(ids, ("row", "col"), swap)
    *mine, extra, packed = own(ids, run_features, right_side, noise_level, flag, *decays)
    khi, klo, part = build(other, *mine)
    product = exchange(first_sum(exchange(part, "row")), "row")
    both = exchange(apply(khi, klo, product, extra, flag), "col")
    chunk, line = chunk_sums(both, packed, which)
    halves = [list(range(k, SIDE, 2)) for k in range(2)]
    mine = lax.all_to_all(join(chunk, exchange(line, "row")), "col", 0, 0, axis_index_groups=halves)
    rest = lax.ppermute(mine, "col", [(k, k ^ 1) for k in range(SIDE)])
    return finish(right_side, mine, rest, which & 1)


def solution(mesh):
    return jax.shard_map(
        on_device,
        mesh=mesh,
        in_specs=(P(None, "row"), P("row"), P("row"), P("row"), P()),
        out_specs=(P(None, "row"), P(None, "row")),
        check_vma=False,
    )
```

```python
import functools
import math

import jax
import jax.numpy as jnp
import numpy as np
from jax import lax
from jax.experimental import pallas as pl
from jax.experimental.pallas import tpu as pltpu
from jax.sharding import PartitionSpec as P

LANES = 128
SIDE = 16
FEAT = 16
PROBES = 9
ROWS = 16
BUILD = 12
BOTH = 32
MORE = 40
LINES = 8
GROUP = 4096
DEPTH = 256
RANK = 24
STEPS = 128
LOG2E = 1.4426950408889634
F32 = jnp.float32
BF16 = jnp.bfloat16
F8 = jnp.float8_e4m3fn
TOP = 240.0
LIFT = 65536.0
VMEM = pltpu.VMEM
MIB = 1024 * 1024


def vspec():
    return pl.BlockSpec(memory_space=VMEM)


def sspec():
    return pl.BlockSpec(memory_space=pltpu.SMEM)


def params(mib=2):
    return pltpu.CompilerParams(vmem_limit_bytes=mib * MIB)


def thirds(x):
    a = x.astype(BF16).astype(F32)
    b = (x - a).astype(BF16).astype(F32)
    return a, b, x - a - b


def to_column(row, first):
    lane = lax.broadcasted_iota(jnp.int32, (PROBES, LANES), 1)
    sub = lax.broadcasted_iota(jnp.int32, (PROBES, LANES), 0)
    return jnp.sum(jnp.where(lane == sub + first, row, 0.0), axis=1, keepdims=True)


def unpack(v_ref, nat, tiles, first=0):
    for t in range(tiles):
        lanes = slice(t * LANES, (t + 1) * LANES)
        row = first + 8 * (t % 2)
        nat[0:8, lanes] = v_ref[t // 2, row : row + 8, :]
        m = 8 * tiles + t
        row = first + m % ROWS
        nat[8:9, lanes] = v_ref[m // ROWS, row : row + 1, :]


def pack_tile(out_ref, res, tile, tiles):
    out_ref[tile // 2, pl.ds(pl.multiple_of(8 * (tile % 2), 8), 8), :] = res[0:8]
    m = 8 * tiles + tile
    out_ref[m // ROWS, pl.ds(m % ROWS, 1), :] = res[8:9]


def clear_rest(out_ref, tiles):
    m = 9 * tiles
    out_ref[m // ROWS, m % ROWS : ROWS, :] = jnp.zeros((ROWS - m % ROWS, LANES), F32)
    for s in range(m // ROWS + 1, SIDE):
        out_ref[s, 0:ROWS, :] = jnp.zeros((ROWS, LANES), F32)


def factors(v):
    zero = jnp.zeros((ROWS - PROBES, v.shape[1]), F32)
    high = v.astype(BF16).astype(F32)
    halves = jnp.concatenate([high, zero, v - high, zero], axis=0).astype(BF16)
    top = jnp.max(jnp.abs(v), axis=1, keepdims=True)
    top = jnp.where(top > 0.0, top, 1.0)
    u = v * (TOP / top)
    coarse = u.astype(F8).astype(F32)
    small = jnp.concatenate([coarse, zero, (u - coarse), zero], axis=0).astype(F8)
    return halves, small, top * (1.0 / (TOP * LIFT))


def fetch(read, table, rows, t, at):
    for p in range(LANES):
        rows[pl.ds(at + p, 1), :] = table[pl.ds(read(t, p), 1), :]


def turn(rows, group):
    turned = jnp.transpose(rows)
    f = turned[0:FEAT]
    for g in range(1, LANES // FEAT):
        f = jnp.where(group == g, turned[g * FEAT : (g + 1) * FEAT], f)
    return f


def pack(out_ref, v, tiles):
    clear_rest(out_ref, tiles)
    for t in range(tiles):
        pack_tile(out_ref, v[:, t * LANES : (t + 1) * LANES], t, tiles)


def operand(f, is_left):
    f = f * math.sqrt(LOG2E)
    a, b, c = thirds(f)
    norm = -0.5 * jnp.sum(f * f, axis=0, keepdims=True)
    if is_left:
        norm = norm + math.log2(LIFT)
    na, nb, nc = thirds(norm)
    one = jnp.ones_like(norm)
    if is_left:
        parts = [a, a, b, b, a, c, na, nb, nc, one, one, one]
    else:
        parts = [a, b, a, b, c, a, one, one, one, na, nb, nc]
    return jnp.concatenate(parts + [jnp.zeros((2, f.shape[1]), F32)], axis=0)


def own_body(idx_ref, flag_ref, ids_ref, tab_ref, b_ref, noise_ref, decay_ref, right_ref,
             right_decay, table, left, vec, small, scale, extra_b, extra, packed,
             ids, tab, b, noise, decay, terms, rows, sems):
    groups = tab_ref.shape[1] // GROUP
    width = GROUP // 4
    tiles = ids_ref.shape[1]
    pairs = [(ids_ref, ids), (decay_ref, decay), (b_ref, b), (noise_ref, noise), (right_ref, right_decay)]
    loads = [pltpu.make_async_copy(src, dst, sems.at[k]) for k, (src, dst) in enumerate(pairs)]
    parts = []
    for c in range(4):
        for g in range(groups):
            at = pl.ds(g * GROUP + c * width, width)
            parts.append(pltpu.make_async_copy(tab_ref.at[:, at], tab.at[:, at], sems.at[5 + c * groups + g]))
    for part in loads + parts:
        part.start()
    loads[0].wait()
    loads[1].wait()
    table_left = decay[...].astype(BF16)
    for t in range(tiles):
        o = slice(t * LANES, (t + 1) * LANES)
        hot = one_hot(ids[2, t : t + 1, :])
        terms[:, o] = jnp.dot(table_left, hot, preferred_element_type=F32)
        left[o, LANES:] = jnp.transpose(hot.astype(F32)).astype(BF16)
    loads[2].wait()
    loads[3].wait()
    vec[...], small[...], factor = factors(b[...])
    scale[...] = jnp.concatenate([jnp.broadcast_to(factor, (PROBES, LANES)), jnp.zeros((ROWS - PROBES, LANES), F32)], axis=0)
    pack(packed, b[...], tiles)
    extra[...] = flag_ref[0] * noise[...]
    extra_b[...] = flag_ref[0] * noise[...] * b[...]
    blank = jnp.zeros((LANES - groups * FEAT, LANES), F32)
    for c in range(4):
        for part in parts[c * groups : (c + 1) * groups]:
            part.wait()
        for t in range(c * (width // LANES), (c + 1) * (width // LANES)):
            pieces = [tab[:, g * GROUP + t * LANES : g * GROUP + (t + 1) * LANES] for g in range(groups)]
            table[t * LANES : (t + 1) * LANES, :] = jnp.transpose(jnp.concatenate(pieces + [blank], axis=0))
    loads[4].wait()

    def get(t, _):
        fetch(lambda t, p: idx_ref[0, t, p], table, rows, t, pl.multiple_of(t * LANES, LANES))
        return 0

    lax.fori_loop(0, tiles, get, 0)
    for t in range(tiles):
        o = slice(t * LANES, (t + 1) * LANES)
        f = turn(rows[o, :], ids[1, t : t + 1, :])
        left[o, 0:LANES] = jnp.transpose(jnp.concatenate([operand(f, True), terms[:, o]], axis=0)).astype(BF16)


def decay_tables():
    rest = np.array([[-1.5 * math.log2((s + t + 8.0) / 8.0) for t in range(STEPS)] for s in range(STEPS)])

    def rounded(x):
        return x.astype(BF16).astype(np.float64)

    left, right = [], []
    for _ in range(RANK):
        s, t = divmod(int(np.argmax(np.abs(rest))), STEPS)
        a, b = rounded(rest[:, t] / rest[s, t]), rounded(rest[s, :])
        left.append(a)
        right.append(b)
        rest = rest - np.outer(a, b)
    return np.array(left).astype(np.float32), np.concatenate([np.array(right), rounded(rest)]).astype(np.float32)


def one_hot(step):
    row = lax.broadcasted_iota(jnp.int32, (STEPS, LANES), 0)
    return jnp.where(row == step, 1.0, 0.0).astype(BF16)


def hbm(x):
    return pltpu.with_memory_space_constraint(x, pltpu.HBM)


def own(ids, table, b, noise, flag, decay, right_decay):
    n = b.shape[1]
    return pl.pallas_call(
        own_body,
        out_shape=(
            VMEM(right_decay.shape, F32),
            VMEM((GROUP, LANES), F32),
            VMEM((n, DEPTH), BF16),
            VMEM((2 * ROWS, n), BF16),
            VMEM((2 * ROWS, n), F8),
            VMEM((ROWS, LANES), F32),
            VMEM((PROBES, n), F32),
            VMEM((1, n), F32),
            jax.ShapeDtypeStruct((SIDE, ROWS, LANES), F32),
        ),
        in_specs=[sspec()] * 2 + [pl.BlockSpec(memory_space=pl.ANY)] * 6,
        out_specs=(vspec(),) * 9,
        scratch_shapes=[
            VMEM(ids.shape, jnp.int32),
            VMEM(table.shape, F32),
            VMEM(b.shape, F32),
            VMEM((1, n), F32),
            VMEM(decay.shape, F32),
            VMEM((RANK, n), F32),
            VMEM((n, LANES), F32),
            pltpu.SemaphoreType.DMA((5 + 4 * (table.shape[1] // GROUP),)),
        ],
        compiler_params=params(12),
        cost_estimate=pl.CostEstimate(flops=n * 6000, bytes_accessed=4 * table.size, transcendentals=0),
        name="own",
    )(ids, flag, ids, *(hbm(x) for x in (table, b, noise.reshape(1, n), decay, right_decay)))


def build_body(idx_ref, other, decay, table, left, vec, small, scale, extra_b,
               khi_ref, klo_ref, out_ref, rows, right, acc, acc8, *, pt, qt):
    n, m = khi_ref.shape
    tiles = m // LANES
    per = qt // LANES

    def ready(jq, slot):
        for k in range(per):
            t = jq * per + k
            o = slice(k * LANES, (k + 1) * LANES)
            fetch(lambda t, p: idx_ref[0, t, p], table, rows, t, k * LANES)
            f = turn(rows[o, :], other[1, pl.ds(t, 1), :])
            terms = jnp.dot(decay[...].astype(BF16), one_hot(other[2, pl.ds(t, 1), :]), preferred_element_type=F32)
            right[slot, :, o] = jnp.concatenate([operand(f, False), terms], axis=0).astype(BF16)

    def column(jq, _):
        oq = pl.ds(pl.multiple_of(jq * qt, qt), qt)
        right_tile = right[jq % 2]
        acc[...] = jnp.zeros_like(acc)
        acc8[...] = jnp.zeros_like(acc8)

        def row(ip, _):
            op = pl.ds(pl.multiple_of(ip * pt, pt), pt)
            power = jnp.dot(left[op, :], right_tile, preferred_element_type=F32)
            k = jnp.exp2(power)
            high = k.astype(BF16)
            low = (k - high.astype(F32)).astype(BF16).astype(F8)
            khi_ref[op, oq] = high
            klo_ref[op, oq] = low
            acc[...] += jnp.dot(vec[:, op], high, preferred_element_type=F32)
            acc8[...] += jnp.dot(small[:, op], low, preferred_element_type=F32)
            return 0

        lax.fori_loop(0, n // pt, row, 0, unroll=n // pt)
        res = (acc[0:ROWS, :] + acc[ROWS:, :]) * (1.0 / LIFT) + scale[:, 0:1] * (acc8[0:ROWS, :] + acc8[ROWS:, :])
        res = res[0:PROBES] + extra_b[:, oq]
        for t in range(qt // LANES):
            pack_tile(out_ref, res[:, t * LANES : (t + 1) * LANES], jq * (qt // LANES) + t, tiles)
        ready(jnp.minimum(jq + 1, m // qt - 1), (jq + 1) % 2)
        return 0

    clear_rest(out_ref, tiles)
    ready(0, 0)
    lax.fori_loop(0, m // qt, column, 0)


def build(other, decay, table, left, vec, small, scale, extra_b, pt=3072, qt=512):
    n = left.shape[0]
    m = other.shape[1] * LANES
    return pl.pallas_call(
        functools.partial(build_body, pt=pt, qt=qt),
        out_shape=(VMEM((n, m), BF16), VMEM((n, m), F8), jax.ShapeDtypeStruct((SIDE, ROWS, LANES), F32)),
        in_specs=[sspec()] + [vspec()] * 8,
        out_specs=(vspec(),) * 3,
        scratch_shapes=[
            VMEM((qt, LANES), F32),
            VMEM((2, DEPTH, qt), BF16),
            VMEM((2 * ROWS, qt), F32),
            VMEM((2 * ROWS, qt), F32),
        ],
        compiler_params=params(BUILD),
        cost_estimate=pl.CostEstimate(flops=n * m * 1000, bytes_accessed=n * m * 3, transcendentals=2 * n * m),
        name="build",
    )(other, other, decay, table, left, vec, small, scale, extra_b)


def apply_body(khi_ref, klo_ref, w_ref, extra, flag_ref, core_ref, keep, give, out_ref, nat, vec, small, *, pt):
    n, m = khi_ref.shape
    unpack(w_ref, nat, m // LANES)
    vec[...], small[...], scale = factors(nat[0:PROBES, :])
    clear_rest(out_ref, n // LANES)
    for s in range(SIDE):
        out_ref[s, ROWS:BOTH, :] = flag_ref[0] * w_ref[s]
    dims = (((1,), (1,)), ((), ()))

    def row(ip, _):
        op = pl.ds(pl.multiple_of(ip * pt, pt), pt)
        y = lax.dot_general(vec[...], khi_ref[op, :], dims, preferred_element_type=F32)
        z = lax.dot_general(small[...], klo_ref[op, :], dims, preferred_element_type=F32)
        res = (y[0:ROWS] + y[ROWS:])[0:PROBES] * (1.0 / LIFT) + scale * (z[0:ROWS] + z[ROWS:])[0:PROBES]
        res = res + extra[:, op] * nat[0:PROBES, op]
        for t in range(pt // LANES):
            pack_tile(out_ref, res[:, t * LANES : (t + 1) * LANES], ip * (pt // LANES) + t, n // LANES)
        return 0

    lax.fori_loop(0, n // pt, row, 0)
    core = core_ref[0]
    for h in range(SIDE // 2):
        keep[h] = out_ref[2 * h + core]
        give[h] = out_ref[2 * h + 1 - core]


def apply(khi, klo, w, extra, flag, core, pt=512):
    n, m = khi.shape
    khi = pltpu.with_memory_space_constraint(khi, VMEM)
    klo = pltpu.with_memory_space_constraint(klo, VMEM)
    return pl.pallas_call(
        functools.partial(apply_body, pt=pt),
        out_shape=(jax.ShapeDtypeStruct((SIDE // 2, BOTH, LANES), F32),) * 2,
        in_specs=[vspec()] * 4 + [sspec()] * 2,
        out_specs=(vspec(), vspec()),
        scratch_shapes=[VMEM((SIDE, BOTH, LANES), F32), VMEM((ROWS, m), F32), VMEM((2 * ROWS, m), BF16), VMEM((2 * ROWS, m), F8)],
        compiler_params=params(4),
        cost_estimate=pl.CostEstimate(flops=n * m * 600, bytes_accessed=n * m * 3, transcendentals=0),
        name="apply",
    )(khi, klo, w, extra, flag, core)


def first_sum_body(in_ref, out_ref):
    total = jnp.sum(in_ref[...], axis=0)
    for s in range(SIDE):
        out_ref[s] = total


def first_sum(got):
    return pl.pallas_call(
        first_sum_body,
        out_shape=jax.ShapeDtypeStruct((SIDE, ROWS, LANES), F32),
        in_specs=[vspec()],
        out_specs=vspec(),
        compiler_params=params(),
        name="first_sum",
    )(got)


def places(which):
    lane = lax.broadcasted_iota(jnp.int32, (ROWS, LANES), 1)
    row = lax.broadcasted_iota(jnp.int32, (ROWS, LANES), 0)
    return lane == jnp.where(which < 8 * 24 // ROWS, row & 7, 8)


def joined(blocks, first):
    def part(k):
        return blocks if k == 0 else pltpu.roll(blocks, LANES - ROWS * k, 1)

    def over(x):
        return jnp.sum(x, axis=0, keepdims=True)

    bb, bw, ww, near, rr, rw, rz, wz = (part(k) for k in range(8))
    all_bb, all_bw, all_ww = over(bb), over(bw), over(ww)
    middle = all_bb / all_bw if first else jnp.where(all_ww > 0.0, all_bw / all_ww, 0.0)
    shift = near - middle
    return (all_bb, all_bw, all_ww, middle, over(rr + shift * (2.0 * rw + shift * ww)), over(rw + shift * ww),
            over(rz + shift * wz), over(wz))


def put(lines):
    lane = lax.broadcasted_iota(jnp.int32, (1, LANES), 1)
    out = jnp.zeros((1, LANES), F32)
    for k, line in enumerate(lines):
        line = jnp.where(lane < PROBES, line, 0.0)
        out = out + (line if k == 0 else pltpu.roll(line, ROWS * k, 1))
    return out


def add_body(a_ref, b_ref, out_ref):
    out_ref[...] = a_ref[...] + b_ref[...]


def add(a, b):
    return pl.pallas_call(
        add_body,
        out_shape=jax.ShapeDtypeStruct(a.shape, F32),
        in_specs=[vspec()] * 2,
        out_specs=vspec(),
        compiler_params=params(),
        name="add",
    )(a, b)


def chunk_body(in_ref, b_ref, which_ref, chunk_ref, line_ref):
    total = jnp.sum(in_ref[...], axis=0)
    chunk_ref[...] = total
    which = which_ref[0]
    b, z, w = b_ref[which], total[0:ROWS], total[ROWS:BOTH]
    here = places(which)

    def dot(x, y):
        return jnp.sum(jnp.where(here, jnp.sum(x * y, axis=1, keepdims=True), 0.0), axis=0, keepdims=True)

    ww, bw = dot(w, w), dot(b, w)
    near = jnp.where(ww > 0.0, bw / ww, 0.0)
    r = b - jnp.sum(jnp.where(here, near, 0.0), axis=1, keepdims=True) * w
    line = put((dot(b, b), bw, ww, near, dot(r, r), dot(r, w), dot(r, z), dot(w, z)))
    for s in range(SIDE):
        line_ref[s] = jnp.broadcast_to(line, (LINES, LANES))


def chunk_sums(got, b, which):
    return pl.pallas_call(
        chunk_body,
        out_shape=(jax.ShapeDtypeStruct((BOTH, LANES), F32), jax.ShapeDtypeStruct((SIDE, LINES, LANES), F32)),
        in_specs=[vspec(), vspec(), sspec()],
        out_specs=(vspec(), vspec()),
        compiler_params=params(),
        name="chunk_sums",
    )(got, b, which)


def join_body(chunk_ref, line_ref, out_ref):
    line = put(joined(jnp.concatenate([line_ref[s, 0:1, :] for s in range(SIDE)], axis=0), False))
    for s in range(SIDE // 2):
        out_ref[s, 0:BOTH, :] = chunk_ref[...]
        out_ref[s, BOTH:MORE, :] = jnp.broadcast_to(line, (MORE - BOTH, LANES))


def join(chunk, line):
    return pl.pallas_call(
        join_body,
        out_shape=jax.ShapeDtypeStruct((SIDE // 2, MORE, LANES), F32),
        in_specs=[vspec(), vspec()],
        out_specs=vspec(),
        compiler_params=params(),
        name="join",
    )(chunk, line)


def finish_body(b_ref, mine, other, core_ref, x_ref, r_ref, a_ref, nw, na):
    core = core_ref[0]
    for h in range(SIDE // 2):
        a_ref[2 * h + core] = mine[h]
        a_ref[2 * h + 1 - core] = other[h]
    tiles = b_ref.shape[1] // LANES
    unpack(a_ref, na, tiles)
    unpack(a_ref, nw, tiles, ROWS)
    lines = joined(jnp.concatenate([a_ref[s, BOTH : BOTH + 1, :] for s in range(SIDE)], axis=0), True)
    bb, bw, _, first, rr, rw, rz, _ = (to_column(line, 0) for line in lines)
    beta = rr / bb
    second = rr / ((rw - first * rz) + 2.0 * beta * rw + beta * beta * bw)
    b = b_ref[...]
    w = nw[0:PROBES, :]
    r = b - first * w
    x_ref[...] = first * b + second * (r + beta * b)
    r_ref[...] = r - second * ((w - first * na[0:PROBES, :]) + beta * w)


def finish(b, mine, other, core):
    n = b.shape[1]
    out = jax.ShapeDtypeStruct((PROBES, n), F32)
    return pl.pallas_call(
        finish_body,
        out_shape=(out, out),
        in_specs=[vspec()] * 3 + [sspec()],
        out_specs=(vspec(), vspec()),
        scratch_shapes=[VMEM((SIDE, MORE, LANES), F32), VMEM((ROWS, n), F32), VMEM((ROWS, n), F32)],
        compiler_params=params(4),
        name="finish",
    )(b, mine, other, core)


def on_device(right_side, noise_level, run_index, step_index, run_features):
    swap = [(i * SIDE + j, j * SIDE + i) for i in range(SIDE) for j in range(SIDE)]

    def exchange(x, axis):
        return lax.all_to_all(x, axis, 0, 0)

    flag = (lax.axis_index("row") == lax.axis_index("col")).astype(F32).reshape(1)
    which = lax.axis_index("col").reshape(1)
    tiles = run_index.shape[0] // LANES
    run = run_index.reshape(tiles, LANES)
    step = step_index.reshape(tiles, LANES)
    decays = (jnp.asarray(x) for x in decay_tables())
    plane = lax.broadcasted_iota(jnp.int32, (3, tiles, LANES), 0)
    ids = jnp.where(plane == 2, step, run)
    ids = (ids >> jnp.where(plane == 1, 12, 0)) & jnp.where(plane == 0, GROUP - 1, -1)
    other = lax.ppermute(ids, ("row", "col"), swap)
    *mine, extra, packed = own(ids, run_features, right_side, noise_level, flag, *decays)
    khi, klo, part = build(other, *mine)
    product = exchange(first_sum(exchange(part, "row")), "row")
    halves = [list(range(k, SIDE, 2)) for k in range(2)]

    def swapped(x):
        return lax.ppermute(x, "col", [(k, k ^ 1) for k in range(SIDE)])

    def half_exchange(x):
        return lax.all_to_all(x, "col", 0, 0, axis_index_groups=halves)

    core = which & 1
    keep, give = apply(khi, klo, product, extra, flag, core)
    chunk, line = chunk_sums(half_exchange(add(keep, swapped(give))), packed, which)
    mine = half_exchange(join(chunk, exchange(line, "row")))
    return finish(right_side, mine, swapped(mine), core)


def solution(mesh):
    return jax.shard_map(
        on_device,
        mesh=mesh,
        in_specs=(P(None, "row"), P("row"), P("row"), P("row"), P()),
        out_specs=(P(None, "row"), P(None, "row")),
        check_vma=False,
    )
```
